32 devices in a mesh: section: 4 (over x, core), dp: 4 (over z), tensor: 2 (over y).
Axes of the slice: x: 2, y: 2, z: 4, core: 2. Of those that a mesh axis runs over, the one named last changes fastest.
Arguments:
- block_inputs: bfloat16 [4, 512, 3072], P('section', ('dp', 'tensor')), may hold values from -16 to 16
- qkv_weights: bfloat16 [4, 3, 3072, 3072], P('section', None, None, ('dp', 'tensor')), may hold values from -0.109375 to 0.109375
- out_weights: bfloat16 [4, 3072, 3072], P('section', ('dp', 'tensor')), may hold values from -0.109375 to 0.109375
- norm_gain: float32 [4, 3072], P('section'), may hold values from 0.25 to 1.75
- query_key_gain: float32 [4, 2, 128], P('section'), may hold values from 1.5 to 1.75
- pool_gain: float32 [4, 3072], P('section'), may hold values from 0.25 to 1.75
- class_head: bfloat16 [4, 3072, 512], P('section'), may hold values from -0.75 to 0.75
- labels: int32 [4, 2], P('section'), may hold values from 0 to 511
Outputs:
- out_rows: bfloat16 [4, 512, 3072], P('section', ('dp', 'tensor'))
- query_key_value_gradient: bfloat16 [4, 3, 3072, 3072], P('section', None, None, ('dp', 'tensor'))
- grad_out: bfloat16 [4, 3072, 3072], P('section', ('dp', 'tensor'))
- grad_head: bfloat16 [4, 3072, 512], P('section', ('dp', 'tensor'))
- losses: float32 [4, 2], P('section')
The draws below stay inside these ranges and needn't reach their ends.
All inputs are finite; a program needn't handle non-finite values.
Results may differ from the reference program's by a relative error of at most 0.03.
Values may be sent and summed in bfloat16 or wider, within the bound.
No kernel may reach another device: no remote copies, remote signals or barrier semaphores. Data moves between devices by JAX's collectives and lax.ppermute only.
A program may use at most 128 MiB of HBM per device.

```python
import math
import jax
import jax.numpy as jnp
from jax import lax

D = 3072
HEADS = 24
HS = 128
CLASSES = 512
PATCHES = 256
IMAGES = 2
SECTIONS = 4
N_DP = 4
N_TENSOR = 2


def draw_block_inputs(key, part):
    key_columns = jax.random.fold_in(key, 11)
    key_values = jax.random.fold_in(key, 12)
    key_rows = jax.random.fold_in(key, 13)
    full_shape = (SECTIONS, IMAGES * PATCHES, D)
    columns = jnp.exp(jax.random.uniform(key_columns, (SECTIONS, 1, D), minval=math.log(0.3), maxval=math.log(3.0)))
    row_scales = jnp.exp(jax.random.uniform(key_rows, (SECTIONS, IMAGES * PATCHES, 1), minval=math.log(0.25), maxval=math.log(2.0)))
    values = jax.random.normal(key_values, full_shape) * row_scales * columns
    return jnp.clip(values, -16.0, 16.0).astype(jnp.bfloat16)


def touch_ends(entries, rng, low, largest):
    dims = entries.shape
    place = [jax.random.randint(jax.random.fold_in(rng, axis), (), 0, dims[axis]) for axis in range(len(dims))]
    entries = entries.at[tuple(place)].set(low)
    longest = dims.index(max(dims))
    place[longest] = (place[longest] + 1) % dims[longest]
    return entries.at[tuple(place)].set(largest)


def level_of(key, dims, shards, smallest, high):
    factor_of, own = 1.0, jax.random.fold_in(key, 6)
    for dim, shards_of in shards:
        draws = jnp.exp(jax.random.uniform(jax.random.fold_in(own, dim), (shards_of,), jnp.float32, smallest / len(shards), high / len(shards)))
        factor_of = factor_of * jnp.repeat(draws, dims[dim] // shards_of).reshape([-1 if axis == dim else 1 for axis in range(len(dims))])
    return factor_of


def normal_values(rng, shape, scale, limit, pieces=(), held_as=jnp.bfloat16):
    entries = jax.random.normal(rng, shape, jnp.float32) * scale
    if len(pieces) > 0:
        entries = level_of(rng, shape, pieces, -0.22, 0.18) * entries
    return jnp.clip(entries, min=-limit, max=limit).astype(held_as)


def setup_inputs(seed: int = 0) -> dict:
    key_list = jax.random.split(jax.random.key(seed), 9)
    block_inputs = draw_block_inputs(jax.random.fold_in(key_list[8], 71), 0)
    qkv_weights = normal_values(key_list[1], (SECTIONS, 3, D, HEADS * HS), D ** -0.5, 0.109375, ((0, 4), (3, 8)))
    out_weights = normal_values(key_list[2], (SECTIONS, HEADS * HS, D), (HEADS * HS) ** -0.5, 0.109375, ((0, 4), (1, 8)))
    norm_gain = jnp.clip(1.0 + 0.15 * jax.random.normal(key_list[3], (SECTIONS, D), jnp.float32), 0.25, 1.75)
    query_key_gain = jnp.clip(1.5 + 0.25 * jax.random.uniform(key_list[4], (SECTIONS, 2, HS), jnp.float32) ** level_of(key_list[4], (SECTIONS, 2, HS), ((0, 4),), -0.2, 0.2), 1.5, 1.75)
    pool_gain = jnp.clip(1.0 + 0.15 * jax.random.normal(key_list[5], (SECTIONS, D), jnp.float32), 0.25, 1.75)
    class_head = normal_values(key_list[6], (SECTIONS, D, CLASSES), 0.054, 0.75, ((0, 4),))
    labels = touch_ends(jax.random.randint(key_list[7], (SECTIONS, IMAGES), 0, CLASSES), jax.random.fold_in(key_list[7], 1), 0, CLASSES - 1).astype(jnp.int32)
    return {"block_inputs": block_inputs, "qkv_weights": qkv_weights, "out_weights": out_weights, "norm_gain": norm_gain, "query_key_gain": query_key_gain, "pool_gain": pool_gain, "class_head": class_head, "labels": labels}


epsilon = 1e-06

def as_half(values):
    return lax.optimization_barrier(values.astype(jnp.bfloat16))

def into_lone_copy(values):
    return values.astype(jnp.float32)

def norm_last(values, gain_row):
    centered = values - lax.optimization_barrier(jnp.mean(values, axis=-1, keepdims=True))
    inverse = lax.rsqrt(lax.optimization_barrier(jnp.mean(centered * centered, axis=-1, keepdims=True)) + epsilon)
    unit_rows = centered * inverse
    return (unit_rows * gain_row, unit_rows, inverse)

def norm_back(grad_normed, unit_rows, inverse, gain_row):
    scaled = grad_normed * gain_row
    return inverse * (scaled - lax.optimization_barrier(jnp.mean(scaled, axis=-1, keepdims=True)) - unit_rows * lax.optimization_barrier(jnp.mean(scaled * unit_rows, axis=-1, keepdims=True)))

def group_product(left, right):
    groups = N_DP * N_TENSOR
    row_count = left.shape[0]
    width = right.shape[0] // groups
    left_split = into_lone_copy(left).reshape(row_count, groups, width)
    right_split = into_lone_copy(right).reshape(groups, width, right.shape[1])
    partials = jnp.einsum('rgw,gwd->grd', left_split, right_split)
    return lax.optimization_barrier(jnp.sum(into_lone_copy(as_half(partials)), axis=0))

def group_input_grad(projection_gradient, query_key_value_nearby):
    groups = N_DP * N_TENSOR
    row_count = projection_gradient.shape[1]
    width = query_key_value_nearby.shape[2] // groups
    grad_split = into_lone_copy(projection_gradient).reshape(3, row_count, groups, width)
    weight_split = into_lone_copy(query_key_value_nearby).reshape(3, query_key_value_nearby.shape[1], groups, width)
    partials = jnp.einsum('trgw,tdgw->grd', grad_split, weight_split)
    return lax.optimization_barrier(jnp.sum(into_lone_copy(as_half(partials)), axis=0))

def attend(normalized_halves, query_key_value_nearby, gain_pair):
    row_count = normalized_halves.shape[0]
    image_count = row_count // PATCHES
    head_count = query_key_value_nearby.shape[2] // HS
    split_shape = (image_count, PATCHES, head_count, HS)
    query_raw = jnp.dot(normalized_halves, query_key_value_nearby[0], preferred_element_type=jnp.float32).reshape(split_shape)
    keys_raw = jnp.dot(normalized_halves, query_key_value_nearby[1], preferred_element_type=jnp.float32).reshape(split_shape)
    values_raw = jnp.dot(normalized_halves, query_key_value_nearby[2], preferred_element_type=jnp.float32).reshape(split_shape)
    query_normed, query_unit, query_inverse = norm_last(query_raw, gain_pair[0])
    key_normed, key_unit, key_inverse = norm_last(keys_raw, gain_pair[1])
    query_half = as_half(query_normed)
    key_half = as_half(key_normed)
    value_half = as_half(values_raw)
    scores = jnp.einsum('iphe,iqhe->ihpq', into_lone_copy(query_half), into_lone_copy(key_half)) / math.sqrt(HS)
    exponent = jnp.exp(scores)
    softmax_probs = exponent / lax.optimization_barrier(jnp.sum(exponent, axis=-1, keepdims=True))
    probs_half = as_half(softmax_probs)
    mixed_values = jnp.einsum('ihpq,iqhe->iphe', into_lone_copy(probs_half), into_lone_copy(value_half))
    attention = mixed_values.astype(jnp.bfloat16).reshape(row_count, head_count * HS)
    saved_state = (query_unit, query_inverse, key_unit, key_inverse, query_half, key_half, value_half, softmax_probs, probs_half)
    return (attention, saved_state)

def attend_back(grad_attention, saved_state, gain_pair):
    query_unit, query_inverse, key_unit, key_inverse, query_half, key_half, value_half, softmax_probs, probs_half = saved_state
    image_count, patch_count, head_count, head_size = query_half.shape
    grad_mixed = into_lone_copy(as_half(grad_attention)).reshape(query_half.shape)
    grad_probs = jnp.einsum('iphe,iqhe->ihpq', grad_mixed, into_lone_copy(value_half))
    grad_value = jnp.einsum('ihpq,iphe->iqhe', into_lone_copy(probs_half), grad_mixed)
    grad_scores = softmax_probs * (grad_probs - lax.optimization_barrier(jnp.sum(softmax_probs * grad_probs, axis=-1, keepdims=True)))
    score_half = into_lone_copy(as_half(grad_scores / math.sqrt(HS)))
    grad_query = jnp.einsum('ihpq,iqhe->iphe', score_half, into_lone_copy(key_half))
    grad_key = jnp.einsum('ihpq,iphe->iqhe', score_half, into_lone_copy(query_half))
    grad_query = norm_back(grad_query, query_unit, query_inverse, gain_pair[0])
    grad_key = norm_back(grad_key, key_unit, key_inverse, gain_pair[1])
    joined = jnp.stack([grad_query, grad_key, grad_value]).reshape(3, image_count * patch_count, head_count * head_size)
    return as_half(joined)

def layer_forward(rows_in, query_key_value_nearby, out_local, gain_row, gain_pair, grouped):
    normed, unit_rows, inverse = norm_last(into_lone_copy(rows_in), gain_row)
    normalized_halves = as_half(normed)
    attention, saved_state = attend(normalized_halves, query_key_value_nearby, gain_pair)
    if grouped:
        branch = group_product(attention, out_local)
    else:
        branch = jnp.dot(attention, out_local, preferred_element_type=jnp.float32)
    return (into_lone_copy(rows_in) + branch, (normalized_halves, unit_rows, inverse, attention, saved_state))

def section_forward(operands):
    rows_in, query_key_value_nearby, out_local, gain_row, gain_pair = operands
    return layer_forward(rows_in, query_key_value_nearby, out_local, gain_row, gain_pair, True)[0].astype(jnp.bfloat16)

def section_margin(operands):
    rows_in, query_key_value_nearby, out_local, gain_row, gain_pair, pool_row, head_local, label_row = operands
    summed, stash = layer_forward(rows_in, query_key_value_nearby, out_local, gain_row, gain_pair, False)
    normalized_halves, unit_rows, inverse, attention, saved_state = stash
    image_count = label_row.shape[0]
    model_width = summed.shape[1]
    pooled = lax.optimization_barrier(jnp.mean(summed.reshape(image_count, PATCHES, model_width), axis=1))
    pooled_normed, pooled_unit, pooled_inverse = norm_last(pooled, pool_row)
    pooled_half = as_half(pooled_normed)
    logits = jnp.dot(pooled_half, head_local, preferred_element_type=jnp.float32)
    targets = (label_row[:, None] == jnp.arange(CLASSES, dtype=jnp.int32)[None, :]).astype(jnp.float32)
    losses = lax.optimization_barrier(jnp.mean(jax.nn.softplus(logits) - targets * logits, axis=-1))
    grad_logits = as_half((jax.nn.sigmoid(logits) - targets) / image_count)
    grad_head = jnp.dot(pooled_half.T, grad_logits, preferred_element_type=jnp.float32)
    grad_pooled = norm_back(jnp.dot(grad_logits, head_local.T, preferred_element_type=jnp.float32), pooled_unit, pooled_inverse, pool_row)
    grad_image = grad_pooled / PATCHES
    grad_rows = jnp.broadcast_to(grad_image[:, None, :], (image_count, PATCHES, model_width)).reshape(summed.shape)
    grad_rows_half = as_half(grad_rows)
    grad_out = jnp.dot(attention.T, grad_rows_half, preferred_element_type=jnp.float32)
    grad_attention = jnp.dot(grad_rows_half, out_local.T, preferred_element_type=jnp.float32)
    projection_gradient = attend_back(grad_attention, saved_state, gain_pair)
    query_key_value_gradient = jnp.einsum('bp,sbn->spn', into_lone_copy(normalized_halves), into_lone_copy(projection_gradient))
    grad_normed = group_input_grad(projection_gradient, query_key_value_nearby)
    grad_inputs = as_half(grad_rows + norm_back(grad_normed, unit_rows, inverse, gain_row))
    return (grad_inputs, query_key_value_gradient, grad_out, grad_head, losses)

def section_own(operands):
    rows_in, query_key_value_nearby, out_local, gain_row, gain_pair, returned = operands
    stash = layer_forward(rows_in, query_key_value_nearby, out_local, gain_row, gain_pair, False)[1]
    normalized_halves, unit_rows, inverse, attention, saved_state = stash
    grad_out = jnp.dot(attention.T, returned, preferred_element_type=jnp.float32)
    grad_attention = jnp.dot(returned, out_local.T, preferred_element_type=jnp.float32)
    projection_gradient = attend_back(grad_attention, saved_state, gain_pair)
    query_key_value_gradient = jnp.einsum('bp,sbn->spn', into_lone_copy(normalized_halves), into_lone_copy(projection_gradient))
    return (query_key_value_gradient, grad_out)

def reference(block_inputs, qkv_weights, out_weights, norm_gain, query_key_gain, pool_gain, class_head, labels):
    out_rows = lax.map(section_forward, (block_inputs, qkv_weights, out_weights, norm_gain, query_key_gain))
    margin_in = jnp.concatenate([block_inputs[:1], out_rows[:-1]], axis=0)
    grad_inputs, qkv_first, out_first, grad_head, losses = lax.map(section_margin, (margin_in, qkv_weights, out_weights, norm_gain, query_key_gain, pool_gain, class_head, labels))
    returned = jnp.concatenate([grad_inputs[1:], jnp.zeros_like(grad_inputs[:1])], axis=0)
    qkv_second, out_second = lax.map(section_own, (block_inputs, qkv_weights, out_weights, norm_gain, query_key_gain, returned))
    query_key_value_gradient = (qkv_first + qkv_second).astype(jnp.bfloat16)
    grad_out = (out_first + out_second).astype(jnp.bfloat16)
    return (out_rows, query_key_value_gradient, grad_out, grad_head.astype(jnp.bfloat16), losses)
```

```python
import functools
import math

import jax
import jax.numpy as jnp
from jax import lax
from jax.experimental import pallas as pl
from jax.experimental.pallas import tpu as pltpu
from jax.sharding import PartitionSpec as P

HS = 128
PATCHES = 256
GROUP = ("dp", "tensor")
HALVES = 2

epsilon = 1e-06
F32 = jnp.float32
BF16 = jnp.bfloat16
VMEM_SPEC = pl.BlockSpec(memory_space=pltpu.VMEM)
SMEM_SPEC = pl.BlockSpec(memory_space=pltpu.SMEM)


def from_behind(block, axis, distance):
    devices = range(lax.axis_size(axis))
    route = [(i - distance, i) for i in devices if i - distance in devices]
    return lax.ppermute(block, axis, route)


def shift(block, axis, distance):
    count = lax.axis_size(axis)
    return lax.ppermute(block, axis, [(i, (i + distance) % count) for i in range(count)])


def after(value, *others):
    return lax.optimization_barrier((value,) + others)[0]


def way(half):
    return 1 if half % 2 == 0 else -1


def gather_slabs(halves):
    depth, width = lax.axis_size("dp"), lax.axis_size("tensor")
    ring = [list(halves)]
    across = [[[shift(h, "tensor", j) for h in halves] for j in range(1, width)]]
    for _ in range(depth - 1):
        ring.append([shift(ring[-1][h], "dp", way(h)) for h in range(HALVES)])
        across.append(
            [
                [
                    shift(after(ring[-1][h], across[-1][j - 1][h]), "tensor", j)
                    for h in range(HALVES)
                ]
                for j in range(1, width)
            ]
        )
    return [
        jnp.concatenate(ring[s] + [p for place in across[s] for p in place], axis=0)
        for s in range(depth)
    ]


def scatter_slabs(slab_term):
    depth, width = lax.axis_size("dp"), lax.axis_size("tensor")
    running = [None] * HALVES
    last = [[None] * HALVES for _ in range(width)]
    for s in list(range(1, depth)) + [0]:
        term = slab_term(s)
        half = term.shape[0] // (width * HALVES)
        for h in range(HALVES):
            total = term[h * half : (h + 1) * half]
            for j in range(1, width):
                start = (j * HALVES + h) * half
                piece = term[start : start + half].astype(BF16)
                if last[j][h] is not None:
                    piece = after(piece, last[j][h])
                last[j][h] = shift(piece, "tensor", -j)
                total = total + last[j][h].astype(F32)
            if running[h] is not None:
                total = total + shift(running[h], "dp", way(h)).astype(F32)
            running[h] = total if s == 0 else total.astype(BF16)
    return running


def sum_group(value):
    for axis in ("tensor", "dp"):
        count = lax.axis_size(axis)
        if count & (count - 1):
            return lax.psum(value, GROUP)
    for axis in ("tensor", "dp"):
        step = 1
        while step < lax.axis_size(axis):
            route = [(i, i ^ step) for i in range(lax.axis_size(axis))]
            value = value + lax.ppermute(value, axis, route)
            step *= 2
    return value


def norm_parts(values):
    centered = values - jnp.mean(values, axis=-1, keepdims=True)
    inverse = lax.rsqrt(jnp.mean(centered * centered, axis=-1, keepdims=True) + epsilon)
    return centered * inverse, inverse


def norm_back(grad_normed, unit_rows, inverse, gain_row):
    scaled = grad_normed * gain_row
    return inverse * (
        scaled
        - jnp.mean(scaled, axis=-1, keepdims=True)
        - unit_rows * jnp.mean(scaled * unit_rows, axis=-1, keepdims=True)
    )


def dot_nt(left, right):
    return lax.dot_general(left, right, (((1,), (1,)), ((), ())), preferred_element_type=F32)


def dot_tn(left, right):
    return lax.dot_general(left, right, (((0,), (0,)), ((), ())), preferred_element_type=F32)


def dot(left, right):
    return jnp.dot(left, right, preferred_element_type=F32)


def call(kernel, out_shape, ins, specs=None, scratch=(), flops=0, moved=1000000, limit=32):
    many = isinstance(out_shape, (tuple, list))
    return pl.pallas_call(
        kernel,
        out_shape=out_shape,
        in_specs=specs or [VMEM_SPEC] * len(ins),
        out_specs=[VMEM_SPEC] * len(out_shape) if many else VMEM_SPEC,
        scratch_shapes=list(scratch),
        compiler_params=pltpu.CompilerParams(vmem_limit_bytes=limit * 2**20),
        cost_estimate=pl.CostEstimate(flops=flops, bytes_accessed=moved, transcendentals=0),
    )(*ins)


def piece_rows(local_count, depth, width):
    half = local_count // HALVES
    z, y = lax.axis_index("dp"), lax.axis_index("tensor")
    out = []
    for s in range(depth):
        for j in range(width):
            for h in range(HALVES):
                far_z = lax.rem(z + (depth - s if way(h) > 0 else s), depth)
                far_y = lax.rem(y + width - j, width)
                first = (far_z * width + far_y) * local_count + h * half
                out.append(
                    (((s * width + j) * HALVES + h) * half, pl.multiple_of(first, half), half)
                )
    return out


def to_section_order(slabs, held, pieces):
    rows = held.shape[-2] // len(slabs)
    for ring, first, count in pieces:
        s, r = divmod(ring, rows)
        if len(held.shape) == 3:
            held[:, pl.ds(first, count), :] = slabs[s][:, r : r + count, :].astype(held.dtype)
        else:
            held[pl.ds(first, count), :] = slabs[s][r : r + count, :].astype(held.dtype)


def to_ring_order(held, out, pieces):
    for ring, first, count in pieces:
        if len(held.shape) == 3:
            out[:, ring : ring + count, :] = held[:, pl.ds(first, count), :].astype(out.dtype)
        else:
            out[ring : ring + count, :] = held[pl.ds(first, count), :].astype(out.dtype)


def head_forward(held, gains, rows, lanes):
    query_unit, query_inverse = norm_parts(held[0, rows, lanes])
    key_unit, key_inverse = norm_parts(held[1, rows, lanes])
    query_half = (query_unit * gains[0:1, :]).astype(BF16)
    key_half = (key_unit * gains[1:2, :]).astype(BF16)
    value_half = held[2, rows, lanes].astype(BF16)
    exponent = jnp.exp(dot_nt(query_half, key_half) * (1.0 / math.sqrt(HS)))
    probs = exponent * (1.0 / jnp.sum(exponent, axis=-1, keepdims=True))
    return (
        probs,
        probs.astype(BF16),
        query_half,
        key_half,
        value_half,
        query_unit,
        query_inverse,
        key_unit,
        key_inverse,
    )


def each_head(held):
    row_count, lane_count = held.shape[-2:]
    for image in range(row_count // PATCHES):
        for head in range(lane_count // HS):
            yield (
                image,
                slice(image * PATCHES, (image + 1) * PATCHES),
                slice(head * HS, (head + 1) * HS),
            )


def attend_own_kernel(local_count, depth, width, *refs):
    slabs, gain_ref, out_ref, held, mixed = refs[:depth], *refs[depth:]
    pieces = piece_rows(local_count, depth, width)
    to_section_order(slabs, held, pieces)
    gains = gain_ref[...]
    for _, rows, lanes in each_head(held):
        state = head_forward(held, gains, rows, lanes)
        mixed[rows, lanes] = dot(state[1], state[4]).astype(BF16)
    to_ring_order(mixed, out_ref, pieces)


def attend_margin_kernel(local_count, depth, width, *refs):
    slabs = refs[:depth]
    gain_ref, out_weight_ref, rows_sum_ref, sums_ref, pooled_ref, held = refs[depth:]
    pieces = piece_rows(local_count, depth, width)
    to_section_order(slabs, held, pieces)
    gains = gain_ref[...]
    for image, rows, lanes in each_head(held):
        state = head_forward(held, gains, rows, lanes)
        mixed = dot(state[1], state[4]).astype(BF16)
        sums_ref[image : image + 1, lanes] = jnp.sum(mixed.astype(F32), axis=0, keepdims=True)
    sums = sums_ref[...]
    high = sums.astype(BF16)
    rest = sums - high.astype(F32)
    middle = rest.astype(BF16)
    low = (rest - middle.astype(F32)).astype(BF16)
    weights = out_weight_ref[...]
    pooled_ref[...] = rows_sum_ref[...] + (
        dot(high, weights) + (dot(middle, weights) + dot(low, weights))
    )


def attend_back_kernel(local_count, depth, width, broadcast, *refs):
    slabs = refs[:depth]
    grads = refs[depth : depth + (1 if broadcast else depth)]
    gain_ref, out_ref, held, *grad_held = refs[depth + len(grads) :]
    pieces = piece_rows(local_count, depth, width)
    to_section_order(slabs, held, pieces)
    if not broadcast:
        to_section_order(grads, grad_held[0], pieces)
    gains = gain_ref[...]
    for image, rows, lanes in each_head(held):
        (
            probs,
            probs_half,
            query_half,
            key_half,
            value_half,
            query_unit,
            query_inverse,
            key_unit,
            key_inverse,
        ) = head_forward(held, gains, rows, lanes)
        if broadcast:
            row = grads[0][image : image + 1, lanes].astype(BF16).astype(F32)
            grad_mixed = jnp.broadcast_to(row, (PATCHES, HS)).astype(BF16)
        else:
            grad_mixed = grad_held[0][rows, lanes].astype(BF16)
        grad_probs = dot_nt(grad_mixed, value_half)
        grad_value = dot_tn(probs_half, grad_mixed)
        weighted = probs * grad_probs
        grad_scores = weighted - probs * jnp.sum(weighted, axis=-1, keepdims=True)
        score_half = (grad_scores * (1.0 / math.sqrt(HS))).astype(BF16)
        grad_query = dot(score_half, key_half)
        grad_key = dot_tn(score_half, query_half)
        held[0, rows, lanes] = norm_back(grad_query, query_unit, query_inverse, gains[0:1, :])
        held[1, rows, lanes] = norm_back(grad_key, key_unit, key_inverse, gains[1:2, :])
        held[2, rows, lanes] = grad_value
    to_ring_order(held, out_ref, pieces)


def norm_rows_kernel(rows_ref, gain_ref, *outs):
    unit_rows, _ = norm_parts(rows_ref[...].astype(F32))
    normed = (unit_rows * gain_ref[...]).astype(BF16)
    half = normed.shape[0] // HALVES
    for h in range(HALVES):
        outs[h][...] = normed[h * half : (h + 1) * half]


def norm_margin_kernel(rows_ref, select_ref, gain_ref, *outs):
    norm_rows_kernel(rows_ref, gain_ref, *outs[:HALVES])
    values = rows_ref[...].astype(F32)
    select = select_ref[...]
    for image in range(select.shape[1]):
        outs[HALVES][image : image + 1, :] = jnp.sum(
            values * select[:, image : image + 1], axis=0, keepdims=True
        )


def judge_kernel(
    patch_count,
    pooled_ref,
    gain_ref,
    head_ref,
    label_ref,
    out_weight_ref,
    loss_ref,
    pooled_half_ref,
    grad_logits_ref,
    grad_image_ref,
    per_image_ref,
):
    image_count = pooled_ref.shape[0]
    unit_rows, inverse = norm_parts(pooled_ref[...] * (1.0 / patch_count))
    gain_row = gain_ref[...]
    pooled_half = (unit_rows * gain_row).astype(BF16)
    pooled_half_ref[...] = pooled_half
    head = head_ref[...]
    logits = dot(pooled_half, head)
    classes = lax.broadcasted_iota(jnp.int32, logits.shape, 1)
    images = lax.broadcasted_iota(jnp.int32, logits.shape, 0)
    label = jnp.zeros_like(classes)
    for image in range(image_count):
        label = jnp.where(images == image, label_ref[image], label)
    targets = (classes == label).astype(F32)
    softplus = jnp.maximum(logits, 0.0) + jnp.log1p(jnp.exp(-jnp.abs(logits)))
    loss_ref[...] = jnp.mean(softplus - targets * logits, axis=-1, keepdims=True)
    sigmoid = 1.0 / (1.0 + jnp.exp(-logits))
    grad_logits = ((sigmoid - targets) * (1.0 / image_count)).astype(BF16)
    grad_logits_ref[...] = grad_logits
    grad_pooled = norm_back(dot_nt(grad_logits, head), unit_rows, inverse, gain_row)
    grad_image = grad_pooled * (1.0 / patch_count)
    grad_image_ref[...] = grad_image
    per_image_ref[...] = dot_nt(grad_image.astype(BF16), out_weight_ref[...])


def grad_rows_kernel(*refs):
    halves = refs[:HALVES]
    rows_ref, select_ref, grad_image_ref, gain_ref, out_ref = refs[HALVES:]
    half = rows_ref.shape[0] // HALVES
    for h in range(HALVES):
        rows = slice(h * half, (h + 1) * half)
        unit_rows, inverse = norm_parts(rows_ref[rows, :].astype(F32))
        total = norm_back(halves[h][...], unit_rows, inverse, gain_ref[...])
        for image in range(grad_image_ref.shape[0]):
            total = total + (
                select_ref[rows, image : image + 1] * grad_image_ref[image : image + 1, :]
            )
        out_ref[rows, :] = total.astype(BF16)


def on_device(
    block_inputs, qkv_weights, out_weights, norm_gain, query_key_gain, pool_gain, class_head, labels
):
    rows_in = block_inputs[0]
    qkv_local = qkv_weights[0]
    out_local = out_weights[0]
    gain_pair = query_key_gain[0]
    label_row = labels[0]
    local_count, model_width = rows_in.shape
    image_count = label_row.shape[0]
    class_count = class_head.shape[2]
    depth, width = lax.axis_size("dp"), lax.axis_size("tensor")
    group_size = depth * width
    row_count = local_count * group_size
    lane_count = qkv_local.shape[2]
    half = local_count // HALVES
    place = (local_count, depth, width)
    member = lax.axis_index(GROUP)
    image_ids = (member * local_count + lax.iota(jnp.int32, local_count)) // PATCHES
    own_select = (image_ids[:, None] == lax.iota(jnp.int32, image_count)[None, :]).astype(F32)

    def shape(dims, dtype=F32):
        return jax.ShapeDtypeStruct(dims, dtype)

    half_shapes = [shape((half, model_width), BF16)] * HALVES
    three = (3, row_count, lane_count)
    product_flops = 2 * row_count * lane_count * PATCHES

    def project(slab):
        return jnp.einsum("ij,cjh->cih", slab, qkv_local, preferred_element_type=F32)

    own_halves = call(norm_rows_kernel, half_shapes, (rows_in, norm_gain))
    own_slabs = gather_slabs(own_halves)
    own_projected = [project(slab) for slab in own_slabs]
    attention = call(
        functools.partial(attend_own_kernel, *place),
        shape((row_count, lane_count), BF16),
        (*own_projected, gain_pair),
        scratch=[pltpu.VMEM(three, F32), pltpu.VMEM(three[1:], BF16)],
        flops=2 * product_flops,
    )
    slab_rows = local_count * width

    def out_term(s):
        return dot(attention[s * slab_rows : (s + 1) * slab_rows], out_local)

    branch = jnp.concatenate(scatter_slabs(out_term), axis=0)
    out_own = (rows_in.astype(F32) + branch).astype(BF16)

    received = from_behind(out_own, "section", 1)
    margin_in = jnp.where(lax.axis_index("section") == 0, rows_in, received)
    *margin_halves, rows_sum = call(
        norm_margin_kernel,
        half_shapes + [shape((image_count, model_width))],
        (margin_in, own_select, norm_gain),
    )
    margin_slabs = gather_slabs(margin_halves)
    margin_projected = [project(slab) for slab in margin_slabs]
    image_sums, pooled_part = call(
        functools.partial(attend_margin_kernel, *place),
        [shape((image_count, lane_count)), shape((image_count, model_width))],
        (*margin_projected, gain_pair, out_local, rows_sum),
        scratch=[pltpu.VMEM(three, F32)],
        flops=2 * product_flops,
    )
    pooled = sum_group(pooled_part)
    losses, pooled_half, grad_logits, grad_image, per_image = call(
        functools.partial(judge_kernel, PATCHES),
        [
            shape((image_count, 1)),
            shape((image_count, model_width), BF16),
            shape((image_count, class_count), BF16),
            shape((image_count, model_width)),
            shape((image_count, lane_count)),
        ],
        (pooled, pool_gain, class_head[0], label_row, out_local),
        specs=[VMEM_SPEC] * 3 + [SMEM_SPEC, VMEM_SPEC],
        flops=4 * class_count * model_width * 8,
    )
    slice_width = model_width // group_size
    pooled_slice = lax.dynamic_slice_in_dim(pooled_half, member * slice_width, slice_width, 1)
    grad_head = jnp.einsum("id,ic->dc", pooled_slice, grad_logits, preferred_element_type=F32)

    margin_gradient = call(
        functools.partial(attend_back_kernel, *place, True),
        shape(three, BF16),
        (*margin_projected, per_image, gain_pair),
        scratch=[pltpu.VMEM(three, F32)],
        flops=7 * product_flops,
    )

    def input_term(s):
        return jnp.einsum(
            "hsx,hbx->sb",
            margin_gradient[:, s * slab_rows : (s + 1) * slab_rows],
            qkv_local,
            preferred_element_type=F32,
        )

    grad_normed = scatter_slabs(input_term)
    grad_inputs = call(
        grad_rows_kernel,
        shape((local_count, model_width), BF16),
        (*grad_normed, margin_in, own_select, grad_image, norm_gain),
    )
    grad_qkv_margin = jnp.einsum(
        "bp,sbn->spn",
        jnp.concatenate(margin_slabs, axis=0),
        margin_gradient,
        preferred_element_type=F32,
    )
    grad_out_margin = jnp.dot(
        image_sums.T, grad_image.astype(BF16).astype(F32), precision=lax.Precision.HIGHEST
    )

    returned = from_behind(grad_inputs, "section", -1)
    cotangent_slabs = gather_slabs([returned[h * half : (h + 1) * half] for h in range(HALVES)])
    grad_attention = [dot_nt(slab, out_local) for slab in cotangent_slabs]
    own_gradient = call(
        functools.partial(attend_back_kernel, *place, False),
        shape(three, BF16),
        (*own_projected, *grad_attention, gain_pair),
        scratch=[pltpu.VMEM(three, F32), pltpu.VMEM(three[1:], F32)],
        flops=7 * product_flops,
    )
    grad_qkv_own = jnp.einsum(
        "bp,sbn->spn", jnp.concatenate(own_slabs, axis=0), own_gradient, preferred_element_type=F32
    )
    grad_out_own = dot_tn(attention, jnp.concatenate(cotangent_slabs, axis=0))
    query_key_value_gradient = (grad_qkv_margin + grad_qkv_own).astype(BF16)
    grad_out = (grad_out_margin + grad_out_own).astype(BF16)
    return (
        out_own[None],
        query_key_value_gradient[None],
        grad_out[None],
        grad_head.astype(BF16)[None],
        losses.reshape(1, image_count),
    )


def solution(mesh):
    in_specs = (
        P("section", GROUP, None),
        P("section", None, None, GROUP),
        P("section", GROUP, None),
        P("section", None),
        P("section", None, None),
        P("section", None),
        P("section", None, None),
        P("section", None),
    )
    out_specs = (
        P("section", GROUP, None),
        P("section", None, None, GROUP),
        P("section", GROUP, None),
        P("section", GROUP, None),
        P("section", None),
    )
    return jax.shard_map(
        on_device, mesh=mesh, in_specs=in_specs, out_specs=out_specs, check_vma=False
    )
```

```python
import functools
import math

import jax
import jax.numpy as jnp
from jax import lax
from jax.experimental import pallas as pl
from jax.experimental.pallas import tpu as pltpu
from jax.sharding import PartitionSpec as P

HS = 128
PATCHES = 256
GROUP = ("dp", "tensor")
HALVES = 2

epsilon = 1e-06
F32 = jnp.float32
BF16 = jnp.bfloat16
VMEM_SPEC = pl.BlockSpec(memory_space=pltpu.VMEM)
SMEM_SPEC = pl.BlockSpec(memory_space=pltpu.SMEM)


def from_behind(block, axis, distance):
    devices = range(lax.axis_size(axis))
    route = [(i - distance, i) for i in devices if i - distance in devices]
    return lax.ppermute(block, axis, route)


def shift(block, axis, distance):
    count = lax.axis_size(axis)
    return lax.ppermute(block, axis, [(i, (i + distance) % count) for i in range(count)])


def after(value, *others):
    return lax.optimization_barrier((value,) + others)[0]


def way(half):
    return 1 if half % 2 == 0 else -1


def balanced(depth, width):
    return width == 2 and depth > 2


def gather_slabs(halves):
    depth, width = lax.axis_size("dp"), lax.axis_size("tensor")
    ring = [list(halves)]
    across = [[[shift(h, "tensor", j) for h in halves] for j in range(1, width)]]
    for s in range(1, depth):
        ring.append([shift(ring[-1][h], "dp", way(h)) for h in range(HALVES)])
        if s == depth - 1 and balanced(depth, width):
            quarter = ring[s][0].shape[0] // 2
            shared = []
            for h in range(HALVES):
                own, other = ring[s][h], across[-1][0][h]
                shared.append(shift(after(own[:quarter], other), "tensor", 1))
                shared.append(shift(after(other[quarter:], own), "dp", way(h)))
            across.append([shared])
            break
        across.append(
            [
                [
                    shift(after(ring[-1][h], across[-1][j - 1][h]), "tensor", j)
                    for h in range(HALVES)
                ]
                for j in range(1, width)
            ]
        )
    return [ring[s] + [p for place in across[s] for p in place] for s in range(depth)]


def scatter_slabs(slab_term):
    depth, width = lax.axis_size("dp"), lax.axis_size("tensor")
    share = balanced(depth, width)
    running = [None] * HALVES
    along = [None] * HALVES
    last = [[None] * HALVES for _ in range(width)]
    for s in list(range(1, depth)) + [0]:
        term = slab_term(s)
        half = term.shape[0] // (width * HALVES)
        quarter = half // 2
        for h in range(HALVES):
            total = term[h * half : (h + 1) * half]
            for j in range(1, width):
                start = (j * HALVES + h) * half
                piece = term[start : start + half]
                if share and s == 1:
                    top, low = piece[:quarter].astype(BF16), piece[quarter:].astype(BF16)
                    last[j][h] = shift(top, "tensor", -j)
                    along[h] = shift(low, "dp", way(h))
                    total = jnp.concatenate(
                        [total[:quarter] + last[j][h].astype(F32), total[quarter:]], axis=0
                    )
                    continue
                if share and s == 2:
                    piece = jnp.concatenate(
                        [piece[:quarter], piece[quarter:] + along[h].astype(F32)], axis=0
                    )
                piece = piece.astype(BF16)
                if last[j][h] is not None:
                    piece = after(piece, last[j][h])
                last[j][h] = shift(piece, "tensor", -j)
                total = total + last[j][h].astype(F32)
            if running[h] is not None:
                total = total + shift(running[h], "dp", way(h)).astype(F32)
            running[h] = total if s == 0 else total.astype(BF16)
    return running


def sum_group(value):
    for axis in ("tensor", "dp"):
        count = lax.axis_size(axis)
        if count & (count - 1):
            return lax.psum(value, GROUP)
    for axis in ("tensor", "dp"):
        step = 1
        while step < lax.axis_size(axis):
            route = [(i, i ^ step) for i in range(lax.axis_size(axis))]
            value = value + lax.ppermute(value, axis, route)
            step *= 2
    return value


def norm_parts(values):
    centered = values - jnp.mean(values, axis=-1, keepdims=True)
    inverse = lax.rsqrt(jnp.mean(centered * centered, axis=-1, keepdims=True) + epsilon)
    return centered * inverse, inverse


def norm_back(grad_normed, unit_rows, inverse, gain_row):
    scaled = grad_normed * gain_row
    return inverse * (
        scaled
        - jnp.mean(scaled, axis=-1, keepdims=True)
        - unit_rows * jnp.mean(scaled * unit_rows, axis=-1, keepdims=True)
    )


def dot_nt(left, right):
    return lax.dot_general(left, right, (((1,), (1,)), ((), ())), preferred_element_type=F32)


def dot_tn(left, right):
    return lax.dot_general(left, right, (((0,), (0,)), ((), ())), preferred_element_type=F32)


def dot(left, right):
    return jnp.dot(left, right, preferred_element_type=F32)


def call(kernel, out_shape, ins, specs=None, scratch=(), flops=0, moved=1000000, limit=24):
    many = isinstance(out_shape, (tuple, list))
    return pl.pallas_call(
        kernel,
        out_shape=out_shape,
        in_specs=specs or [VMEM_SPEC] * len(ins),
        out_specs=[VMEM_SPEC] * len(out_shape) if many else VMEM_SPEC,
        scratch_shapes=list(scratch),
        compiler_params=pltpu.CompilerParams(vmem_limit_bytes=limit * 2**20),
        cost_estimate=pl.CostEstimate(flops=flops, bytes_accessed=moved, transcendentals=0),
    )(*ins)


def piece_rows(local_count, depth, width):
    half = local_count // HALVES
    z, y = lax.axis_index("dp"), lax.axis_index("tensor")
    out = []
    for s in range(depth):
        for j in range(width):
            for h in range(HALVES):
                far_z = lax.rem(z + (depth - s if way(h) > 0 else s), depth)
                far_y = lax.rem(y + width - j, width)
                first = (far_z * width + far_y) * local_count + h * half
                out.append(
                    (((s * width + j) * HALVES + h) * half, pl.multiple_of(first, half), half)
                )
    return out


def to_section_order(slabs, held, pieces):
    rows = held.shape[-2] // len(slabs)
    for ring, first, count in pieces:
        s, r = divmod(ring, rows)
        if len(held.shape) == 3:
            held[:, pl.ds(first, count), :] = slabs[s][:, r : r + count, :].astype(held.dtype)
        else:
            held[pl.ds(first, count), :] = slabs[s][r : r + count, :].astype(held.dtype)


def to_ring_order(held, out, pieces):
    for ring, first, count in pieces:
        if len(held.shape) == 3:
            out[:, ring : ring + count, :] = held[:, pl.ds(first, count), :].astype(out.dtype)
        else:
            out[ring : ring + count, :] = held[pl.ds(first, count), :].astype(out.dtype)


def head_forward(held, gains, rows, lanes):
    query_unit, query_inverse = norm_parts(held[0, rows, lanes])
    key_unit, key_inverse = norm_parts(held[1, rows, lanes])
    query_half = (query_unit * gains[0:1, :]).astype(BF16)
    key_half = (key_unit * gains[1:2, :]).astype(BF16)
    value_half = held[2, rows, lanes].astype(BF16)
    exponent = jnp.exp(dot_nt(query_half, key_half) * (1.0 / math.sqrt(HS)))
    probs = exponent * (1.0 / jnp.sum(exponent, axis=-1, keepdims=True))
    return (
        probs,
        probs.astype(BF16),
        query_half,
        key_half,
        value_half,
        query_unit,
        query_inverse,
        key_unit,
        key_inverse,
    )


def each_head(held):
    row_count, lane_count = held.shape[-2:]
    for image in range(row_count // PATCHES):
        for head in range(lane_count // HS):
            yield (
                image,
                slice(image * PATCHES, (image + 1) * PATCHES),
                slice(head * HS, (head + 1) * HS),
            )


def attend_own_kernel(local_count, depth, width, *refs):
    slabs, gain_ref, out_ref, held, mixed = refs[:depth], *refs[depth:]
    pieces = piece_rows(local_count, depth, width)
    to_section_order(slabs, held, pieces)
    gains = gain_ref[...]
    for _, rows, lanes in each_head(held):
        state = head_forward(held, gains, rows, lanes)
        mixed[rows, lanes] = dot(state[1], state[4]).astype(BF16)
    to_ring_order(mixed, out_ref, pieces)


def attend_margin_kernel(local_count, depth, width, *refs):
    slabs = refs[:depth]
    gain_ref, out_weight_ref, select_ref = refs[depth : depth + 3]
    rows = refs[depth + 3 : depth + 3 + HALVES]
    sums_ref, pooled_ref, held = refs[depth + 3 + HALVES :]
    select = select_ref[...]
    rows_own = jnp.concatenate([ref[...] for ref in rows], axis=0).astype(F32)
    for image in range(select.shape[1]):
        pooled_ref[image : image + 1, :] = jnp.sum(
            rows_own * select[:, image : image + 1], axis=0, keepdims=True
        )
    pieces = piece_rows(local_count, depth, width)
    to_section_order(slabs, held, pieces)
    gains = gain_ref[...]
    for image, rows, lanes in each_head(held):
        state = head_forward(held, gains, rows, lanes)
        mixed = dot(state[1], state[4]).astype(BF16)
        sums_ref[image : image + 1, lanes] = jnp.sum(mixed.astype(F32), axis=0, keepdims=True)
    sums = sums_ref[...]
    high = sums.astype(BF16)
    rest = sums - high.astype(F32)
    middle = rest.astype(BF16)
    low = (rest - middle.astype(F32)).astype(BF16)
    weights = out_weight_ref[...]
    pooled_ref[...] = pooled_ref[...] + (
        dot(high, weights) + (dot(middle, weights) + dot(low, weights))
    )


def attend_back_kernel(local_count, depth, width, broadcast, *refs):
    slabs = refs[:depth]
    grads = refs[depth : depth + (1 if broadcast else depth)]
    gain_ref, out_ref, held, *grad_held = refs[depth + len(grads) :]
    pieces = piece_rows(local_count, depth, width)
    to_section_order(slabs, held, pieces)
    if not broadcast:
        to_section_order(grads, grad_held[0], pieces)
    gains = gain_ref[...]
    for image, rows, lanes in each_head(held):
        (
            probs,
            probs_half,
            query_half,
            key_half,
            value_half,
            query_unit,
            query_inverse,
            key_unit,
            key_inverse,
        ) = head_forward(held, gains, rows, lanes)
        if broadcast:
            row = grads[0][image : image + 1, lanes].astype(BF16).astype(F32)
            grad_mixed = jnp.broadcast_to(row, (PATCHES, HS)).astype(BF16)
        else:
            grad_mixed = grad_held[0][rows, lanes].astype(BF16)
        grad_probs = dot_nt(grad_mixed, value_half)
        grad_value = dot_tn(probs_half, grad_mixed)
        weighted = probs * grad_probs
        grad_scores = weighted - probs * jnp.sum(weighted, axis=-1, keepdims=True)
        score_half = (grad_scores * (1.0 / math.sqrt(HS))).astype(BF16)
        grad_query = dot(score_half, key_half)
        grad_key = dot_tn(score_half, query_half)
        held[0, rows, lanes] = norm_back(grad_query, query_unit, query_inverse, gains[0:1, :])
        held[1, rows, lanes] = norm_back(grad_key, key_unit, key_inverse, gains[1:2, :])
        held[2, rows, lanes] = grad_value
    to_ring_order(held, out_ref, pieces)


def project_kernel(*refs):
    weights_ref, projected_ref, turned_ref = refs[-3:]
    rows = jnp.concatenate([ref[...] for ref in refs[:-3]], axis=0)
    for t in range(weights_ref.shape[0]):
        projected_ref[t, :, :] = dot(rows, weights_ref[t])
    turned_ref[...] = rows.T


def cotangent_kernel(*refs):
    weights_ref, out_ref = refs[-2:]
    rows = jnp.concatenate([ref[...] for ref in refs[:-2]], axis=0)
    out_ref[...] = dot_nt(rows, weights_ref[...])


def input_kernel(first, count, gradient_ref, weights_ref, out_ref):
    rows = slice(first, first + count)
    total = dot_nt(gradient_ref[0, rows, :], weights_ref[0])
    for t in range(1, weights_ref.shape[0]):
        total = total + dot_nt(gradient_ref[t, rows, :], weights_ref[t])
    out_ref[...] = total


def weight_gradient_kernel(depth, *refs):
    turned = jnp.concatenate([ref[...] for ref in refs[:depth]], axis=1)
    gradient_ref, *added, out_ref = refs[depth:]
    for t in range(gradient_ref.shape[0]):
        total = dot(turned, gradient_ref[t])
        if added:
            total = total + added[0][t].astype(F32)
        out_ref[t, :, :] = total.astype(BF16)


def out_gradient_kernel(*refs):
    attention_ref, sums_ref, grad_image_ref, out_ref = refs[-4:]
    cotangent = jnp.concatenate([ref[...] for ref in refs[:-4]], axis=0)
    total = dot_tn(attention_ref[...], cotangent)
    sums = sums_ref[...]
    grad_image = grad_image_ref[...].astype(BF16).astype(F32)
    for image in range(sums.shape[1]):
        total = total + sums[:, image : image + 1] * grad_image[image : image + 1, :]
    out_ref[...] = total.astype(BF16)


def norm_rows_kernel(rows_ref, gain_ref, out_ref):
    unit_rows, _ = norm_parts(rows_ref[...].astype(F32))
    out_ref[...] = (unit_rows * gain_ref[...]).astype(BF16)


def judge_kernel(
    patch_count,
    pooled_ref,
    gain_ref,
    head_ref,
    label_ref,
    out_weight_ref,
    loss_ref,
    pooled_half_ref,
    grad_logits_ref,
    grad_image_ref,
    per_image_ref,
):
    image_count = pooled_ref.shape[0]
    unit_rows, inverse = norm_parts(pooled_ref[...] * (1.0 / patch_count))
    gain_row = gain_ref[...]
    pooled_half = (unit_rows * gain_row).astype(BF16)
    pooled_half_ref[...] = pooled_half
    head = head_ref[...]
    logits = dot(pooled_half, head)
    classes = lax.broadcasted_iota(jnp.int32, logits.shape, 1)
    images = lax.broadcasted_iota(jnp.int32, logits.shape, 0)
    label = jnp.zeros_like(classes)
    for image in range(image_count):
        label = jnp.where(images == image, label_ref[image], label)
    targets = (classes == label).astype(F32)
    softplus = jnp.maximum(logits, 0.0) + jnp.log1p(jnp.exp(-jnp.abs(logits)))
    loss_ref[...] = jnp.mean(softplus - targets * logits, axis=-1, keepdims=True)
    sigmoid = 1.0 / (1.0 + jnp.exp(-logits))
    grad_logits = ((sigmoid - targets) * (1.0 / image_count)).astype(BF16)
    grad_logits_ref[...] = grad_logits
    grad_pooled = norm_back(dot_nt(grad_logits, head), unit_rows, inverse, gain_row)
    grad_image = grad_pooled * (1.0 / patch_count)
    grad_image_ref[...] = grad_image
    per_image_ref[...] = dot_nt(grad_image.astype(BF16), out_weight_ref[...])


def grad_rows_kernel(grad_ref, rows_ref, select_ref, grad_image_ref, gain_ref, out_ref):
    unit_rows, inverse = norm_parts(rows_ref[...].astype(F32))
    total = norm_back(grad_ref[...], unit_rows, inverse, gain_ref[...])
    select = select_ref[...]
    for image in range(grad_image_ref.shape[0]):
        total = total + select[:, image : image + 1] * grad_image_ref[image : image + 1, :]
    out_ref[...] = total.astype(BF16)


def on_device(
    block_inputs, qkv_weights, out_weights, norm_gain, query_key_gain, pool_gain, class_head, labels
):
    rows_in = block_inputs[0]
    qkv_local = qkv_weights[0]
    out_local = out_weights[0]
    gain_pair = query_key_gain[0]
    label_row = labels[0]
    local_count, model_width = rows_in.shape
    image_count = label_row.shape[0]
    class_count = class_head.shape[2]
    depth, width = lax.axis_size("dp"), lax.axis_size("tensor")
    group_size = depth * width
    row_count = local_count * group_size
    lane_count = qkv_local.shape[2]
    half = local_count // HALVES
    place = (local_count, depth, width)
    member = lax.axis_index(GROUP)
    image_ids = (member * local_count + lax.iota(jnp.int32, local_count)) // PATCHES
    own_select = (image_ids[:, None] == lax.iota(jnp.int32, image_count)[None, :]).astype(F32)

    def shape(dims, dtype=F32):
        return jax.ShapeDtypeStruct(dims, dtype)

    half_shape = shape((half, model_width), BF16)
    three = (3, row_count, lane_count)
    slab_rows = local_count * width
    product_flops = 2 * row_count * lane_count * PATCHES
    slab_flops = 2 * slab_rows * model_width * lane_count

    def halves_of(rows):
        return [rows[h * half : (h + 1) * half] for h in range(HALVES)]

    def norm_rows(rows):
        return call(norm_rows_kernel, half_shape, (rows, norm_gain))

    def project(slab):
        return call(
            project_kernel,
            [shape((3, slab_rows, lane_count)), shape((model_width, slab_rows), BF16)],
            (*slab, qkv_local),
            flops=3 * slab_flops,
        )

    def weight_gradient(turned, gradient, *added):
        chunk = PATCHES * 2 if model_width % (PATCHES * 2) == 0 else PATCHES
        block = pl.BlockSpec((3, chunk, lane_count), lambda i: (0, i, 0))
        return pl.pallas_call(
            functools.partial(weight_gradient_kernel, depth),
            grid=(model_width // chunk,),
            out_shape=shape((3, model_width, lane_count), BF16),
            in_specs=[pl.BlockSpec((chunk, slab_rows), lambda i: (i, 0))] * depth
            + [pl.BlockSpec(three, lambda i: (0, 0, 0))]
            + [block] * len(added),
            out_specs=block,
            compiler_params=pltpu.CompilerParams(vmem_limit_bytes=24 * 2**20),
            cost_estimate=pl.CostEstimate(
                flops=3 * depth * slab_flops,
                bytes_accessed=6 * model_width * lane_count,
                transcendentals=0,
            ),
        )(*turned, gradient, *added)

    own_slabs = gather_slabs([norm_rows(rows) for rows in halves_of(rows_in)])
    own_projected, own_turned = zip(*[project(slab) for slab in own_slabs])
    attention = call(
        functools.partial(attend_own_kernel, *place),
        shape((row_count, lane_count), BF16),
        (*own_projected, gain_pair),
        scratch=[pltpu.VMEM(three, F32), pltpu.VMEM(three[1:], BF16)],
        flops=2 * product_flops,
    )

    def out_term(s):
        return dot(attention[s * slab_rows : (s + 1) * slab_rows], out_local)

    out_halves = [
        (rows.astype(F32) + branch).astype(BF16)
        for rows, branch in zip(halves_of(rows_in), scatter_slabs(out_term))
    ]

    first = lax.axis_index("section") == 0
    margin_halves = [
        jnp.where(first, rows, from_behind(out, "section", 1))
        for rows, out in zip(halves_of(rows_in), out_halves)
    ]
    margin_slabs = gather_slabs([norm_rows(rows) for rows in margin_halves])
    margin_projected, margin_turned = zip(*[project(slab) for slab in margin_slabs])
    image_sums, pooled_part = call(
        functools.partial(attend_margin_kernel, *place),
        [shape((image_count, lane_count)), shape((image_count, model_width))],
        (*margin_projected, gain_pair, out_local, own_select, *margin_halves),
        scratch=[pltpu.VMEM(three, F32)],
        flops=2 * product_flops,
    )
    pooled = sum_group(pooled_part)
    losses, pooled_half, grad_logits, grad_image, per_image = call(
        functools.partial(judge_kernel, PATCHES),
        [
            shape((image_count, 1)),
            shape((image_count, model_width), BF16),
            shape((image_count, class_count), BF16),
            shape((image_count, model_width)),
            shape((image_count, lane_count)),
        ],
        (pooled, pool_gain, class_head[0], label_row, out_local),
        specs=[VMEM_SPEC] * 3 + [SMEM_SPEC, VMEM_SPEC],
        flops=4 * class_count * model_width * 8,
    )
    slice_width = model_width // group_size
    pooled_slice = lax.dynamic_slice_in_dim(pooled_half, member * slice_width, slice_width, 1)
    grad_head = jnp.einsum("id,ic->dc", pooled_slice, grad_logits, preferred_element_type=F32)

    margin_gradient = call(
        functools.partial(attend_back_kernel, *place, True),
        shape(three, BF16),
        (*margin_projected, per_image, gain_pair),
        scratch=[pltpu.VMEM(three, F32)],
        flops=7 * product_flops,
    )

    def input_term(s):
        return call(
            functools.partial(input_kernel, s * slab_rows, slab_rows),
            shape((slab_rows, model_width)),
            (margin_gradient, qkv_local),
            flops=3 * slab_flops,
        )

    grad_normed = scatter_slabs(input_term)
    grad_inputs = [
        call(grad_rows_kernel, half_shape, (grad, rows, select, grad_image, norm_gain))
        for grad, rows, select in zip(grad_normed, margin_halves, halves_of(own_select))
    ]
    grad_qkv_margin = weight_gradient(margin_turned, margin_gradient)

    returned = [from_behind(grad, "section", -1) for grad in grad_inputs]
    cotangent_slabs = gather_slabs(returned)
    grad_attention = [
        call(
            cotangent_kernel,
            shape((slab_rows, lane_count)),
            (*slab, out_local),
            flops=slab_flops,
        )
        for slab in cotangent_slabs
    ]
    own_gradient = call(
        functools.partial(attend_back_kernel, *place, False),
        shape(three, BF16),
        (*own_projected, *grad_attention, gain_pair),
        scratch=[pltpu.VMEM(three, F32), pltpu.VMEM(three[1:], F32)],
        flops=7 * product_flops,
    )
    query_key_value_gradient = weight_gradient(own_turned, own_gradient, grad_qkv_margin)
    pieces = [piece for slab in cotangent_slabs for piece in slab]
    chunk = 2 * PATCHES if model_width % (2 * PATCHES) == 0 else PATCHES
    grad_out = pl.pallas_call(
        out_gradient_kernel,
        grid=(model_width // chunk,),
        out_shape=shape((lane_count, model_width), BF16),
        in_specs=[pl.BlockSpec((piece.shape[0], chunk), lambda i: (0, i)) for piece in pieces]
        + [
            pl.BlockSpec((row_count, lane_count), lambda i: (0, 0)),
            pl.BlockSpec((lane_count, image_count), lambda i: (0, 0)),
            pl.BlockSpec((image_count, chunk), lambda i: (0, i)),
        ],
        out_specs=pl.BlockSpec((lane_count, chunk), lambda i: (0, i)),
        compiler_params=pltpu.CompilerParams(vmem_limit_bytes=24 * 2**20),
        cost_estimate=pl.CostEstimate(
            flops=depth * slab_flops,
            bytes_accessed=4 * model_width * lane_count,
            transcendentals=0,
        ),
    )(*pieces, attention, image_sums.T, grad_image)
    return (
        jnp.concatenate(out_halves, axis=0)[None],
        query_key_value_gradient[None],
        grad_out[None],
        grad_head.astype(BF16)[None],
        losses.reshape(1, image_count),
    )


def solution(mesh):
    in_specs = (
        P("section", GROUP, None),
        P("section", None, None, GROUP),
        P("section", GROUP, None),
        P("section", None),
        P("section", None, None),
        P("section", None),
        P("section", None, None),
        P("section", None),
    )
    out_specs = (
        P("section", GROUP, None),
        P("section", None, None, GROUP),
        P("section", GROUP, None),
        P("section", GROUP, None),
        P("section", None),
    )
    return jax.shard_map(
        on_device, mesh=mesh, in_specs=in_specs, out_specs=out_specs, check_vma=False
    )
```

```python
import functools
import math

import jax
import jax.numpy as jnp
from jax import lax
from jax.experimental import pallas as pl
from jax.experimental.pallas import tpu as pltpu
from jax.sharding import PartitionSpec as P

HS = 128
PATCHES = 256
GROUP = ("dp", "tensor")
HALVES = 2

epsilon = 1e-06
F32 = jnp.float32
BF16 = jnp.bfloat16
VMEM_SPEC = pl.BlockSpec(memory_space=pltpu.VMEM)
SMEM_SPEC = pl.BlockSpec(memory_space=pltpu.SMEM)


def from_behind(block, axis, distance):
    devices = range(lax.axis_size(axis))
    route = [(i - distance, i) for i in devices if i - distance in devices]
    return lax.ppermute(block, axis, route)


def shift(block, axis, distance):
    count = lax.axis_size(axis)
    return lax.ppermute(block, axis, [(i, (i + distance) % count) for i in range(count)])


def after(value, *others):
    return lax.optimization_barrier((value,) + others)[0]


def way(half):
    return 1 if half % 2 == 0 else -1


def gather_slabs(halves, work):
    depth, width = lax.axis_size("dp"), lax.axis_size("tensor")
    ring, slabs, results = [list(halves)], [], []
    across = [[None] * HALVES for _ in range(width)]
    for s in range(depth):
        if s:
            ring.append([shift(ring[-1][h], "dp", way(h)) for h in range(HALVES)])
        pieces = list(ring[s])
        for j in range(1, width):
            for h in range(HALVES):
                piece = ring[s][h]
                if s:
                    piece = after(piece, across[j][h], *results[: s - 1][-1:])
                across[j][h] = shift(piece, "tensor", j)
                pieces.append(across[j][h])
        slabs.append(pieces)
        results.append(work(s, pieces))
    return slabs, results


def scatter_slabs(slab_pieces):
    depth, width = lax.axis_size("dp"), lax.axis_size("tensor")
    running = [None] * HALVES
    last = [[None] * HALVES for _ in range(width)]
    for s in list(range(1, depth)) + [0]:
        terms = slab_pieces(s)
        for h in range(HALVES):
            total = terms[h].astype(F32)
            for j in range(1, width):
                piece = terms[j * HALVES + h]
                if last[j][h] is not None:
                    piece = after(piece, last[j][h])
                last[j][h] = shift(piece, "tensor", -j)
                total = total + last[j][h].astype(F32)
            if running[h] is not None:
                total = total + shift(running[h], "dp", way(h)).astype(F32)
            running[h] = total if s == 0 else total.astype(BF16)
    return running


def exchange(value, axis, steps):
    route = [(i, i ^ steps) for i in range(lax.axis_size(axis))]
    return lax.ppermute(value, axis, route)


def sum_group(value):
    counts = [lax.axis_size(axis) for axis in ("tensor", "dp")]
    if any(count & (count - 1) for count in counts):
        return lax.psum(value, GROUP)
    for axis, count in zip(("tensor", "dp"), counts):
        parts = [value] + [exchange(value, axis, step) for step in range(1, count)]
        while len(parts) > 1:
            parts = [parts[i] + parts[i + 1] for i in range(0, len(parts), 2)]
        value = parts[0]
    return value


def norm_parts(values):
    centered = values - jnp.mean(values, axis=-1, keepdims=True)
    inverse = lax.rsqrt(jnp.mean(centered * centered, axis=-1, keepdims=True) + epsilon)
    return centered * inverse, inverse


def norm_back(grad_normed, unit_rows, inverse, gain_row):
    scaled = grad_normed * gain_row
    return inverse * (
        scaled
        - jnp.mean(scaled, axis=-1, keepdims=True)
        - unit_rows * jnp.mean(scaled * unit_rows, axis=-1, keepdims=True)
    )


def dot_nt(left, right):
    return lax.dot_general(left, right, (((1,), (1,)), ((), ())), preferred_element_type=F32)


def dot_tn(left, right):
    return lax.dot_general(left, right, (((0,), (0,)), ((), ())), preferred_element_type=F32)


def dot(left, right):
    return jnp.dot(left, right, preferred_element_type=F32)


def call(kernel, out_shape, ins, specs=None, scratch=(), flops=0, moved=1000000, limit=24):
    many = isinstance(out_shape, (tuple, list))
    return pl.pallas_call(
        kernel,
        out_shape=out_shape,
        in_specs=specs or [VMEM_SPEC] * len(ins),
        out_specs=[VMEM_SPEC] * len(out_shape) if many else VMEM_SPEC,
        scratch_shapes=list(scratch),
        compiler_params=pltpu.CompilerParams(vmem_limit_bytes=limit * 2**20),
        cost_estimate=pl.CostEstimate(flops=flops, bytes_accessed=moved, transcendentals=0),
    )(*ins)


def piece_rows(local_count, depth, width):
    half = local_count // HALVES
    z, y = lax.axis_index("dp"), lax.axis_index("tensor")
    out = []
    for s in range(depth):
        for j in range(width):
            for h in range(HALVES):
                far_z = lax.rem(z + (depth - s if way(h) > 0 else s), depth)
                far_y = lax.rem(y + width - j, width)
                first = (far_z * width + far_y) * local_count + h * half
                out.append(
                    (((s * width + j) * HALVES + h) * half, pl.multiple_of(first, half), half)
                )
    return out


def to_section_order(slabs, held, pieces):
    rows = held.shape[-2] // len(slabs)
    for ring, first, count in pieces:
        s, r = divmod(ring, rows)
        if len(held.shape) == 3:
            held[:, pl.ds(first, count), :] = slabs[s][:, r : r + count, :].astype(held.dtype)
        else:
            held[pl.ds(first, count), :] = slabs[s][r : r + count, :].astype(held.dtype)


def to_ring_order(held, out, pieces):
    for ring, first, count in pieces:
        if len(held.shape) == 3:
            out[:, ring : ring + count, :] = held[:, pl.ds(first, count), :].astype(out.dtype)
        else:
            out[ring : ring + count, :] = held[pl.ds(first, count), :].astype(out.dtype)


def head_forward(held, gains, rows, lanes):
    query_unit, query_inverse = norm_parts(held[0, rows, lanes])
    key_unit, key_inverse = norm_parts(held[1, rows, lanes])
    query_half = (query_unit * gains[0:1, :]).astype(BF16)
    key_half = (key_unit * gains[1:2, :]).astype(BF16)
    value_half = held[2, rows, lanes].astype(BF16)
    exponent = jnp.exp(dot_nt(query_half, key_half) * (1.0 / math.sqrt(HS)))
    probs = exponent * (1.0 / jnp.sum(exponent, axis=-1, keepdims=True))
    return (
        probs,
        probs.astype(BF16),
        query_half,
        key_half,
        value_half,
        query_unit,
        query_inverse,
        key_unit,
        key_inverse,
    )


def each_head(held):
    row_count, lane_count = held.shape[-2:]
    for image in range(row_count // PATCHES):
        for head in range(lane_count // HS):
            yield (
                image,
                slice(image * PATCHES, (image + 1) * PATCHES),
                slice(head * HS, (head + 1) * HS),
            )


def attend_own_kernel(local_count, depth, width, *refs):
    slabs, gain_ref, out_ref, held, mixed = refs[:depth], *refs[depth:]
    pieces = piece_rows(local_count, depth, width)
    to_section_order(slabs, held, pieces)
    gains = gain_ref[...]
    for _, rows, lanes in each_head(held):
        state = head_forward(held, gains, rows, lanes)
        mixed[rows, lanes] = dot(state[1], state[4]).astype(BF16)
    to_ring_order(mixed, out_ref, pieces)


def attend_margin_kernel(local_count, depth, width, *refs):
    slabs = refs[:depth]
    gain_ref, out_weight_ref, select_ref = refs[depth : depth + 3]
    rows = refs[depth + 3 : depth + 3 + HALVES]
    sums_ref, pooled_ref, held = refs[depth + 3 + HALVES :]
    select = select_ref[...]
    rows_own = jnp.concatenate([ref[...] for ref in rows], axis=0).astype(F32)
    for image in range(select.shape[1]):
        pooled_ref[image : image + 1, :] = jnp.sum(
            rows_own * select[:, image : image + 1], axis=0, keepdims=True
        )
    pieces = piece_rows(local_count, depth, width)
    to_section_order(slabs, held, pieces)
    gains = gain_ref[...]
    for image, rows, lanes in each_head(held):
        state = head_forward(held, gains, rows, lanes)
        mixed = dot(state[1], state[4]).astype(BF16)
        sums_ref[image : image + 1, lanes] = jnp.sum(mixed.astype(F32), axis=0, keepdims=True)
    sums = sums_ref[...]
    high = sums.astype(BF16)
    rest = sums - high.astype(F32)
    middle = rest.astype(BF16)
    low = (rest - middle.astype(F32)).astype(BF16)
    weights = out_weight_ref[...]
    pooled_ref[...] = pooled_ref[...] + (
        dot(high, weights) + (dot(middle, weights) + dot(low, weights))
    )


def state_kernel(local_count, depth, width, *refs):
    slabs = refs[:depth]
    gain_ref, probs_ref, turned_ref, halves_ref, units_ref, inverse_ref, held = refs[depth:]
    to_section_order(slabs, held, piece_rows(local_count, depth, width))
    gains = gain_ref[...]
    for place, (_, rows, lanes) in enumerate(each_head(held)):
        head = lanes.start // HS
        state = head_forward(held, gains, rows, lanes)
        probs_ref[place, :, :] = state[0]
        turned_ref[place, :, :] = state[1].T
        for t in range(3):
            halves_ref[t, rows, lanes] = state[2 + t]
        for t in range(2):
            units_ref[t, rows, lanes] = state[5 + 2 * t]
            inverse_ref[t, rows, head : head + 1] = state[6 + 2 * t]


def attend_back_kernel(local_count, depth, width, broadcast, *refs):
    probs_ref, turned_ref, halves_ref, units_ref, inverse_ref = refs[:5]
    grads = refs[5 : 6 if broadcast else 5 + depth]
    gain_ref, out_ref, held, *grad_held = refs[5 + len(grads) :]
    pieces = piece_rows(local_count, depth, width)
    if not broadcast:
        to_section_order(grads, grad_held[0], pieces)
    gains = gain_ref[...]
    for place, (image, rows, lanes) in enumerate(each_head(held)):
        head = lanes.start // HS
        if broadcast:
            row = grads[0][image : image + 1, lanes].astype(BF16).astype(F32)
            grad_mixed = jnp.broadcast_to(row, (PATCHES, HS)).astype(BF16)
        else:
            grad_mixed = grad_held[0][rows, lanes].astype(BF16)
        probs = probs_ref[place]
        grad_probs = dot_nt(grad_mixed, halves_ref[2, rows, lanes])
        weighted = probs * grad_probs
        grad_scores = weighted - probs * jnp.sum(weighted, axis=-1, keepdims=True)
        score_half = (grad_scores * (1.0 / math.sqrt(HS))).astype(BF16)
        grads_out = (
            dot(score_half, halves_ref[1, rows, lanes]),
            dot_tn(score_half, halves_ref[0, rows, lanes]),
        )
        for t in range(2):
            held[t, rows, lanes] = norm_back(
                grads_out[t],
                units_ref[t, rows, lanes],
                inverse_ref[t, rows, head : head + 1],
                gains[t : t + 1, :],
            )
        held[2, rows, lanes] = dot(turned_ref[place], grad_mixed)
    to_ring_order(held, out_ref, pieces)


def project_kernel(*refs):
    weights_ref, projected_ref = refs[-2:]
    rows = jnp.concatenate([ref[...] for ref in refs[:-2]], axis=0)
    for t in range(weights_ref.shape[0]):
        projected_ref[t, :, :] = dot(rows, weights_ref[t])


def cotangent_kernel(*refs):
    weights_ref, out_ref = refs[-2:]
    rows = jnp.concatenate([ref[...] for ref in refs[:-2]], axis=0)
    out_ref[...] = dot_nt(rows, weights_ref[...])


def to_pieces(total, outs):
    count = outs[0].shape[0]
    for i, out in enumerate(outs):
        out[...] = total[i * count : (i + 1) * count].astype(BF16)


def branch_kernel(first, count, attention_ref, weights_ref, *outs):
    to_pieces(dot(attention_ref[first : first + count, :], weights_ref[...]), outs)


def input_kernel(first, count, gradient_ref, weights_ref, *outs):
    rows = slice(first, first + count)
    total = dot_nt(gradient_ref[0, rows, :], weights_ref[0])
    for t in range(1, weights_ref.shape[0]):
        total = total + dot_nt(gradient_ref[t, rows, :], weights_ref[t])
    to_pieces(total, outs)


def weight_gradient_kernel(count, first, *refs):
    pieces, gradient_ref, added, out_ref = refs[:count], refs[count], refs[count + 1 : -1], refs[-1]
    rows = jnp.concatenate([ref[...] for ref in pieces], axis=0)
    for t in range(out_ref.shape[0]):
        total = dot_tn(rows, gradient_ref[first + t])
        if added:
            total = total + added[t][0].astype(F32)
        out_ref[t, :, :] = total.astype(BF16)


def out_gradient_kernel(*refs):
    attention_ref, sums_ref, grad_image_ref, out_ref = refs[-4:]
    cotangent = jnp.concatenate([ref[...] for ref in refs[:-4]], axis=0)
    total = dot_tn(attention_ref[...], cotangent)
    sums = sums_ref[...]
    image_count, lane_count = sums.shape
    sums = jnp.concatenate([sums, jnp.zeros((-image_count % 8, lane_count), F32)], axis=0).T
    grad_image = grad_image_ref[...].astype(BF16).astype(F32)
    for image in range(image_count):
        total = total + sums[:, image : image + 1] * grad_image[image : image + 1, :]
    out_ref[...] = total.astype(BF16)


def head_gradient_kernel(width, pooled_half_ref, grad_logits_ref, out_ref):
    member = lax.axis_index("dp") * width + lax.axis_index("tensor")
    count = out_ref.shape[0]
    start = pl.multiple_of(member * count, HS)
    pooled = pooled_half_ref[:, pl.ds(start, count)].astype(F32)
    grad_logits = grad_logits_ref[...].astype(F32)

    def padded(rows):
        empty = jnp.zeros((-rows.shape[0] % 16, rows.shape[1]), F32)
        return jnp.concatenate([rows, empty], axis=0).astype(BF16)

    out_ref[...] = dot_tn(padded(pooled), padded(grad_logits)).astype(BF16)


def join_kernel(*refs):
    refs[-1][...] = jnp.concatenate([ref[...] for ref in refs[:-1]], axis=0)


def norm_rows_kernel(rows_ref, gain_ref, out_ref):
    unit_rows, _ = norm_parts(rows_ref[...].astype(F32))
    out_ref[...] = (unit_rows * gain_ref[...]).astype(BF16)


def norm_margin_kernel(first_ref, rows_ref, received_ref, gain_ref, out_ref, margin_ref):
    first = first_ref[0] == 1

    @pl.when(first)
    def _():
        margin_ref[...] = rows_ref[...]

    @pl.when(jnp.logical_not(first))
    def _():
        margin_ref[...] = received_ref[...]

    norm_rows_kernel(margin_ref, gain_ref, out_ref)


def judge_kernel(
    patch_count,
    pooled_ref,
    gain_ref,
    head_ref,
    label_ref,
    out_weight_ref,
    loss_ref,
    pooled_half_ref,
    grad_logits_ref,
    grad_image_ref,
    per_image_ref,
):
    image_count = pooled_ref.shape[0]
    unit_rows, inverse = norm_parts(pooled_ref[...] * (1.0 / patch_count))
    gain_row = gain_ref[...]
    pooled_half = (unit_rows * gain_row).astype(BF16)
    pooled_half_ref[...] = pooled_half
    head = head_ref[...]
    logits = dot(pooled_half, head)
    classes = lax.broadcasted_iota(jnp.int32, logits.shape, 1)
    images = lax.broadcasted_iota(jnp.int32, logits.shape, 0)
    label = jnp.zeros_like(classes)
    for image in range(image_count):
        label = jnp.where(images == image, label_ref[image], label)
    targets = (classes == label).astype(F32)
    softplus = jnp.maximum(logits, 0.0) + jnp.log1p(jnp.exp(-jnp.abs(logits)))
    loss_ref[...] = jnp.mean(softplus - targets * logits, axis=-1, keepdims=True)
    sigmoid = 1.0 / (1.0 + jnp.exp(-logits))
    grad_logits = ((sigmoid - targets) * (1.0 / image_count)).astype(BF16)
    grad_logits_ref[...] = grad_logits
    grad_pooled = norm_back(dot_nt(grad_logits, head), unit_rows, inverse, gain_row)
    grad_image = grad_pooled * (1.0 / patch_count)
    grad_image_ref[...] = grad_image
    per_image_ref[...] = dot_nt(grad_image.astype(BF16), out_weight_ref[...])


def grad_rows_kernel(grad_ref, rows_ref, select_ref, grad_image_ref, gain_ref, out_ref):
    unit_rows, inverse = norm_parts(rows_ref[...].astype(F32))
    total = norm_back(grad_ref[...], unit_rows, inverse, gain_ref[...])
    select = select_ref[...]
    for image in range(grad_image_ref.shape[0]):
        total = total + select[:, image : image + 1] * grad_image_ref[image : image + 1, :]
    out_ref[...] = total.astype(BF16)


def on_device(
    block_inputs, qkv_weights, out_weights, norm_gain, query_key_gain, pool_gain, class_head, labels
):
    rows_in = block_inputs[0]
    qkv_local = qkv_weights[0]
    out_local = out_weights[0]
    gain_pair = query_key_gain[0]
    label_row = labels[0]
    local_count, model_width = rows_in.shape
    image_count = label_row.shape[0]
    class_count = class_head.shape[2]
    depth, width = lax.axis_size("dp"), lax.axis_size("tensor")
    group_size = depth * width
    row_count = local_count * group_size
    lane_count = qkv_local.shape[2]
    half = local_count // HALVES
    place = (local_count, depth, width)
    member = lax.axis_index(GROUP)
    image_ids = (member * local_count + lax.iota(jnp.int32, local_count)) // PATCHES
    own_select = (image_ids[:, None] == lax.iota(jnp.int32, image_count)[None, :]).astype(F32)

    def shape(dims, dtype=F32):
        return jax.ShapeDtypeStruct(dims, dtype)

    half_shape = shape((half, model_width), BF16)
    three = (3, row_count, lane_count)
    slab_rows = local_count * width
    heads = image_count * (lane_count // HS)
    product_flops = 2 * row_count * lane_count * PATCHES
    slab_flops = 2 * slab_rows * model_width * lane_count
    chunk = 2 * PATCHES if model_width % (2 * PATCHES) == 0 else PATCHES
    piece_shapes = [half_shape] * (width * HALVES)

    def halves_of(rows):
        return [rows[h * half : (h + 1) * half] for h in range(HALVES)]

    def project(_, pieces):
        return call(
            project_kernel,
            shape((3, slab_rows, lane_count)),
            (*pieces, qkv_local),
            flops=3 * slab_flops,
            limit=16,
        )

    def state_of(projected):
        return call(
            functools.partial(state_kernel, *place),
            [
                shape((heads, PATCHES, PATCHES)),
                shape((heads, PATCHES, PATCHES), BF16),
                shape(three, BF16),
                shape((2, row_count, lane_count)),
                shape((2, row_count, lane_count // HS)),
            ],
            (*projected, gain_pair),
            scratch=[pltpu.VMEM(three, F32)],
            flops=2 * product_flops,
        )

    def weight_gradient(slabs, gradient, first, count, *added):
        pieces = [piece for slab in slabs for piece in slab]
        return pl.pallas_call(
            functools.partial(weight_gradient_kernel, len(pieces), first),
            grid=(model_width // chunk,),
            out_shape=shape((count, model_width, lane_count), BF16),
            in_specs=[pl.BlockSpec((half, chunk), lambda i: (0, i))] * len(pieces)
            + [pl.BlockSpec(three, lambda i: (0, 0, 0))]
            + [pl.BlockSpec((1, chunk, lane_count), lambda i: (0, i, 0))] * len(added),
            out_specs=pl.BlockSpec((count, chunk, lane_count), lambda i: (0, i, 0)),
            compiler_params=pltpu.CompilerParams(vmem_limit_bytes=20 * 2**20),
            cost_estimate=pl.CostEstimate(
                flops=count * depth * slab_flops,
                bytes_accessed=4 * count * model_width * lane_count,
                transcendentals=0,
            ),
        )(*pieces, gradient, *added)

    own_slabs, own_projected = gather_slabs(
        [
            call(norm_rows_kernel, half_shape, (rows, norm_gain), limit=4)
            for rows in halves_of(rows_in)
        ],
        project,
    )
    attention = call(
        functools.partial(attend_own_kernel, *place),
        shape((row_count, lane_count), BF16),
        (*own_projected, gain_pair),
        scratch=[pltpu.VMEM(three, F32), pltpu.VMEM(three[1:], BF16)],
        flops=2 * product_flops,
    )

    def branch(s):
        return call(
            functools.partial(branch_kernel, s * slab_rows, slab_rows),
            piece_shapes,
            (attention, out_local),
            flops=slab_flops,
            limit=16,
        )

    out_halves = [
        (rows.astype(F32) + total).astype(BF16)
        for rows, total in zip(halves_of(rows_in), scatter_slabs(branch))
    ]

    first = (lax.axis_index("section") == 0).astype(jnp.int32).reshape(1)
    margin_normed, margin_halves = zip(
        *[
            call(
                norm_margin_kernel,
                [half_shape] * 2,
                (first, rows, from_behind(out, "section", 1), norm_gain),
                specs=[SMEM_SPEC] + [VMEM_SPEC] * 3,
                limit=4,
            )
            for rows, out in zip(halves_of(rows_in), out_halves)
        ]
    )
    margin_slabs, margin_projected = gather_slabs(margin_normed, project)
    image_sums, pooled_part = call(
        functools.partial(attend_margin_kernel, *place),
        [shape((image_count, lane_count)), shape((image_count, model_width))],
        (*margin_projected, gain_pair, out_local, own_select, *margin_halves),
        scratch=[pltpu.VMEM(three, F32)],
        flops=2 * product_flops,
    )
    own_state = state_of(own_projected)
    margin_state = state_of(margin_projected)
    pooled = after(sum_group(pooled_part), own_state[4], margin_state[4])
    losses, pooled_half, grad_logits, grad_image, per_image = call(
        functools.partial(judge_kernel, PATCHES),
        [
            shape((image_count, 1)),
            shape((image_count, model_width), BF16),
            shape((image_count, class_count), BF16),
            shape((image_count, model_width)),
            shape((image_count, lane_count)),
        ],
        (pooled, pool_gain, class_head[0], label_row, out_local),
        specs=[VMEM_SPEC] * 3 + [SMEM_SPEC, VMEM_SPEC],
        flops=4 * class_count * model_width * 8,
        limit=16,
    )
    grad_head = call(
        functools.partial(head_gradient_kernel, width),
        shape((model_width // group_size, class_count), BF16),
        (pooled_half, grad_logits),
        limit=4,
    )

    margin_gradient = call(
        functools.partial(attend_back_kernel, *place, True),
        shape(three, BF16),
        (*margin_state, per_image, gain_pair),
        scratch=[pltpu.VMEM(three, F32)],
        flops=5 * product_flops,
    )

    def input_term(s):
        return call(
            functools.partial(input_kernel, s * slab_rows, slab_rows),
            piece_shapes,
            (margin_gradient, qkv_local),
            flops=3 * slab_flops,
            limit=16,
        )

    grad_normed = scatter_slabs(input_term)
    grad_inputs = [
        call(grad_rows_kernel, half_shape, (grad, rows, select, grad_image, norm_gain), limit=6)
        for grad, rows, select in zip(grad_normed, margin_halves, halves_of(own_select))
    ]
    margin_parts = [weight_gradient(margin_slabs, margin_gradient, t, 1) for t in range(3)]

    returned = [from_behind(grad, "section", -1) for grad in grad_inputs]

    def cotangent(s, pieces):
        if s < len(margin_parts):
            pieces = [after(pieces[0], margin_parts[s])] + pieces[1:]
        return call(
            cotangent_kernel,
            shape((slab_rows, lane_count)),
            (*pieces, out_local),
            flops=slab_flops,
            limit=16,
        )

    cotangent_slabs, grad_attention = gather_slabs(returned, cotangent)
    own_gradient = call(
        functools.partial(attend_back_kernel, *place, False),
        shape(three, BF16),
        (*own_state, *grad_attention, gain_pair),
        scratch=[pltpu.VMEM(three, F32), pltpu.VMEM(three[1:], F32)],
        flops=5 * product_flops,
    )
    query_key_value_gradient = weight_gradient(own_slabs, own_gradient, 0, 3, *margin_parts)
    pieces = [piece for slab in cotangent_slabs for piece in slab]
    wide = 2 * chunk if model_width % (2 * chunk) == 0 else chunk
    grad_out = pl.pallas_call(
        out_gradient_kernel,
        grid=(model_width // wide,),
        out_shape=shape((lane_count, model_width), BF16),
        in_specs=[pl.BlockSpec((half, wide), lambda i: (0, i))] * len(pieces)
        + [
            pl.BlockSpec((row_count, lane_count), lambda i: (0, 0)),
            pl.BlockSpec((image_count, lane_count), lambda i: (0, 0)),
            pl.BlockSpec((image_count, wide), lambda i: (0, i)),
        ],
        out_specs=pl.BlockSpec((lane_count, wide), lambda i: (0, i)),
        compiler_params=pltpu.CompilerParams(vmem_limit_bytes=20 * 2**20),
        cost_estimate=pl.CostEstimate(
            flops=depth * slab_flops,
            bytes_accessed=4 * model_width * lane_count,
            transcendentals=0,
        ),
    )(*pieces, attention, image_sums, grad_image)
    out_own = call(join_kernel, shape((local_count, model_width), BF16), tuple(out_halves), limit=4)
    return (
        out_own[None],
        query_key_value_gradient[None],
        grad_out[None],
        grad_head[None],
        losses.reshape(1, image_count),
    )


def solution(mesh):
    in_specs = (
        P("section", GROUP, None),
        P("section", None, None, GROUP),
        P("section", GROUP, None),
        P("section", None),
        P("section", None, None),
        P("section", None),
        P("section", None, None),
        P("section", None),
    )
    out_specs = (
        P("section", GROUP, None),
        P("section", None, None, GROUP),
        P("section", GROUP, None),
        P("section", GROUP, None),
        P("section", None),
    )
    return jax.shard_map(
        on_device, mesh=mesh, in_specs=in_specs, out_specs=out_specs, check_vma=False
    )
```

```python
import functools
import math

import jax
import jax.numpy as jnp
from jax import lax
from jax.experimental import pallas as pl
from jax.experimental.pallas import tpu as pltpu
from jax.sharding import PartitionSpec as P

HS = 128
PATCHES = 256
GROUP = ("dp", "tensor")
HALVES = 2

epsilon = 1e-06
F32 = jnp.float32
BF16 = jnp.bfloat16
VMEM_SPEC = pl.BlockSpec(memory_space=pltpu.VMEM)
HBM_SPEC = pl.BlockSpec(memory_space=pltpu.HBM)
SMEM_SPEC = pl.BlockSpec(memory_space=pltpu.SMEM)


def from_behind(block, axis, distance):
    devices = range(lax.axis_size(axis))
    route = [(i - distance, i) for i in devices if i - distance in devices]
    return lax.ppermute(block, axis, route)


def shift(block, axis, distance):
    count = lax.axis_size(axis)
    return lax.ppermute(block, axis, [(i, (i + distance) % count) for i in range(count)])


def after(value, *others):
    return lax.optimization_barrier((value,) + others)[0]


def way(half):
    return 1 if half % 2 == 0 else -1


def gather_slabs(halves, work):
    depth, width = lax.axis_size("dp"), lax.axis_size("tensor")
    ring, slabs, results = [list(halves)], [], []
    across = [[None] * HALVES for _ in range(width)]
    for s in range(depth):
        if s:
            ring.append([shift(ring[-1][h], "dp", way(h)) for h in range(HALVES)])
        pieces = list(ring[s])
        for j in range(1, width):
            for h in range(HALVES):
                piece = ring[s][h]
                if s:
                    piece = after(piece, across[j][h], *results[: s - 1][-1:])
                across[j][h] = shift(piece, "tensor", j)
                pieces.append(across[j][h])
        slabs.append(pieces)
        results.append(work(s, pieces))
    return slabs, results


def scatter_slabs(slab_pieces):
    depth, width = lax.axis_size("dp"), lax.axis_size("tensor")
    running = [None] * HALVES
    last = [[None] * HALVES for _ in range(width)]
    for s in list(range(1, depth)) + [0]:
        terms = slab_pieces(s)
        for h in range(HALVES):
            parts = [terms[h]]
            for j in range(1, width):
                piece = terms[j * HALVES + h]
                if last[j][h] is not None:
                    piece = after(piece, last[j][h])
                last[j][h] = shift(piece, "tensor", -j)
                parts.append(last[j][h])
            if running[h] is not None:
                parts.append(shift(running[h], "dp", way(h)))
            running[h] = parts if s == 0 else sum(part.astype(F32) for part in parts).astype(BF16)
    return running


def exchange(value, axis, steps):
    route = [(i, i ^ steps) for i in range(lax.axis_size(axis))]
    return lax.ppermute(value, axis, route)


def sum_group(value):
    counts = [lax.axis_size(axis) for axis in ("tensor", "dp")]
    if any(count & (count - 1) for count in counts):
        return lax.psum(value, GROUP)
    for axis, count in zip(("tensor", "dp"), counts):
        parts = [value] + [exchange(value, axis, step) for step in range(1, count)]
        while len(parts) > 1:
            parts = [parts[i] + parts[i + 1] for i in range(0, len(parts), 2)]
        value = parts[0]
    return value


def norm_parts(values):
    centered = values - jnp.mean(values, axis=-1, keepdims=True)
    inverse = lax.rsqrt(jnp.mean(centered * centered, axis=-1, keepdims=True) + epsilon)
    return centered * inverse, inverse


def norm_back(grad_normed, unit_rows, inverse, gain_row):
    scaled = grad_normed * gain_row
    return inverse * (
        scaled
        - jnp.mean(scaled, axis=-1, keepdims=True)
        - unit_rows * jnp.mean(scaled * unit_rows, axis=-1, keepdims=True)
    )


def dot_nt(left, right):
    return lax.dot_general(left, right, (((1,), (1,)), ((), ())), preferred_element_type=F32)


def dot_tn(left, right):
    return lax.dot_general(left, right, (((0,), (0,)), ((), ())), preferred_element_type=F32)


def dot(left, right):
    return jnp.dot(left, right, preferred_element_type=F32)


def call(
    kernel, out_shape, ins, specs=None, outs=None, scratch=(), flops=0, moved=1000000, limit=16
):
    many = isinstance(out_shape, (tuple, list))
    return pl.pallas_call(
        kernel,
        out_shape=out_shape,
        in_specs=specs or [VMEM_SPEC] * len(ins),
        out_specs=outs or ([VMEM_SPEC] * len(out_shape) if many else VMEM_SPEC),
        scratch_shapes=list(scratch),
        compiler_params=pltpu.CompilerParams(vmem_limit_bytes=limit * 2**20),
        cost_estimate=pl.CostEstimate(flops=flops, bytes_accessed=moved, transcendentals=0),
    )(*ins)


def piece_rows(local_count, depth, width):
    half = local_count // HALVES
    z, y = lax.axis_index("dp"), lax.axis_index("tensor")
    out = []
    for s in range(depth):
        for j in range(width):
            for h in range(HALVES):
                far_z = lax.rem(z + (depth - s if way(h) > 0 else s), depth)
                far_y = lax.rem(y + width - j, width)
                first = (far_z * width + far_y) * local_count + h * half
                out.append(
                    (((s * width + j) * HALVES + h) * half, pl.multiple_of(first, half), half)
                )
    return out


def to_section_order(slabs, held, pieces):
    rows = held.shape[-2] // len(slabs)
    for ring, first, count in pieces:
        s, r = divmod(ring, rows)
        if len(held.shape) == 3:
            held[:, pl.ds(first, count), :] = slabs[s][:, r : r + count, :].astype(held.dtype)
        else:
            held[pl.ds(first, count), :] = slabs[s][r : r + count, :].astype(held.dtype)


def to_ring_order(held, out, pieces):
    for ring, first, count in pieces:
        if len(held.shape) == 3:
            out[:, ring : ring + count, :] = held[:, pl.ds(first, count), :].astype(out.dtype)
        else:
            out[ring : ring + count, :] = held[pl.ds(first, count), :].astype(out.dtype)


def to_joined_order(held, out, pieces):
    lane_count = held.shape[2]
    for ring, first, count in pieces:
        for t in range(held.shape[0]):
            part = held[t, pl.ds(first, count), :].astype(out.dtype)
            out[ring : ring + count, t * lane_count : (t + 1) * lane_count] = part


def head_forward(held, gains, rows, lanes):
    query_unit, query_inverse = norm_parts(held[0, rows, lanes])
    key_unit, key_inverse = norm_parts(held[1, rows, lanes])
    query_half = (query_unit * gains[0:1, :]).astype(BF16)
    key_half = (key_unit * gains[1:2, :]).astype(BF16)
    value_half = held[2, rows, lanes].astype(BF16)
    exponent = jnp.exp(dot_nt(query_half, key_half) * (1.0 / math.sqrt(HS)))
    probs = exponent * (1.0 / jnp.sum(exponent, axis=-1, keepdims=True))
    return (
        probs,
        probs.astype(BF16),
        query_half,
        key_half,
        value_half,
        query_unit,
        query_inverse,
        key_unit,
        key_inverse,
    )


def each_head(held):
    row_count, lane_count = held.shape[-2:]
    for image in range(row_count // PATCHES):
        for head in range(lane_count // HS):
            yield (
                image,
                slice(image * PATCHES, (image + 1) * PATCHES),
                slice(head * HS, (head + 1) * HS),
            )


def attend_own_kernel(local_count, depth, width, *refs):
    slabs, gain_ref, out_ref, held, mixed = refs[:depth], *refs[depth:]
    pieces = piece_rows(local_count, depth, width)
    to_section_order(slabs, held, pieces)
    gains = gain_ref[...]
    for _, rows, lanes in each_head(held):
        state = head_forward(held, gains, rows, lanes)
        mixed[rows, lanes] = dot(state[1], state[4]).astype(BF16)
    to_ring_order(mixed, out_ref, pieces)


def attend_margin_kernel(local_count, depth, width, *refs):
    slabs = refs[:depth]
    gain_ref, out_weight_ref = refs[depth : depth + 2]
    row_sums = refs[depth + 2 : depth + 2 + HALVES]
    sums_ref, pooled_ref, held = refs[depth + 2 + HALVES :]
    pieces = piece_rows(local_count, depth, width)
    to_section_order(slabs, held, pieces)
    gains = gain_ref[...]
    for image, rows, lanes in each_head(held):
        state = head_forward(held, gains, rows, lanes)
        mixed = dot(state[1], state[4]).astype(BF16)
        sums_ref[image : image + 1, lanes] = jnp.sum(mixed.astype(F32), axis=0, keepdims=True)
    sums = sums_ref[...]
    high = sums.astype(BF16)
    rest = sums - high.astype(F32)
    middle = rest.astype(BF16)
    low = (rest - middle.astype(F32)).astype(BF16)
    weights = out_weight_ref[...]
    pooled_ref[...] = sum(ref[...] for ref in row_sums) + (
        dot(high, weights) + (dot(middle, weights) + dot(low, weights))
    )


def state_kernel(local_count, depth, width, *refs):
    slabs = refs[:depth]
    gain_ref, probs_ref, turned_ref, halves_ref, units_ref, inverse_ref, held = refs[depth:]
    to_section_order(slabs, held, piece_rows(local_count, depth, width))
    gains = gain_ref[...]
    for place, (_, rows, lanes) in enumerate(each_head(held)):
        head = lanes.start // HS
        state = head_forward(held, gains, rows, lanes)
        probs_ref[place, :, :] = state[0]
        turned_ref[place, :, :] = state[1].T
        for t in range(3):
            halves_ref[t, rows, lanes] = state[2 + t]
        for t in range(2):
            units_ref[t, rows, lanes] = state[5 + 2 * t]
            inverse_ref[t, rows, head : head + 1] = state[6 + 2 * t]


def attend_back_kernel(local_count, depth, width, broadcast, *refs):
    probs_ref, turned_ref, halves_ref, units_ref, inverse_ref = refs[:5]
    grads = refs[5 : 6 if broadcast else 5 + depth]
    gain_ref, out_ref, held, *grad_held = refs[5 + len(grads) :]
    pieces = piece_rows(local_count, depth, width)
    if not broadcast:
        to_section_order(grads, grad_held[0], pieces)
    gains = gain_ref[...]
    for place, (image, rows, lanes) in enumerate(each_head(held)):
        head = lanes.start // HS
        if broadcast:
            row = grads[0][image : image + 1, lanes].astype(BF16).astype(F32)
            grad_mixed = jnp.broadcast_to(row, (PATCHES, HS)).astype(BF16)
        else:
            grad_mixed = grad_held[0][rows, lanes].astype(BF16)
        probs = probs_ref[place]
        grad_probs = dot_nt(grad_mixed, halves_ref[2, rows, lanes])
        weighted = probs * grad_probs
        grad_scores = weighted - probs * jnp.sum(weighted, axis=-1, keepdims=True)
        score_half = (grad_scores * (1.0 / math.sqrt(HS))).astype(BF16)
        grads_out = (
            dot(score_half, halves_ref[1, rows, lanes]),
            dot_tn(score_half, halves_ref[0, rows, lanes]),
        )
        for t in range(2):
            held[t, rows, lanes] = norm_back(
                grads_out[t],
                units_ref[t, rows, lanes],
                inverse_ref[t, rows, head : head + 1],
                gains[t : t + 1, :],
            )
        held[2, rows, lanes] = dot(turned_ref[place], grad_mixed)
    to_joined_order(held, out_ref, pieces)


def project_kernel(*refs):
    *pieces, weights_ref, projected_ref = refs
    rows = jnp.concatenate([ref[...] for ref in pieces], axis=0)
    for t in range(weights_ref.shape[0]):
        projected_ref[t, :, :] = dot(rows, weights_ref[t])


def cotangent_kernel(*refs):
    *pieces, weights_ref, out_ref = refs
    rows = jnp.concatenate([ref[...] for ref in pieces], axis=0)
    out_ref[...] = dot_nt(rows, weights_ref[...])


def to_pieces(total, outs):
    count = outs[0].shape[0]
    for i, out in enumerate(outs):
        out[...] = total[i * count : (i + 1) * count].astype(BF16)


def branch_kernel(first, count, attention_ref, weights_ref, *outs):
    to_pieces(dot(attention_ref[first : first + count, :], weights_ref[...]), outs)


def input_kernel(first, count, gradient_ref, weights_ref, *outs):
    projections, _, lane_count = weights_ref.shape
    total = None
    for t in range(projections):
        part = gradient_ref[first : first + count, t * lane_count : (t + 1) * lane_count]
        part = dot_nt(part, weights_ref[t])
        total = part if total is None else total + part
    to_pieces(total, outs)


def weight_gradient_kernel(counts, chunk, *refs):
    pieces, grads = refs[: sum(counts)], refs[sum(counts) : -2]
    out_ref, joined = refs[-2:]
    projections, model_width, lane_count = out_ref.shape
    first = 0
    for grad in grads:
        joined[first : first + grad.shape[0], :] = grad[...]
        first += grad.shape[0]

    def step(*blocks):
        rows = jnp.concatenate([block[...] for block in blocks[:-1]], axis=0)
        total = dot_tn(rows, joined[...]).astype(BF16)
        for t in range(projections):
            blocks[-1][t, :, :] = total[:, t * lane_count : (t + 1) * lane_count]

    pltpu.emit_pipeline(
        step,
        grid=(model_width // chunk,),
        in_specs=[pl.BlockSpec((p.shape[0], chunk), lambda i: (0, i)) for p in pieces],
        out_specs=[pl.BlockSpec((projections, chunk, lane_count), lambda i: (0, i, 0))],
    )(*pieces, out_ref)


def out_gradient_kernel(chunk, *refs):
    *pieces, attention_ref, sums_ref, grad_image_ref, out_ref = refs
    sums = sums_ref[...]
    image_count, lane_count = sums.shape
    sums = jnp.concatenate([sums, jnp.zeros((-image_count % 8, lane_count), F32)], axis=0).T

    def step(*blocks):
        cotangent = jnp.concatenate([block[...] for block in blocks[:-2]], axis=0)
        total = dot_tn(attention_ref[...], cotangent)
        grad_image = blocks[-2][...].astype(BF16).astype(F32)
        for image in range(image_count):
            total = total + sums[:, image : image + 1] * grad_image[image : image + 1, :]
        blocks[-1][...] = total.astype(BF16)

    pltpu.emit_pipeline(
        step,
        grid=(out_ref.shape[1] // chunk,),
        in_specs=[pl.BlockSpec((p.shape[0], chunk), lambda i: (0, i)) for p in pieces]
        + [pl.BlockSpec((image_count, chunk), lambda i: (0, i))],
        out_specs=[pl.BlockSpec((lane_count, chunk), lambda i: (0, i))],
    )(*pieces, grad_image_ref, out_ref)


def head_gradient_kernel(width, pooled_half_ref, grad_logits_ref, out_ref):
    member = lax.axis_index("dp") * width + lax.axis_index("tensor")
    count = out_ref.shape[0]
    start = pl.multiple_of(member * count, HS)
    pooled = pooled_half_ref[:, pl.ds(start, count)].astype(F32)
    grad_logits = grad_logits_ref[...].astype(F32)

    def padded(rows):
        empty = jnp.zeros((-rows.shape[0] % 16, rows.shape[1]), F32)
        return jnp.concatenate([rows, empty], axis=0).astype(BF16)

    out_ref[...] = dot_tn(padded(pooled), padded(grad_logits)).astype(BF16)


def join_kernel(*refs):
    refs[-1][...] = jnp.concatenate([ref[...] for ref in refs[:-1]], axis=0)


def norm_rows_kernel(first, rows_ref, gain_ref, out_ref):
    rows = rows_ref[first : first + out_ref.shape[0], :].astype(F32)
    unit_rows, _ = norm_parts(rows)
    out_ref[...] = (unit_rows * gain_ref[...]).astype(BF16)


def norm_margin_kernel(
    first, flag_ref, rows_ref, received_ref, select_ref, gain_ref, out_ref, margin_ref, sums_ref
):
    own = rows_ref[first : first + out_ref.shape[0], :]
    margin = jnp.where(flag_ref[0] == 1, own.astype(F32), received_ref[...].astype(F32))
    margin_ref[...] = margin.astype(BF16)
    unit_rows, _ = norm_parts(margin)
    out_ref[...] = (unit_rows * gain_ref[...]).astype(BF16)
    select = select_ref[...]
    for image in range(select.shape[1]):
        sums_ref[image : image + 1, :] = jnp.sum(
            margin * select[:, image : image + 1], axis=0, keepdims=True
        )


def out_rows_kernel(first, rows_ref, *refs):
    *terms, out_ref = refs
    total = sum(term[...].astype(F32) for term in terms)
    rows = rows_ref[first : first + out_ref.shape[0], :].astype(F32)
    out_ref[...] = (rows + total).astype(BF16)


def judge_kernel(
    patch_count,
    pooled_ref,
    gain_ref,
    head_ref,
    label_ref,
    out_weight_ref,
    loss_ref,
    pooled_half_ref,
    grad_logits_ref,
    grad_image_ref,
    per_image_ref,
):
    image_count = pooled_ref.shape[0]
    unit_rows, inverse = norm_parts(pooled_ref[...] * (1.0 / patch_count))
    gain_row = gain_ref[...]
    pooled_half = (unit_rows * gain_row).astype(BF16)
    pooled_half_ref[...] = pooled_half
    head = head_ref[...]
    logits = dot(pooled_half, head)
    classes = lax.broadcasted_iota(jnp.int32, logits.shape, 1)
    images = lax.broadcasted_iota(jnp.int32, logits.shape, 0)
    label = jnp.zeros_like(classes)
    for image in range(image_count):
        label = jnp.where(images == image, label_ref[image], label)
    targets = (classes == label).astype(F32)
    softplus = jnp.maximum(logits, 0.0) + jnp.log1p(jnp.exp(-jnp.abs(logits)))
    loss_ref[...] = jnp.mean(softplus - targets * logits, axis=-1, keepdims=True)
    sigmoid = 1.0 / (1.0 + jnp.exp(-logits))
    grad_logits = ((sigmoid - targets) * (1.0 / image_count)).astype(BF16)
    grad_logits_ref[...] = grad_logits
    grad_pooled = norm_back(dot_nt(grad_logits, head), unit_rows, inverse, gain_row)
    grad_image = grad_pooled * (1.0 / patch_count)
    grad_image_ref[...] = grad_image
    per_image_ref[...] = dot_nt(grad_image.astype(BF16), out_weight_ref[...])


def grad_rows_kernel(rows_ref, select_ref, grad_image_ref, gain_ref, *refs):
    *terms, out_ref = refs
    unit_rows, inverse = norm_parts(rows_ref[...].astype(F32))
    grad = sum(term[...].astype(F32) for term in terms)
    total = norm_back(grad, unit_rows, inverse, gain_ref[...])
    select = select_ref[...]
    for image in range(grad_image_ref.shape[0]):
        total = total + select[:, image : image + 1] * grad_image_ref[image : image + 1, :]
    out_ref[...] = total.astype(BF16)


def on_device(
    block_inputs, qkv_weights, out_weights, norm_gain, query_key_gain, pool_gain, class_head, labels
):
    rows_in = block_inputs[0]
    qkv_local = qkv_weights[0]
    out_local = out_weights[0]
    gain_pair = query_key_gain[0]
    label_row = labels[0]
    local_count, model_width = rows_in.shape
    image_count = label_row.shape[0]
    class_count = class_head.shape[2]
    depth, width = lax.axis_size("dp"), lax.axis_size("tensor")
    group_size = depth * width
    row_count = local_count * group_size
    lane_count = qkv_local.shape[2]
    half = local_count // HALVES
    place = (local_count, depth, width)
    member = lax.axis_index(GROUP)
    image_ids = (member * local_count + lax.iota(jnp.int32, local_count)) // PATCHES
    own_select = (image_ids[:, None] == lax.iota(jnp.int32, image_count)[None, :]).astype(F32)

    def shape(dims, dtype=F32):
        return jax.ShapeDtypeStruct(dims, dtype)

    half_shape = shape((half, model_width), BF16)
    three = (3, row_count, lane_count)
    slab_rows = local_count * width
    heads = image_count * (lane_count // HS)
    product_flops = 2 * row_count * lane_count * PATCHES
    slab_flops = 2 * slab_rows * model_width * lane_count
    chunk = 2 * PATCHES if model_width % (2 * PATCHES) == 0 else PATCHES
    piece_shapes = [half_shape] * (width * HALVES)

    select_halves = [own_select[h * half : (h + 1) * half] for h in range(HALVES)]

    def project(_, pieces):
        return call(
            project_kernel,
            shape((3, slab_rows, lane_count)),
            (*pieces, qkv_local),
            flops=3 * slab_flops,
            limit=12,
        )

    def state_of(projected):
        return call(
            functools.partial(state_kernel, *place),
            [
                shape((heads, PATCHES, PATCHES)),
                shape((heads, PATCHES, PATCHES), BF16),
                shape(three, BF16),
                shape((2, row_count, lane_count)),
                shape((2, row_count, lane_count // HS)),
            ],
            (*projected, gain_pair),
            scratch=[pltpu.VMEM(three, F32)],
            flops=2 * product_flops,
        )

    own_slabs, own_projected = gather_slabs(
        [
            call(
                functools.partial(norm_rows_kernel, h * half),
                half_shape,
                (rows_in, norm_gain),
                limit=4,
            )
            for h in range(HALVES)
        ],
        project,
    )
    attention = call(
        functools.partial(attend_own_kernel, *place),
        shape((row_count, lane_count), BF16),
        (*own_projected, gain_pair),
        scratch=[pltpu.VMEM(three, F32), pltpu.VMEM(three[1:], BF16)],
        flops=2 * product_flops,
    )

    def branch(s):
        return call(
            functools.partial(branch_kernel, s * slab_rows, slab_rows),
            piece_shapes,
            (attention, out_local),
            flops=slab_flops,
            limit=12,
        )

    out_halves = [
        call(
            functools.partial(out_rows_kernel, h * half),
            half_shape,
            (rows_in, *terms),
            limit=4,
        )
        for h, terms in enumerate(scatter_slabs(branch))
    ]

    first = (lax.axis_index("section") == 0).astype(jnp.int32).reshape(1)
    margin_normed, margin_halves, row_sums = zip(
        *[
            call(
                functools.partial(norm_margin_kernel, h * half),
                [half_shape, half_shape, shape((image_count, model_width))],
                (first, rows_in, from_behind(out, "section", 1), select, norm_gain),
                specs=[SMEM_SPEC] + [VMEM_SPEC] * 4,
                limit=4,
            )
            for h, (out, select) in enumerate(zip(out_halves, select_halves))
        ]
    )
    margin_slabs, margin_projected = gather_slabs(margin_normed, project)
    image_sums, pooled_part = call(
        functools.partial(attend_margin_kernel, *place),
        [shape((image_count, lane_count)), shape((image_count, model_width))],
        (*margin_projected, gain_pair, out_local, *row_sums),
        scratch=[pltpu.VMEM(three, F32)],
        flops=2 * product_flops,
    )
    margin_state = state_of(margin_projected)
    pooled = after(sum_group(pooled_part), margin_state[4])
    losses, pooled_half, grad_logits, grad_image, per_image = call(
        functools.partial(judge_kernel, PATCHES),
        [
            shape((image_count, 1)),
            shape((image_count, model_width), BF16),
            shape((image_count, class_count), BF16),
            shape((image_count, model_width)),
            shape((image_count, lane_count)),
        ],
        (pooled, pool_gain, class_head[0], label_row, out_local),
        specs=[VMEM_SPEC] * 3 + [SMEM_SPEC, VMEM_SPEC],
        flops=4 * class_count * model_width * 8,
        limit=12,
    )
    grad_head = call(
        functools.partial(head_gradient_kernel, width),
        shape((model_width // group_size, class_count), BF16),
        (pooled_half, grad_logits),
        limit=4,
    )

    margin_gradient = call(
        functools.partial(attend_back_kernel, *place, True),
        shape((row_count, 3 * lane_count), BF16),
        (*margin_state, per_image, gain_pair),
        scratch=[pltpu.VMEM(three, F32)],
        flops=5 * product_flops,
    )

    def input_term(s):
        return call(
            functools.partial(input_kernel, s * slab_rows, slab_rows),
            piece_shapes,
            (margin_gradient, qkv_local),
            flops=3 * slab_flops,
            limit=12,
        )

    grad_normed = scatter_slabs(input_term)
    grad_inputs = [
        call(
            grad_rows_kernel,
            half_shape,
            (rows, select, grad_image, norm_gain, *terms),
            limit=6,
        )
        for terms, rows, select in zip(grad_normed, margin_halves, select_halves)
    ]
    returned = [from_behind(grad, "section", -1) for grad in grad_inputs]

    def cotangent(_, pieces):
        return call(
            cotangent_kernel,
            shape((slab_rows, lane_count)),
            (*pieces, out_local),
            flops=slab_flops,
            limit=12,
        )

    cotangent_slabs, grad_attention = gather_slabs(returned, cotangent)
    own_gradient = call(
        functools.partial(attend_back_kernel, *place, False),
        shape((row_count, 3 * lane_count), BF16),
        (*state_of(own_projected), *grad_attention, gain_pair),
        scratch=[pltpu.VMEM(three, F32), pltpu.VMEM(three[1:], F32)],
        flops=5 * product_flops,
    )
    passes = [[p for slab in slabs for p in slab] for slabs in (margin_slabs, own_slabs)]
    counts = [len(pieces) for pieces in passes]
    query_key_value_gradient = call(
        functools.partial(weight_gradient_kernel, counts, chunk),
        shape((3, model_width, lane_count), BF16),
        (*passes[0], *passes[1], margin_gradient, own_gradient),
        specs=[HBM_SPEC] * sum(counts) + [VMEM_SPEC] * 2,
        outs=HBM_SPEC,
        scratch=[pltpu.VMEM((2 * row_count, 3 * lane_count), BF16)],
        flops=6 * depth * slab_flops,
        moved=6 * model_width * lane_count,
        limit=60,
    )
    pieces = [piece for slab in cotangent_slabs for piece in slab]
    wide = 2 * chunk if model_width % (2 * chunk) == 0 else chunk
    grad_out = call(
        functools.partial(out_gradient_kernel, wide),
        shape((lane_count, model_width), BF16),
        (*pieces, attention, image_sums, grad_image),
        specs=[HBM_SPEC] * len(pieces) + [VMEM_SPEC] * 2 + [HBM_SPEC],
        outs=HBM_SPEC,
        flops=depth * slab_flops,
        moved=4 * model_width * lane_count,
        limit=60,
    )
    out_own = call(join_kernel, shape((local_count, model_width), BF16), tuple(out_halves), limit=4)
    return (
        out_own[None],
        query_key_value_gradient[None],
        grad_out[None],
        grad_head[None],
        losses.reshape(1, image_count),
    )


def solution(mesh):
    in_specs = (
        P("section", GROUP, None),
        P("section", None, None, GROUP),
        P("section", GROUP, None),
        P("section", None),
        P("section", None, None),
        P("section", None),
        P("section", None, None),
        P("section", None),
    )
    out_specs = (
        P("section", GROUP, None),
        P("section", None, None, GROUP),
        P("section", GROUP, None),
        P("section", GROUP, None),
        P("section", None),
    )
    return jax.shard_map(
        on_device, mesh=mesh, in_specs=in_specs, out_specs=out_specs, check_vma=False
    )
```

```python
import functools
import math

import jax
import jax.numpy as jnp
from jax import lax
from jax.experimental import pallas as pl
from jax.experimental.pallas import tpu as pltpu
from jax.sharding import PartitionSpec as P

HS = 128
PATCHES = 256
GROUP = ("dp", "tensor")
HALVES = 2
OUT_WAYS = (1, -1)
GRAD_WAYS = (1, -1)

epsilon = 1e-06
F32 = jnp.float32
BF16 = jnp.bfloat16
VMEM_SPEC = pl.BlockSpec(memory_space=pltpu.VMEM)
HBM_SPEC = pl.BlockSpec(memory_space=pltpu.HBM)
SMEM_SPEC = pl.BlockSpec(memory_space=pltpu.SMEM)


def from_behind(block, axis, distance):
    devices = range(lax.axis_size(axis))
    route = [(i - distance, i) for i in devices if i - distance in devices]
    return lax.ppermute(block, axis, route)


def shift(block, axis, distance):
    count = lax.axis_size(axis)
    return lax.ppermute(block, axis, [(i, (i + distance) % count) for i in range(count)])


def after(value, *others):
    return lax.optimization_barrier((value,) + others)[0]


def way(half):
    return 1 if half % 2 == 0 else -1


def gather_slabs(halves, work):
    depth, width = lax.axis_size("dp"), lax.axis_size("tensor")
    ring, slabs, results = [list(halves)], [], []
    across = [[None] * HALVES for _ in range(width)]
    for s in range(depth):
        if s:
            ring.append([shift(ring[-1][h], "dp", way(h)) for h in range(HALVES)])
        pieces = list(ring[s])
        for j in range(1, width):
            for h in range(HALVES):
                piece = ring[s][h]
                if s:
                    piece = after(piece, across[j][h], *[r[0] for r in results[: s - 1][-1:]])
                across[j][h] = shift(piece, "tensor", j)
                pieces.append(across[j][h])
        slabs.append(pieces)
        results.append(work(s, pieces))
    return slabs, results


def scatter_slabs(slab_pieces, ways):
    depth, width = lax.axis_size("dp"), lax.axis_size("tensor")
    running = [None] * HALVES
    last = [[None] * HALVES for _ in range(width)]
    for s in list(range(1, depth)) + [0]:
        terms = slab_pieces(s)
        for h in range(HALVES):
            parts = [terms[h]]
            for j in range(1, width):
                piece = terms[j * HALVES + h]
                if last[j][h] is not None:
                    piece = after(piece, last[j][h])
                last[j][h] = shift(piece, "tensor", -j)
                parts.append(last[j][h])
            if running[h] is not None:
                parts.append(shift(running[h], "dp", ways[h]))
            running[h] = parts if s == 0 else sum(part.astype(F32) for part in parts).astype(BF16)
    return running


def slab_starts(s, half, depth, width, ways):
    starts = []
    for j in range(width):
        for h in range(HALVES):
            slab = s if ways[h] == way(h) else (depth - s) % depth
            starts.append(((slab * width + j) * HALVES + h) * half)
    return tuple(starts)


def exchange(value, axis, steps):
    route = [(i, i ^ steps) for i in range(lax.axis_size(axis))]
    return lax.ppermute(value, axis, route)


def sum_group(value):
    counts = [lax.axis_size(axis) for axis in ("tensor", "dp")]
    if any(count & (count - 1) for count in counts):
        return lax.psum(value, GROUP)
    for axis, count in zip(("tensor", "dp"), counts):
        parts = [value] + [exchange(value, axis, step) for step in range(1, count)]
        while len(parts) > 1:
            parts = [parts[i] + parts[i + 1] for i in range(0, len(parts), 2)]
        value = parts[0]
    return value


def norm_parts(values):
    centered = values - jnp.mean(values, axis=-1, keepdims=True)
    inverse = lax.rsqrt(jnp.mean(centered * centered, axis=-1, keepdims=True) + epsilon)
    return centered * inverse, inverse


def norm_back(grad_normed, unit_rows, inverse, gain_row):
    scaled = grad_normed * gain_row
    return inverse * (
        scaled
        - jnp.mean(scaled, axis=-1, keepdims=True)
        - unit_rows * jnp.mean(scaled * unit_rows, axis=-1, keepdims=True)
    )


def dot_nt(left, right):
    return lax.dot_general(left, right, (((1,), (1,)), ((), ())), preferred_element_type=F32)


def dot_tn(left, right):
    return lax.dot_general(left, right, (((0,), (0,)), ((), ())), preferred_element_type=F32)


def dot(left, right):
    return jnp.dot(left, right, preferred_element_type=F32)


def call(
    kernel, out_shape, ins, specs=None, outs=None, scratch=(), flops=0, moved=1000000, limit=16
):
    many = isinstance(out_shape, (tuple, list))
    return pl.pallas_call(
        kernel,
        out_shape=out_shape,
        in_specs=specs or [VMEM_SPEC] * len(ins),
        out_specs=outs or ([VMEM_SPEC] * len(out_shape) if many else VMEM_SPEC),
        scratch_shapes=list(scratch),
        compiler_params=pltpu.CompilerParams(vmem_limit_bytes=limit * 2**20),
        cost_estimate=pl.CostEstimate(flops=flops, bytes_accessed=moved, transcendentals=0),
    )(*ins)


def piece_rows(local_count, depth, width):
    half = local_count // HALVES
    z, y = lax.axis_index("dp"), lax.axis_index("tensor")
    out = []
    for s in range(depth):
        for j in range(width):
            for h in range(HALVES):
                far_z = lax.rem(z + (depth - s if way(h) > 0 else s), depth)
                far_y = lax.rem(y + width - j, width)
                first = (far_z * width + far_y) * local_count + h * half
                out.append(
                    (((s * width + j) * HALVES + h) * half, pl.multiple_of(first, half), half)
                )
    return out


def to_section_order(slabs, held, pieces):
    rows = held.shape[-2] // len(slabs)
    for ring, first, count in pieces:
        s, r = divmod(ring, rows)
        if len(held.shape) == 3:
            held[:, pl.ds(first, count), :] = slabs[s][:, r : r + count, :].astype(held.dtype)
        else:
            held[pl.ds(first, count), :] = slabs[s][r : r + count, :].astype(held.dtype)


def to_ring_order(held, out, pieces):
    for ring, first, count in pieces:
        if len(held.shape) == 3:
            out[:, ring : ring + count, :] = held[:, pl.ds(first, count), :].astype(out.dtype)
        else:
            out[ring : ring + count, :] = held[pl.ds(first, count), :].astype(out.dtype)


def to_joined_order(held, out, pieces):
    lane_count = held.shape[2]
    for ring, first, count in pieces:
        for t in range(held.shape[0]):
            part = held[t, pl.ds(first, count), :].astype(out.dtype)
            out[ring : ring + count, t * lane_count : (t + 1) * lane_count] = part


def head_forward(held, gains, rows, lanes):
    query_unit, query_inverse = norm_parts(held[0, rows, lanes])
    key_unit, key_inverse = norm_parts(held[1, rows, lanes])
    query_half = (query_unit * gains[0:1, :]).astype(BF16)
    key_half = (key_unit * gains[1:2, :]).astype(BF16)
    value_half = held[2, rows, lanes].astype(BF16)
    exponent = jnp.exp(dot_nt(query_half, key_half) * (1.0 / math.sqrt(HS)))
    probs = exponent * (1.0 / jnp.sum(exponent, axis=-1, keepdims=True))
    return (
        probs,
        probs.astype(BF16),
        query_half,
        key_half,
        value_half,
        query_unit,
        query_inverse,
        key_unit,
        key_inverse,
    )


def each_head(held):
    row_count, lane_count = held.shape[-2:]
    for image in range(row_count // PATCHES):
        for head in range(lane_count // HS):
            yield (
                image,
                slice(image * PATCHES, (image + 1) * PATCHES),
                slice(head * HS, (head + 1) * HS),
            )


def attend_own_kernel(local_count, depth, width, *refs):
    slabs, gain_ref, out_ref, held, mixed = refs[:depth], *refs[depth:]
    pieces = piece_rows(local_count, depth, width)
    to_section_order(slabs, held, pieces)
    gains = gain_ref[...]
    for _, rows, lanes in each_head(held):
        state = head_forward(held, gains, rows, lanes)
        mixed[rows, lanes] = dot(state[1], state[4]).astype(BF16)
    to_ring_order(mixed, out_ref, pieces)


def attend_margin_kernel(local_count, depth, width, *refs):
    slabs = refs[:depth]
    gain_ref, out_weight_ref = refs[depth : depth + 2]
    row_sums = refs[depth + 2 : depth + 2 + HALVES]
    sums_ref, pooled_ref, held = refs[depth + 2 + HALVES :]
    pieces = piece_rows(local_count, depth, width)
    to_section_order(slabs, held, pieces)
    gains = gain_ref[...]
    for image, rows, lanes in each_head(held):
        state = head_forward(held, gains, rows, lanes)
        mixed = dot(state[1], state[4]).astype(BF16)
        sums_ref[image : image + 1, lanes] = jnp.sum(mixed.astype(F32), axis=0, keepdims=True)
    sums = sums_ref[...]
    high = sums.astype(BF16)
    rest = sums - high.astype(F32)
    middle = rest.astype(BF16)
    low = (rest - middle.astype(F32)).astype(BF16)
    weights = out_weight_ref[...]
    pooled_ref[...] = sum(ref[...] for ref in row_sums) + (
        dot(high, weights) + (dot(middle, weights) + dot(low, weights))
    )


def state_kernel(local_count, depth, width, *refs):
    slabs = refs[:depth]
    gain_ref, probs_ref, turned_ref, halves_ref, units_ref, inverse_ref, held = refs[depth:]
    to_section_order(slabs, held, piece_rows(local_count, depth, width))
    gains = gain_ref[...]
    for place, (_, rows, lanes) in enumerate(each_head(held)):
        head = lanes.start // HS
        state = head_forward(held, gains, rows, lanes)
        probs_ref[place, :, :] = state[0]
        turned_ref[place, :, :] = state[1].T
        for t in range(3):
            halves_ref[t, rows, lanes] = state[2 + t]
        for t in range(2):
            units_ref[t, rows, lanes] = state[5 + 2 * t]
            inverse_ref[t, rows, head : head + 1] = state[6 + 2 * t]


def attend_back_kernel(local_count, depth, width, broadcast, *refs):
    probs_ref, turned_ref, halves_ref, units_ref, inverse_ref = refs[:5]
    grads = refs[5 : 6 if broadcast else 5 + depth]
    gain_ref, out_ref, held, *grad_held = refs[5 + len(grads) :]
    pieces = piece_rows(local_count, depth, width)
    if not broadcast:
        to_section_order(grads, grad_held[0], pieces)
    gains = gain_ref[...]
    for place, (image, rows, lanes) in enumerate(each_head(held)):
        head = lanes.start // HS
        if broadcast:
            row = grads[0][image : image + 1, lanes].astype(BF16).astype(F32)
            grad_mixed = jnp.broadcast_to(row, (PATCHES, HS)).astype(BF16)
        else:
            grad_mixed = grad_held[0][rows, lanes].astype(BF16)
        probs = probs_ref[place]
        grad_probs = dot_nt(grad_mixed, halves_ref[2, rows, lanes])
        weighted = probs * grad_probs
        grad_scores = weighted - probs * jnp.sum(weighted, axis=-1, keepdims=True)
        score_half = (grad_scores * (1.0 / math.sqrt(HS))).astype(BF16)
        grads_out = (
            dot(score_half, halves_ref[1, rows, lanes]),
            dot_tn(score_half, halves_ref[0, rows, lanes]),
        )
        for t in range(2):
            held[t, rows, lanes] = norm_back(
                grads_out[t],
                units_ref[t, rows, lanes],
                inverse_ref[t, rows, head : head + 1],
                gains[t : t + 1, :],
            )
        held[2, rows, lanes] = dot(turned_ref[place], grad_mixed)
    to_joined_order(held, out_ref, pieces)


def project_kernel(*refs):
    *pieces, weights_ref, projected_ref, turned_ref = refs
    rows = jnp.concatenate([ref[...] for ref in pieces], axis=0)
    for t in range(weights_ref.shape[0]):
        projected_ref[t, :, :] = dot(rows, weights_ref[t])
    turned_ref[...] = rows.T


def cotangent_kernel(*refs):
    *pieces, weights_ref, out_ref, slab_ref = refs
    rows = jnp.concatenate([ref[...] for ref in pieces], axis=0)
    out_ref[...] = dot_nt(rows, weights_ref[...])
    slab_ref[...] = rows


def to_pieces(total, outs):
    count = outs[0].shape[0]
    for i, out in enumerate(outs):
        out[...] = total[i * count : (i + 1) * count].astype(BF16)


def branch_kernel(starts, attention_ref, weights_ref, *outs):
    half = outs[0].shape[0]
    rows = jnp.concatenate([attention_ref[i : i + half, :] for i in starts], axis=0)
    to_pieces(dot(rows, weights_ref[...]), outs)


def input_kernel(starts, gradient_ref, weights_ref, *outs):
    half = outs[0].shape[0]
    projections, _, lane_count = weights_ref.shape
    total = None
    for t in range(projections):
        lanes = slice(t * lane_count, (t + 1) * lane_count)
        part = jnp.concatenate([gradient_ref[i : i + half, lanes] for i in starts], axis=0)
        part = dot_nt(part, weights_ref[t])
        total = part if total is None else total + part
    to_pieces(total, outs)


def weight_gradient_kernel(slab_count, chunk, *refs):
    slabs, grads = refs[:slab_count], refs[slab_count:-2]
    out_ref, joined = refs[-2:]
    projections, model_width, lane_count = out_ref.shape
    first = 0
    for grad in grads:
        joined[first : first + grad.shape[0], :] = grad[...]
        first += grad.shape[0]

    def step(*blocks):
        turned = jnp.concatenate([block[...] for block in blocks[:-1]], axis=1)
        total = dot(turned, joined[...]).astype(BF16)
        for t in range(projections):
            blocks[-1][t, :, :] = total[:, t * lane_count : (t + 1) * lane_count]

    pltpu.emit_pipeline(
        step,
        grid=(model_width // chunk,),
        in_specs=[pl.BlockSpec((chunk, slab.shape[1]), lambda i: (i, 0)) for slab in slabs],
        out_specs=[pl.BlockSpec((projections, chunk, lane_count), lambda i: (0, i, 0))],
    )(*slabs, out_ref)


def out_gradient_kernel(chunk, *refs):
    *pieces, attention_ref, sums_ref, grad_image_ref, out_ref = refs
    sums = sums_ref[...]
    image_count, lane_count = sums.shape
    sums = jnp.concatenate([sums, jnp.zeros((-image_count % 8, lane_count), F32)], axis=0).T

    def step(*blocks):
        cotangent = jnp.concatenate([block[...] for block in blocks[:-2]], axis=0)
        total = dot_tn(attention_ref[...], cotangent)
        grad_image = blocks[-2][...].astype(BF16).astype(F32)
        for image in range(image_count):
            total = total + sums[:, image : image + 1] * grad_image[image : image + 1, :]
        blocks[-1][...] = total.astype(BF16)

    pltpu.emit_pipeline(
        step,
        grid=(out_ref.shape[1] // chunk,),
        in_specs=[pl.BlockSpec((p.shape[0], chunk), lambda i: (0, i)) for p in pieces]
        + [pl.BlockSpec((image_count, chunk), lambda i: (0, i))],
        out_specs=[pl.BlockSpec((lane_count, chunk), lambda i: (0, i))],
    )(*pieces, grad_image_ref, out_ref)


def head_gradient_kernel(width, pooled_half_ref, grad_logits_ref, out_ref):
    member = lax.axis_index("dp") * width + lax.axis_index("tensor")
    count = out_ref.shape[0]
    start = pl.multiple_of(member * count, HS)
    pooled = pooled_half_ref[:, pl.ds(start, count)].astype(F32)
    grad_logits = grad_logits_ref[...].astype(F32)

    def padded(rows):
        empty = jnp.zeros((-rows.shape[0] % 16, rows.shape[1]), F32)
        return jnp.concatenate([rows, empty], axis=0).astype(BF16)

    out_ref[...] = dot_tn(padded(pooled), padded(grad_logits)).astype(BF16)


def join_kernel(*refs):
    refs[-1][...] = jnp.concatenate([ref[...] for ref in refs[:-1]], axis=0)


def norm_rows_kernel(first, rows_ref, gain_ref, out_ref):
    rows = rows_ref[first : first + out_ref.shape[0], :].astype(F32)
    unit_rows, _ = norm_parts(rows)
    out_ref[...] = (unit_rows * gain_ref[...]).astype(BF16)


def norm_margin_kernel(
    first, flag_ref, rows_ref, received_ref, select_ref, gain_ref, out_ref, margin_ref, sums_ref
):
    own = rows_ref[first : first + out_ref.shape[0], :]
    margin = jnp.where(flag_ref[0] == 1, own.astype(F32), received_ref[...].astype(F32))
    margin_ref[...] = margin.astype(BF16)
    unit_rows, _ = norm_parts(margin)
    out_ref[...] = (unit_rows * gain_ref[...]).astype(BF16)
    select = select_ref[...]
    for image in range(select.shape[1]):
        sums_ref[image : image + 1, :] = jnp.sum(
            margin * select[:, image : image + 1], axis=0, keepdims=True
        )


def out_rows_kernel(first, rows_ref, *refs):
    *terms, out_ref = refs
    total = sum(term[...].astype(F32) for term in terms)
    rows = rows_ref[first : first + out_ref.shape[0], :].astype(F32)
    out_ref[...] = (rows + total).astype(BF16)


def judge_kernel(
    patch_count,
    pooled_ref,
    gain_ref,
    head_ref,
    label_ref,
    out_weight_ref,
    loss_ref,
    pooled_half_ref,
    grad_logits_ref,
    grad_image_ref,
    per_image_ref,
):
    image_count = pooled_ref.shape[0]
    unit_rows, inverse = norm_parts(pooled_ref[...] * (1.0 / patch_count))
    gain_row = gain_ref[...]
    pooled_half = (unit_rows * gain_row).astype(BF16)
    pooled_half_ref[...] = pooled_half
    head = head_ref[...]
    logits = dot(pooled_half, head)
    classes = lax.broadcasted_iota(jnp.int32, logits.shape, 1)
    images = lax.broadcasted_iota(jnp.int32, logits.shape, 0)
    label = jnp.zeros_like(classes)
    for image in range(image_count):
        label = jnp.where(images == image, label_ref[image], label)
    targets = (classes == label).astype(F32)
    softplus = jnp.maximum(logits, 0.0) + jnp.log1p(jnp.exp(-jnp.abs(logits)))
    terms = softplus - targets * logits
    for image in range(image_count):
        loss_ref[0, image] = jnp.sum(terms[image : image + 1, :]) * (1.0 / terms.shape[1])
    sigmoid = 1.0 / (1.0 + jnp.exp(-logits))
    grad_logits = ((sigmoid - targets) * (1.0 / image_count)).astype(BF16)
    grad_logits_ref[...] = grad_logits
    grad_pooled = norm_back(dot_nt(grad_logits, head), unit_rows, inverse, gain_row)
    grad_image = grad_pooled * (1.0 / patch_count)
    grad_image_ref[...] = grad_image
    per_image_ref[...] = dot_nt(grad_image.astype(BF16), out_weight_ref[...])


def grad_rows_kernel(rows_ref, select_ref, grad_image_ref, gain_ref, *refs):
    *terms, out_ref = refs
    unit_rows, inverse = norm_parts(rows_ref[...].astype(F32))
    grad = sum(term[...].astype(F32) for term in terms)
    total = norm_back(grad, unit_rows, inverse, gain_ref[...])
    select = select_ref[...]
    for image in range(grad_image_ref.shape[0]):
        total = total + select[:, image : image + 1] * grad_image_ref[image : image + 1, :]
    out_ref[...] = total.astype(BF16)


def on_device(
    block_inputs, qkv_weights, out_weights, norm_gain, query_key_gain, pool_gain, class_head, labels
):
    rows_in = block_inputs[0]
    qkv_local = qkv_weights[0]
    out_local = out_weights[0]
    gain_pair = query_key_gain[0]
    label_row = labels[0]
    local_count, model_width = rows_in.shape
    image_count = label_row.shape[0]
    class_count = class_head.shape[2]
    depth, width = lax.axis_size("dp"), lax.axis_size("tensor")
    group_size = depth * width
    row_count = local_count * group_size
    lane_count = qkv_local.shape[2]
    half = local_count // HALVES
    place = (local_count, depth, width)
    member = lax.axis_index(GROUP)
    image_ids = (member * local_count + lax.iota(jnp.int32, local_count)) // PATCHES
    own_select = (image_ids[:, None] == lax.iota(jnp.int32, image_count)[None, :]).astype(F32)

    def shape(dims, dtype=F32):
        return jax.ShapeDtypeStruct(dims, dtype)

    half_shape = shape((half, model_width), BF16)
    three = (3, row_count, lane_count)
    slab_rows = local_count * width
    heads = image_count * (lane_count // HS)
    product_flops = 2 * row_count * lane_count * PATCHES
    slab_flops = 2 * slab_rows * model_width * lane_count
    chunk = 2 * PATCHES if model_width % (2 * PATCHES) == 0 else PATCHES
    piece_shapes = [half_shape] * (width * HALVES)

    select_halves = [own_select[h * half : (h + 1) * half] for h in range(HALVES)]

    def project(_, pieces):
        return call(
            project_kernel,
            [shape((3, slab_rows, lane_count)), shape((model_width, slab_rows), BF16)],
            (*pieces, qkv_local),
            flops=3 * slab_flops,
            limit=12,
        )

    def state_of(projected):
        return call(
            functools.partial(state_kernel, *place),
            [
                shape((heads, PATCHES, PATCHES)),
                shape((heads, PATCHES, PATCHES), BF16),
                shape(three, BF16),
                shape((2, row_count, lane_count)),
                shape((2, row_count, lane_count // HS)),
            ],
            (*projected, gain_pair),
            scratch=[pltpu.VMEM(three, F32)],
            flops=2 * product_flops,
        )

    _, own_results = gather_slabs(
        [
            call(
                functools.partial(norm_rows_kernel, h * half),
                half_shape,
                (rows_in, norm_gain),
                limit=4,
            )
            for h in range(HALVES)
        ],
        project,
    )
    own_projected, own_turned = zip(*own_results)
    attention = call(
        functools.partial(attend_own_kernel, *place),
        shape((row_count, lane_count), BF16),
        (*own_projected, gain_pair),
        scratch=[pltpu.VMEM(three, F32), pltpu.VMEM(three[1:], BF16)],
        flops=2 * product_flops,
    )

    def branch(s):
        return call(
            functools.partial(branch_kernel, slab_starts(s, half, depth, width, OUT_WAYS)),
            piece_shapes,
            (attention, out_local),
            flops=slab_flops,
            limit=12,
        )

    out_halves = [
        call(
            functools.partial(out_rows_kernel, h * half),
            half_shape,
            (rows_in, *terms),
            limit=4,
        )
        for h, terms in enumerate(scatter_slabs(branch, OUT_WAYS))
    ]

    first = (lax.axis_index("section") == 0).astype(jnp.int32).reshape(1)
    margin_normed, margin_halves, row_sums = zip(
        *[
            call(
                functools.partial(norm_margin_kernel, h * half),
                [half_shape, half_shape, shape((image_count, model_width))],
                (first, rows_in, from_behind(out, "section", 1), select, norm_gain),
                specs=[SMEM_SPEC] + [VMEM_SPEC] * 4,
                limit=4,
            )
            for h, (out, select) in enumerate(zip(out_halves, select_halves))
        ]
    )
    _, margin_results = gather_slabs(margin_normed, project)
    margin_projected, margin_turned = zip(*margin_results)
    image_sums, pooled_part = call(
        functools.partial(attend_margin_kernel, *place),
        [shape((image_count, lane_count)), shape((image_count, model_width))],
        (*margin_projected, gain_pair, out_local, *row_sums),
        scratch=[pltpu.VMEM(three, F32)],
        flops=2 * product_flops,
    )
    margin_state = state_of(margin_projected)
    own_state = state_of(own_projected)
    out_own = call(join_kernel, shape((local_count, model_width), BF16), tuple(out_halves), limit=4)
    pooled = after(sum_group(pooled_part), margin_state[4], own_state[4], out_own)
    losses, pooled_half, grad_logits, grad_image, per_image = call(
        functools.partial(judge_kernel, PATCHES),
        [
            shape((1, image_count)),
            shape((image_count, model_width), BF16),
            shape((image_count, class_count), BF16),
            shape((image_count, model_width)),
            shape((image_count, lane_count)),
        ],
        (pooled, pool_gain, class_head[0], label_row, out_local),
        specs=[VMEM_SPEC] * 3 + [SMEM_SPEC, VMEM_SPEC],
        outs=[SMEM_SPEC] + [VMEM_SPEC] * 4,
        flops=4 * class_count * model_width * 8,
        limit=12,
    )
    grad_head = call(
        functools.partial(head_gradient_kernel, width),
        shape((model_width // group_size, class_count), BF16),
        (pooled_half, grad_logits),
        limit=4,
    )

    margin_gradient = call(
        functools.partial(attend_back_kernel, *place, True),
        shape((row_count, 3 * lane_count), BF16),
        (*margin_state, per_image, gain_pair),
        scratch=[pltpu.VMEM(three, F32)],
        flops=5 * product_flops,
    )

    def input_term(s):
        return call(
            functools.partial(input_kernel, slab_starts(s, half, depth, width, GRAD_WAYS)),
            piece_shapes,
            (margin_gradient, qkv_local),
            flops=3 * slab_flops,
            limit=12,
        )

    grad_normed = scatter_slabs(input_term, GRAD_WAYS)
    grad_inputs = [
        call(
            grad_rows_kernel,
            half_shape,
            (rows, select, grad_image, norm_gain, *terms),
            limit=6,
        )
        for terms, rows, select in zip(grad_normed, margin_halves, select_halves)
    ]
    returned = [from_behind(grad, "section", -1) for grad in grad_inputs]

    def cotangent(s, pieces):
        if s == 0:
            pieces = [after(pieces[0], grad_head)] + pieces[1:]
        return call(
            cotangent_kernel,
            [shape((slab_rows, lane_count)), shape((slab_rows, model_width), BF16)],
            (*pieces, out_local),
            flops=slab_flops,
            limit=12,
        )

    _, cotangent_results = gather_slabs(returned, cotangent)
    grad_attention, cotangent_slabs = zip(*cotangent_results)
    own_gradient = call(
        functools.partial(attend_back_kernel, *place, False),
        shape((row_count, 3 * lane_count), BF16),
        (*own_state, *grad_attention, gain_pair),
        scratch=[pltpu.VMEM(three, F32), pltpu.VMEM(three[1:], F32)],
        flops=5 * product_flops,
    )
    turned = (*margin_turned, *own_turned)
    query_key_value_gradient = call(
        functools.partial(weight_gradient_kernel, len(turned), chunk),
        shape((3, model_width, lane_count), BF16),
        (*turned, margin_gradient, own_gradient),
        specs=[HBM_SPEC] * len(turned) + [VMEM_SPEC] * 2,
        outs=HBM_SPEC,
        scratch=[pltpu.VMEM((2 * row_count, 3 * lane_count), BF16)],
        flops=6 * depth * slab_flops,
        moved=6 * model_width * lane_count,
        limit=60,
    )
    wide = 2 * chunk if model_width % (2 * chunk) == 0 else chunk
    grad_out = call(
        functools.partial(out_gradient_kernel, wide),
        shape((lane_count, model_width), BF16),
        (*cotangent_slabs, attention, image_sums, grad_image),
        specs=[HBM_SPEC] * depth + [VMEM_SPEC] * 2 + [HBM_SPEC],
        outs=HBM_SPEC,
        flops=depth * slab_flops,
        moved=4 * model_width * lane_count,
        limit=60,
    )
    return (
        out_own[None],
        query_key_value_gradient[None],
        grad_out[None],
        grad_head[None],
        losses,
    )


def solution(mesh):
    in_specs = (
        P("section", GROUP, None),
        P("section", None, None, GROUP),
        P("section", GROUP, None),
        P("section", None),
        P("section", None, None),
        P("section", None),
        P("section", None, None),
        P("section", None),
    )
    out_specs = (
        P("section", GROUP, None),
        P("section", None, None, GROUP),
        P("section", GROUP, None),
        P("section", GROUP, None),
        P("section", None),
    )
    return jax.shard_map(
        on_device, mesh=mesh, in_specs=in_specs, out_specs=out_specs, check_vma=False
    )
```

```python
import functools
import math

import jax
import jax.numpy as jnp
from jax import lax
from jax.experimental import pallas as pl
from jax.experimental.pallas import tpu as pltpu
from jax.sharding import PartitionSpec as P

HS = 128
PATCHES = 256
GROUP = ("dp", "tensor")
HALVES = 2
OUT_WAYS = (1, 1)
GRAD_WAYS = (1, 1)
GRAD_OUT_LIMIT = 24

epsilon = 1e-06
F32 = jnp.float32
BF16 = jnp.bfloat16
VMEM_SPEC = pl.BlockSpec(memory_space=pltpu.VMEM)
HBM_SPEC = pl.BlockSpec(memory_space=pltpu.HBM)
SMEM_SPEC = pl.BlockSpec(memory_space=pltpu.SMEM)


def from_behind(block, axis, distance):
    devices = range(lax.axis_size(axis))
    route = [(i - distance, i) for i in devices if i - distance in devices]
    return lax.ppermute(block, axis, route)


def shift(block, axis, distance):
    count = lax.axis_size(axis)
    return lax.ppermute(block, axis, [(i, (i + distance) % count) for i in range(count)])


def after(value, *others):
    return lax.optimization_barrier((value,) + others)[0]


def way(half):
    return 1 if half % 2 == 0 else -1


def gather_slabs(halves, work):
    depth, width = lax.axis_size("dp"), lax.axis_size("tensor")
    ring, slabs, results = [list(halves)], [], []
    across = [[None] * HALVES for _ in range(width)]
    for s in range(depth):
        if s:
            ring.append([shift(ring[-1][h], "dp", way(h)) for h in range(HALVES)])
        pieces = list(ring[s])
        for j in range(1, width):
            for h in range(HALVES):
                piece = ring[s][h]
                if s:
                    piece = after(piece, across[j][h], *[r[0] for r in results[: s - 1][-1:]])
                across[j][h] = shift(piece, "tensor", j)
                pieces.append(across[j][h])
        slabs.append(pieces)
        results.append(work(s, pieces))
    return slabs, results


def scatter_slabs(slab_pieces, ways):
    depth, width = lax.axis_size("dp"), lax.axis_size("tensor")
    running = [None] * HALVES
    last = [[None] * HALVES for _ in range(width)]
    for s in list(range(1, depth)) + [0]:
        terms = slab_pieces(s)
        for h in range(HALVES):
            parts = [terms[h]]
            for j in range(1, width):
                piece = terms[j * HALVES + h]
                if last[j][h] is not None:
                    piece = after(piece, last[j][h])
                last[j][h] = shift(piece, "tensor", -j)
                parts.append(last[j][h])
            if running[h] is not None:
                parts.append(shift(running[h], "dp", ways[h]))
            running[h] = parts if s == 0 else sum(part.astype(F32) for part in parts).astype(BF16)
    return running


def slab_starts(s, half, depth, width, ways):
    starts = []
    for j in range(width):
        for h in range(HALVES):
            slab = s if ways[h] == way(h) else (depth - s) % depth
            starts.append(((slab * width + j) * HALVES + h) * half)
    return tuple(starts)


def exchange(value, axis, steps):
    route = [(i, i ^ steps) for i in range(lax.axis_size(axis))]
    return lax.ppermute(value, axis, route)


def sum_group(value):
    counts = [lax.axis_size(axis) for axis in ("tensor", "dp")]
    if any(count & (count - 1) for count in counts):
        return lax.psum(value, GROUP)
    for axis, count in zip(("tensor", "dp"), counts):
        parts = [value] + [exchange(value, axis, step) for step in range(1, count)]
        while len(parts) > 1:
            parts = [parts[i] + parts[i + 1] for i in range(0, len(parts), 2)]
        value = parts[0]
    return value


def norm_parts(values):
    centered = values - jnp.mean(values, axis=-1, keepdims=True)
    inverse = lax.rsqrt(jnp.mean(centered * centered, axis=-1, keepdims=True) + epsilon)
    return centered * inverse, inverse


def norm_back(grad_normed, unit_rows, inverse, gain_row):
    scaled = grad_normed * gain_row
    return inverse * (
        scaled
        - jnp.mean(scaled, axis=-1, keepdims=True)
        - unit_rows * jnp.mean(scaled * unit_rows, axis=-1, keepdims=True)
    )


def dot_nt(left, right):
    return lax.dot_general(left, right, (((1,), (1,)), ((), ())), preferred_element_type=F32)


def dot_tn(left, right):
    return lax.dot_general(left, right, (((0,), (0,)), ((), ())), preferred_element_type=F32)


def dot(left, right):
    return jnp.dot(left, right, preferred_element_type=F32)


def call(
    kernel, out_shape, ins, specs=None, outs=None, scratch=(), flops=0, moved=1000000, limit=16
):
    many = isinstance(out_shape, (tuple, list))
    return pl.pallas_call(
        kernel,
        out_shape=out_shape,
        in_specs=specs or [VMEM_SPEC] * len(ins),
        out_specs=outs or ([VMEM_SPEC] * len(out_shape) if many else VMEM_SPEC),
        scratch_shapes=list(scratch),
        compiler_params=pltpu.CompilerParams(vmem_limit_bytes=limit * 2**20),
        cost_estimate=pl.CostEstimate(flops=flops, bytes_accessed=moved, transcendentals=0),
    )(*ins)


def piece_rows(local_count, depth, width):
    half = local_count // HALVES
    z, y = lax.axis_index("dp"), lax.axis_index("tensor")
    out = []
    for s in range(depth):
        for j in range(width):
            for h in range(HALVES):
                far_z = lax.rem(z + (depth - s if way(h) > 0 else s), depth)
                far_y = lax.rem(y + width - j, width)
                first = (far_z * width + far_y) * local_count + h * half
                out.append(
                    (((s * width + j) * HALVES + h) * half, pl.multiple_of(first, half), half)
                )
    return out


def to_section_order(slabs, held, pieces):
    rows = held.shape[-2] // len(slabs)
    for ring, first, count in pieces:
        s, r = divmod(ring, rows)
        if len(held.shape) == 3:
            held[:, pl.ds(first, count), :] = slabs[s][:, r : r + count, :].astype(held.dtype)
        else:
            held[pl.ds(first, count), :] = slabs[s][r : r + count, :].astype(held.dtype)


def to_ring_order(held, out, pieces):
    for ring, first, count in pieces:
        if len(held.shape) == 3:
            out[:, ring : ring + count, :] = held[:, pl.ds(first, count), :].astype(out.dtype)
        else:
            out[ring : ring + count, :] = held[pl.ds(first, count), :].astype(out.dtype)


def to_joined_order(held, out, pieces):
    lane_count = held.shape[2]
    for ring, first, count in pieces:
        for t in range(held.shape[0]):
            part = held[t, pl.ds(first, count), :].astype(out.dtype)
            out[ring : ring + count, t * lane_count : (t + 1) * lane_count] = part


def head_forward(held, gains, rows, lanes):
    query_unit, query_inverse = norm_parts(held[0, rows, lanes])
    key_unit, key_inverse = norm_parts(held[1, rows, lanes])
    query_half = (query_unit * gains[0:1, :]).astype(BF16)
    key_half = (key_unit * gains[1:2, :]).astype(BF16)
    value_half = held[2, rows, lanes].astype(BF16)
    exponent = jnp.exp(dot_nt(query_half, key_half) * (1.0 / math.sqrt(HS)))
    probs = exponent * (1.0 / jnp.sum(exponent, axis=-1, keepdims=True))
    return (
        probs,
        probs.astype(BF16),
        query_half,
        key_half,
        value_half,
        query_unit,
        query_inverse,
        key_unit,
        key_inverse,
    )


def each_head(held):
    row_count, lane_count = held.shape[-2:]
    for image in range(row_count // PATCHES):
        for head in range(lane_count // HS):
            yield (
                image,
                slice(image * PATCHES, (image + 1) * PATCHES),
                slice(head * HS, (head + 1) * HS),
            )


def attend_own_kernel(local_count, depth, width, *refs):
    slabs, gain_ref, out_ref, held, mixed = refs[:depth], *refs[depth:]
    pieces = piece_rows(local_count, depth, width)
    to_section_order(slabs, held, pieces)
    gains = gain_ref[...]
    for _, rows, lanes in each_head(held):
        state = head_forward(held, gains, rows, lanes)
        mixed[rows, lanes] = dot(state[1], state[4]).astype(BF16)
    to_ring_order(mixed, out_ref, pieces)


def attend_margin_kernel(local_count, depth, width, *refs):
    slabs = refs[:depth]
    gain_ref, out_weight_ref = refs[depth : depth + 2]
    row_sums = refs[depth + 2 : depth + 2 + HALVES]
    sums_ref, pooled_ref, held = refs[depth + 2 + HALVES :]
    pieces = piece_rows(local_count, depth, width)
    to_section_order(slabs, held, pieces)
    gains = gain_ref[...]
    for image, rows, lanes in each_head(held):
        state = head_forward(held, gains, rows, lanes)
        mixed = dot(state[1], state[4]).astype(BF16)
        sums_ref[image : image + 1, lanes] = jnp.sum(mixed.astype(F32), axis=0, keepdims=True)
    sums = sums_ref[...]
    count = sums.shape[0]
    high = sums.astype(BF16).astype(F32)
    middle = (sums - high).astype(BF16).astype(F32)
    low = sums - high - middle
    empty = jnp.zeros((-3 * count % 16, sums.shape[1]), F32)
    stacked = jnp.concatenate([high, middle, low, empty], axis=0).astype(BF16)
    product = dot(stacked, out_weight_ref[...])
    pooled_ref[...] = sum(ref[...] for ref in row_sums) + (
        product[:count] + (product[count : 2 * count] + product[2 * count : 3 * count])
    )


def state_kernel(local_count, depth, width, *refs):
    slabs = refs[:depth]
    gain_ref, probs_ref, turned_ref, halves_ref, units_ref, inverse_ref, held = refs[depth:]
    to_section_order(slabs, held, piece_rows(local_count, depth, width))
    gains = gain_ref[...]
    for place, (_, rows, lanes) in enumerate(each_head(held)):
        head = lanes.start // HS
        state = head_forward(held, gains, rows, lanes)
        probs_ref[place, :, :] = state[0]
        turned_ref[place, :, :] = state[1].T
        for t in range(3):
            halves_ref[t, rows, lanes] = state[2 + t]
        for t in range(2):
            units_ref[t, rows, lanes] = state[5 + 2 * t]
            inverse_ref[t, rows, head : head + 1] = state[6 + 2 * t]


def attend_back_kernel(local_count, depth, width, broadcast, *refs):
    probs_ref, turned_ref, halves_ref, units_ref, inverse_ref = refs[:5]
    grads = refs[5 : 6 if broadcast else 5 + depth]
    gain_ref, out_ref, held, *grad_held = refs[5 + len(grads) :]
    pieces = piece_rows(local_count, depth, width)
    if not broadcast:
        to_section_order(grads, grad_held[0], pieces)
    gains = gain_ref[...]
    for place, (image, rows, lanes) in enumerate(each_head(held)):
        head = lanes.start // HS
        if broadcast:
            row = grads[0][image : image + 1, lanes].astype(BF16).astype(F32)
            grad_mixed = jnp.broadcast_to(row, (PATCHES, HS)).astype(BF16)
        else:
            grad_mixed = grad_held[0][rows, lanes].astype(BF16)
        probs = probs_ref[place]
        grad_probs = dot_nt(grad_mixed, halves_ref[2, rows, lanes])
        weighted = probs * grad_probs
        grad_scores = weighted - probs * jnp.sum(weighted, axis=-1, keepdims=True)
        score_half = (grad_scores * (1.0 / math.sqrt(HS))).astype(BF16)
        grads_out = (
            dot(score_half, halves_ref[1, rows, lanes]),
            dot_tn(score_half, halves_ref[0, rows, lanes]),
        )
        for t in range(2):
            held[t, rows, lanes] = norm_back(
                grads_out[t],
                units_ref[t, rows, lanes],
                inverse_ref[t, rows, head : head + 1],
                gains[t : t + 1, :],
            )
        held[2, rows, lanes] = dot(turned_ref[place], grad_mixed)
    to_joined_order(held, out_ref, pieces)


def project_kernel(*refs):
    *pieces, weights_ref, projected_ref, turned_ref = refs
    rows = jnp.concatenate([ref[...] for ref in pieces], axis=0)
    for t in range(weights_ref.shape[0]):
        projected_ref[t, :, :] = dot(rows, weights_ref[t])
    turned_ref[...] = rows.T


def cotangent_kernel(*refs):
    *pieces, weights_ref, out_ref, slab_ref = refs
    rows = jnp.concatenate([ref[...] for ref in pieces], axis=0)
    out_ref[...] = dot_nt(rows, weights_ref[...])
    slab_ref[...] = rows


def to_pieces(total, outs):
    count = outs[0].shape[0]
    for i, out in enumerate(outs):
        out[...] = total[i * count : (i + 1) * count].astype(BF16)


def branch_kernel(starts, attention_ref, weights_ref, *outs):
    half = outs[0].shape[0]
    rows = jnp.concatenate([attention_ref[i : i + half, :] for i in starts], axis=0)
    to_pieces(dot(rows, weights_ref[...]), outs)


def input_kernel(starts, gradient_ref, weights_ref, *outs):
    half = outs[0].shape[0]
    projections, _, lane_count = weights_ref.shape
    total = None
    for t in range(projections):
        lanes = slice(t * lane_count, (t + 1) * lane_count)
        part = jnp.concatenate([gradient_ref[i : i + half, lanes] for i in starts], axis=0)
        part = dot_nt(part, weights_ref[t])
        total = part if total is None else total + part
    to_pieces(total, outs)


def weight_gradient_kernel(depth, *refs):
    *slabs, margin_ref, own_ref, out_ref = refs
    lane_count = out_ref.shape[2]
    total = None
    for blocks, gradient_ref in ((slabs[:depth], margin_ref), (slabs[depth:], own_ref)):
        turned = jnp.concatenate([block[...] for block in blocks], axis=1)
        part = dot(turned, gradient_ref[...])
        total = part if total is None else total + part
    for t in range(out_ref.shape[0]):
        out_ref[t, :, :] = total[:, t * lane_count : (t + 1) * lane_count].astype(BF16)


def out_gradient_kernel(*refs):
    *slabs, attention_ref, sums_ref, grad_image_ref, out_ref, turned = refs

    @pl.when(pl.program_id(0) == 0)
    def _():
        turned[...] = attention_ref[...].T

    total = dot(turned[...], jnp.concatenate([block[...] for block in slabs], axis=0))
    sums = sums_ref[...]
    image_count, lane_count = sums.shape
    sums = jnp.concatenate([sums, jnp.zeros((-image_count % 8, lane_count), F32)], axis=0).T
    grad_image = grad_image_ref[...].astype(BF16).astype(F32)
    for image in range(image_count):
        total = total + sums[:, image : image + 1] * grad_image[image : image + 1, :]
    out_ref[...] = total.astype(BF16)


def head_gradient_kernel(width, pooled_half_ref, grad_logits_ref, out_ref):
    member = lax.axis_index("dp") * width + lax.axis_index("tensor")
    count = out_ref.shape[0]
    start = pl.multiple_of(member * count, HS)
    pooled = pooled_half_ref[:, pl.ds(start, count)].astype(F32)
    grad_logits = grad_logits_ref[...].astype(F32)

    def padded(rows):
        empty = jnp.zeros((-rows.shape[0] % 16, rows.shape[1]), F32)
        return jnp.concatenate([rows, empty], axis=0).astype(BF16)

    out_ref[...] = dot_tn(padded(pooled), padded(grad_logits)).astype(BF16)


def join_kernel(*refs):
    refs[-1][...] = jnp.concatenate([ref[...] for ref in refs[:-1]], axis=0)


def norm_rows_kernel(first, rows_ref, gain_ref, out_ref):
    rows = rows_ref[first : first + out_ref.shape[0], :].astype(F32)
    unit_rows, _ = norm_parts(rows)
    out_ref[...] = (unit_rows * gain_ref[...]).astype(BF16)


def norm_margin_kernel(
    first, flag_ref, rows_ref, received_ref, select_ref, gain_ref, out_ref, margin_ref, sums_ref
):
    own = rows_ref[first : first + out_ref.shape[0], :]
    margin = jnp.where(flag_ref[0] == 1, own.astype(F32), received_ref[...].astype(F32))
    margin_ref[...] = margin.astype(BF16)
    unit_rows, _ = norm_parts(margin)
    out_ref[...] = (unit_rows * gain_ref[...]).astype(BF16)
    select = select_ref[...]
    for image in range(select.shape[1]):
        sums_ref[image : image + 1, :] = jnp.sum(
            margin * select[:, image : image + 1], axis=0, keepdims=True
        )


def out_rows_kernel(first, rows_ref, *refs):
    *terms, out_ref = refs
    total = sum(term[...].astype(F32) for term in terms)
    rows = rows_ref[first : first + out_ref.shape[0], :].astype(F32)
    out_ref[...] = (rows + total).astype(BF16)


def judge_kernel(
    patch_count,
    pooled_ref,
    gain_ref,
    head_ref,
    label_ref,
    out_weight_ref,
    loss_ref,
    pooled_half_ref,
    grad_logits_ref,
    grad_image_ref,
    per_image_ref,
):
    image_count = pooled_ref.shape[0]
    unit_rows, inverse = norm_parts(pooled_ref[...] * (1.0 / patch_count))
    gain_row = gain_ref[...]
    pooled_half = (unit_rows * gain_row).astype(BF16)
    pooled_half_ref[...] = pooled_half
    head = head_ref[...]
    logits = dot(pooled_half, head)
    classes = lax.broadcasted_iota(jnp.int32, logits.shape, 1)
    images = lax.broadcasted_iota(jnp.int32, logits.shape, 0)
    label = jnp.zeros_like(classes)
    for image in range(image_count):
        label = jnp.where(images == image, label_ref[image], label)
    targets = (classes == label).astype(F32)
    softplus = jnp.maximum(logits, 0.0) + jnp.log1p(jnp.exp(-jnp.abs(logits)))
    terms = softplus - targets * logits
    for image in range(image_count):
        loss_ref[0, image] = jnp.sum(terms[image : image + 1, :]) * (1.0 / terms.shape[1])
    sigmoid = 1.0 / (1.0 + jnp.exp(-logits))
    grad_logits = ((sigmoid - targets) * (1.0 / image_count)).astype(BF16)
    grad_logits_ref[...] = grad_logits
    grad_pooled = norm_back(dot_nt(grad_logits, head), unit_rows, inverse, gain_row)
    grad_image = grad_pooled * (1.0 / patch_count)
    grad_image_ref[...] = grad_image
    per_image_ref[...] = dot_nt(grad_image.astype(BF16), out_weight_ref[...])


def grad_rows_kernel(rows_ref, select_ref, grad_image_ref, gain_ref, *refs):
    *terms, out_ref = refs
    unit_rows, inverse = norm_parts(rows_ref[...].astype(F32))
    grad = sum(term[...].astype(F32) for term in terms)
    total = norm_back(grad, unit_rows, inverse, gain_ref[...])
    select = select_ref[...]
    for image in range(grad_image_ref.shape[0]):
        total = total + select[:, image : image + 1] * grad_image_ref[image : image + 1, :]
    out_ref[...] = total.astype(BF16)


def on_device(
    block_inputs, qkv_weights, out_weights, norm_gain, query_key_gain, pool_gain, class_head, labels
):
    rows_in = block_inputs[0]
    qkv_local = qkv_weights[0]
    out_local = out_weights[0]
    gain_pair = query_key_gain[0]
    label_row = labels[0]
    local_count, model_width = rows_in.shape
    image_count = label_row.shape[0]
    class_count = class_head.shape[2]
    depth, width = lax.axis_size("dp"), lax.axis_size("tensor")
    group_size = depth * width
    row_count = local_count * group_size
    lane_count = qkv_local.shape[2]
    half = local_count // HALVES
    place = (local_count, depth, width)
    member = lax.axis_index(GROUP)
    image_ids = (member * local_count + lax.iota(jnp.int32, local_count)) // PATCHES
    own_select = (image_ids[:, None] == lax.iota(jnp.int32, image_count)[None, :]).astype(F32)

    def shape(dims, dtype=F32):
        return jax.ShapeDtypeStruct(dims, dtype)

    half_shape = shape((half, model_width), BF16)
    three = (3, row_count, lane_count)
    slab_rows = local_count * width
    heads = image_count * (lane_count // HS)
    product_flops = 2 * row_count * lane_count * PATCHES
    slab_flops = 2 * slab_rows * model_width * lane_count
    chunk = 2 * PATCHES if model_width % (2 * PATCHES) == 0 else PATCHES
    piece_shapes = [half_shape] * (width * HALVES)

    select_halves = [own_select[h * half : (h + 1) * half] for h in range(HALVES)]

    def project(_, pieces):
        return call(
            project_kernel,
            [shape((3, slab_rows, lane_count)), shape((model_width, slab_rows), BF16)],
            (*pieces, qkv_local),
            flops=3 * slab_flops,
            limit=12,
        )

    def state_of(projected):
        return call(
            functools.partial(state_kernel, *place),
            [
                shape((heads, PATCHES, PATCHES)),
                shape((heads, PATCHES, PATCHES), BF16),
                shape(three, BF16),
                shape((2, row_count, lane_count)),
                shape((2, row_count, lane_count // HS)),
            ],
            (*projected, gain_pair),
            scratch=[pltpu.VMEM(three, F32)],
            flops=2 * product_flops,
        )

    _, own_results = gather_slabs(
        [
            call(
                functools.partial(norm_rows_kernel, h * half),
                half_shape,
                (rows_in, norm_gain),
                limit=4,
            )
            for h in range(HALVES)
        ],
        project,
    )
    own_projected, own_turned = zip(*own_results)
    attention = call(
        functools.partial(attend_own_kernel, *place),
        shape((row_count, lane_count), BF16),
        (*own_projected, gain_pair),
        scratch=[pltpu.VMEM(three, F32), pltpu.VMEM(three[1:], BF16)],
        flops=2 * product_flops,
    )

    def branch(s):
        return call(
            functools.partial(branch_kernel, slab_starts(s, half, depth, width, OUT_WAYS)),
            piece_shapes,
            (attention, out_local),
            flops=slab_flops,
            limit=12,
        )

    out_halves = [
        call(
            functools.partial(out_rows_kernel, h * half),
            half_shape,
            (rows_in, *terms),
            limit=4,
        )
        for h, terms in enumerate(scatter_slabs(branch, OUT_WAYS))
    ]

    first = (lax.axis_index("section") == 0).astype(jnp.int32).reshape(1)
    margin_normed, margin_halves, row_sums = zip(
        *[
            call(
                functools.partial(norm_margin_kernel, h * half),
                [half_shape, half_shape, shape((image_count, model_width))],
                (first, rows_in, from_behind(out, "section", 1), select, norm_gain),
                specs=[SMEM_SPEC] + [VMEM_SPEC] * 4,
                limit=4,
            )
            for h, (out, select) in enumerate(zip(out_halves, select_halves))
        ]
    )
    _, margin_results = gather_slabs(margin_normed, project)
    margin_projected, margin_turned = zip(*margin_results)
    image_sums, pooled_part = call(
        functools.partial(attend_margin_kernel, *place),
        [shape((image_count, lane_count)), shape((image_count, model_width))],
        (*margin_projected, gain_pair, out_local, *row_sums),
        scratch=[pltpu.VMEM(three, F32)],
        flops=2 * product_flops,
    )
    margin_state = state_of(margin_projected)
    own_state = state_of(own_projected)
    out_own = call(join_kernel, shape((local_count, model_width), BF16), tuple(out_halves), limit=4)
    pooled = after(sum_group(pooled_part), margin_state[4])
    losses, pooled_half, grad_logits, grad_image, per_image = call(
        functools.partial(judge_kernel, PATCHES),
        [
            shape((1, image_count)),
            shape((image_count, model_width), BF16),
            shape((image_count, class_count), BF16),
            shape((image_count, model_width)),
            shape((image_count, lane_count)),
        ],
        (pooled, pool_gain, class_head[0], label_row, out_local),
        specs=[VMEM_SPEC] * 3 + [SMEM_SPEC, VMEM_SPEC],
        outs=[SMEM_SPEC] + [VMEM_SPEC] * 4,
        flops=4 * class_count * model_width * 8,
        limit=12,
    )
    grad_head = call(
        functools.partial(head_gradient_kernel, width),
        shape((model_width // group_size, class_count), BF16),
        (pooled_half, grad_logits),
        limit=4,
    )

    margin_gradient = call(
        functools.partial(attend_back_kernel, *place, True),
        shape((row_count, 3 * lane_count), BF16),
        (*margin_state, per_image, gain_pair),
        scratch=[pltpu.VMEM(three, F32)],
        flops=5 * product_flops,
    )

    def input_term(s):
        return call(
            functools.partial(input_kernel, slab_starts(s, half, depth, width, GRAD_WAYS)),
            piece_shapes,
            (margin_gradient, qkv_local),
            flops=3 * slab_flops,
            limit=12,
        )

    grad_normed = scatter_slabs(input_term, GRAD_WAYS)
    grad_inputs = [
        call(
            grad_rows_kernel,
            half_shape,
            (rows, select, grad_image, norm_gain, *terms),
            limit=6,
        )
        for terms, rows, select in zip(grad_normed, margin_halves, select_halves)
    ]
    returned = [from_behind(grad, "section", -1) for grad in grad_inputs]

    def cotangent(s, pieces):
        if s < 2:
            beside = (grad_head, out_own) if s == 0 else (own_state[4],)
            pieces = [after(pieces[0], *beside)] + pieces[1:]
        return call(
            cotangent_kernel,
            [shape((slab_rows, lane_count)), shape((slab_rows, model_width), BF16)],
            (*pieces, out_local),
            flops=slab_flops,
            limit=12,
        )

    _, cotangent_results = gather_slabs(returned, cotangent)
    grad_attention, cotangent_slabs = zip(*cotangent_results)
    own_gradient = call(
        functools.partial(attend_back_kernel, *place, False),
        shape((row_count, 3 * lane_count), BF16),
        (*own_state, *grad_attention, gain_pair),
        scratch=[pltpu.VMEM(three, F32), pltpu.VMEM(three[1:], F32)],
        flops=5 * product_flops,
    )
    turned = (*margin_turned, *own_turned)
    query_key_value_gradient = pl.pallas_call(
        functools.partial(weight_gradient_kernel, depth),
        grid=(model_width // chunk,),
        out_shape=shape((3, model_width, lane_count), BF16),
        in_specs=[pl.BlockSpec((chunk, slab_rows), lambda i: (i, 0))] * len(turned)
        + [pl.BlockSpec((row_count, 3 * lane_count), lambda i: (0, 0))] * 2,
        out_specs=pl.BlockSpec((3, chunk, lane_count), lambda i: (0, i, 0)),
        compiler_params=pltpu.CompilerParams(vmem_limit_bytes=60 * 2**20),
        cost_estimate=pl.CostEstimate(
            flops=6 * depth * slab_flops,
            bytes_accessed=6 * model_width * lane_count,
            transcendentals=0,
        ),
    )(*turned, margin_gradient, own_gradient)
    wide = 2 * chunk if model_width % (2 * chunk) == 0 else chunk
    grad_out = pl.pallas_call(
        out_gradient_kernel,
        grid=(model_width // wide,),
        out_shape=shape((lane_count, model_width), BF16),
        in_specs=[pl.BlockSpec((slab_rows, wide), lambda i: (0, i))] * depth
        + [
            pl.BlockSpec((row_count, lane_count), lambda i: (0, 0)),
            pl.BlockSpec((image_count, lane_count), lambda i: (0, 0)),
            pl.BlockSpec((image_count, wide), lambda i: (0, i)),
        ],
        out_specs=pl.BlockSpec((lane_count, wide), lambda i: (0, i)),
        scratch_shapes=[pltpu.VMEM((lane_count, row_count), BF16)],
        compiler_params=pltpu.CompilerParams(vmem_limit_bytes=GRAD_OUT_LIMIT * 2**20),
        cost_estimate=pl.CostEstimate(
            flops=depth * slab_flops,
            bytes_accessed=4 * model_width * lane_count,
            transcendentals=0,
        ),
    )(*cotangent_slabs, attention, image_sums, grad_image)
    return (
        out_own[None],
        query_key_value_gradient[None],
        grad_out[None],
        grad_head[None],
        losses,
    )


def solution(mesh):
    in_specs = (
        P("section", GROUP, None),
        P("section", None, None, GROUP),
        P("section", GROUP, None),
        P("section", None),
        P("section", None, None),
        P("section", None),
        P("section", None, None),
        P("section", None),
    )
    out_specs = (
        P("section", GROUP, None),
        P("section", None, None, GROUP),
        P("section", GROUP, None),
        P("section", GROUP, None),
        P("section", None),
    )
    return jax.shard_map(
        on_device, mesh=mesh, in_specs=in_specs, out_specs=out_specs, check_vma=False
    )
```

```python
import functools
import math

import jax
import jax.numpy as jnp
from jax import lax
from jax.experimental import pallas as pl
from jax.experimental.pallas import tpu as pltpu
from jax.sharding import PartitionSpec as P

HS = 128
PATCHES = 256
GROUP = ("dp", "tensor")
HALVES = 2
OUT_WAYS = (1, 1)
GRAD_WAYS = (1, 1)
GRAD_OUT_LIMIT = 24

epsilon = 1e-06
F32 = jnp.float32
BF16 = jnp.bfloat16
VMEM_SPEC = pl.BlockSpec(memory_space=pltpu.VMEM)
HBM_SPEC = pl.BlockSpec(memory_space=pltpu.HBM)
SMEM_SPEC = pl.BlockSpec(memory_space=pltpu.SMEM)


def from_behind(block, axis, distance):
    devices = range(lax.axis_size(axis))
    route = [(i - distance, i) for i in devices if i - distance in devices]
    return lax.ppermute(block, axis, route)


def shift(block, axis, distance):
    count = lax.axis_size(axis)
    return lax.ppermute(block, axis, [(i, (i + distance) % count) for i in range(count)])


def after(value, *others):
    return lax.optimization_barrier((value,) + others)[0]


def way(half):
    return 1


def gather_slabs(halves, work):
    depth, width = lax.axis_size("dp"), lax.axis_size("tensor")
    ring, slabs, results = [list(halves)], [], []
    across = [[None] * HALVES for _ in range(width)]
    for s in range(depth):
        if s:
            ring.append([shift(ring[-1][h], "dp", way(h)) for h in range(HALVES)])
        pieces = list(ring[s])
        for j in range(1, width):
            for h in range(HALVES):
                piece = ring[s][h]
                if s:
                    piece = after(piece, across[j][h], *[r[0] for r in results[: s - 1][-1:]])
                across[j][h] = shift(piece, "tensor", j)
                pieces.append(across[j][h])
        slabs.append(pieces)
        results.append(work(s, pieces))
    return slabs, results


def scatter_slabs(slab_pieces, ways):
    depth, width = lax.axis_size("dp"), lax.axis_size("tensor")
    running = [None] * HALVES
    last = [[None] * HALVES for _ in range(width)]
    for s in list(range(1, depth)) + [0]:
        terms = slab_pieces(s)
        for h in range(HALVES):
            parts = [terms[h]]
            for j in range(1, width):
                piece = terms[j * HALVES + h]
                if last[j][h] is not None:
                    piece = after(piece, last[j][h])
                last[j][h] = shift(piece, "tensor", -j)
                parts.append(last[j][h])
            if running[h] is not None:
                parts.append(shift(running[h], "dp", ways[h]))
            running[h] = parts if s == 0 else sum(part.astype(F32) for part in parts).astype(BF16)
    return running


def slab_starts(s, half, depth, width, ways):
    starts = []
    for j in range(width):
        for h in range(HALVES):
            slab = s if ways[h] == way(h) else (depth - s) % depth
            starts.append(((slab * width + j) * HALVES + h) * half)
    return tuple(starts)


def exchange(value, axis, steps):
    route = [(i, i ^ steps) for i in range(lax.axis_size(axis))]
    return lax.ppermute(value, axis, route)


def sum_group(value):
    counts = [lax.axis_size(axis) for axis in ("tensor", "dp")]
    if any(count & (count - 1) for count in counts):
        return lax.psum(value, GROUP)
    for axis, count in zip(("tensor", "dp"), counts):
        parts = [value] + [exchange(value, axis, step) for step in range(1, count)]
        while len(parts) > 1:
            parts = [parts[i] + parts[i + 1] for i in range(0, len(parts), 2)]
        value = parts[0]
    return value


def norm_parts(values):
    centered = values - jnp.mean(values, axis=-1, keepdims=True)
    inverse = lax.rsqrt(jnp.mean(centered * centered, axis=-1, keepdims=True) + epsilon)
    return centered * inverse, inverse


def norm_back(grad_normed, unit_rows, inverse, gain_row):
    scaled = grad_normed * gain_row
    return inverse * (
        scaled
        - jnp.mean(scaled, axis=-1, keepdims=True)
        - unit_rows * jnp.mean(scaled * unit_rows, axis=-1, keepdims=True)
    )


def dot_nt(left, right):
    return lax.dot_general(left, right, (((1,), (1,)), ((), ())), preferred_element_type=F32)


def dot_tn(left, right):
    return lax.dot_general(left, right, (((0,), (0,)), ((), ())), preferred_element_type=F32)


def dot(left, right):
    return jnp.dot(left, right, preferred_element_type=F32)


def call(
    kernel, out_shape, ins, specs=None, outs=None, scratch=(), flops=0, moved=1000000, limit=16
):
    many = isinstance(out_shape, (tuple, list))
    return pl.pallas_call(
        kernel,
        out_shape=out_shape,
        in_specs=specs or [VMEM_SPEC] * len(ins),
        out_specs=outs or ([VMEM_SPEC] * len(out_shape) if many else VMEM_SPEC),
        scratch_shapes=list(scratch),
        compiler_params=pltpu.CompilerParams(vmem_limit_bytes=limit * 2**20),
        cost_estimate=pl.CostEstimate(flops=flops, bytes_accessed=moved, transcendentals=0),
    )(*ins)


def piece_rows(local_count, depth, width):
    half = local_count // HALVES
    z, y = lax.axis_index("dp"), lax.axis_index("tensor")
    out = []
    for s in range(depth):
        for j in range(width):
            for h in range(HALVES):
                far_z = lax.rem(z + (depth - s if way(h) > 0 else s), depth)
                far_y = lax.rem(y + width - j, width)
                first = (far_z * width + far_y) * local_count + h * half
                out.append(
                    (((s * width + j) * HALVES + h) * half, pl.multiple_of(first, half), half)
                )
    return out


def to_section_order(slabs, held, pieces):
    rows = held.shape[-2] // len(slabs)
    for ring, first, count in pieces:
        s, r = divmod(ring, rows)
        if len(held.shape) == 3:
            held[:, pl.ds(first, count), :] = slabs[s][:, r : r + count, :].astype(held.dtype)
        else:
            held[pl.ds(first, count), :] = slabs[s][r : r + count, :].astype(held.dtype)


def to_ring_order(held, out, pieces):
    for ring, first, count in pieces:
        if len(held.shape) == 3:
            out[:, ring : ring + count, :] = held[:, pl.ds(first, count), :].astype(out.dtype)
        else:
            out[ring : ring + count, :] = held[pl.ds(first, count), :].astype(out.dtype)


def to_joined_order(held, out, pieces):
    lane_count = held.shape[2]
    for ring, first, count in pieces:
        for t in range(held.shape[0]):
            part = held[t, pl.ds(first, count), :].astype(out.dtype)
            out[ring : ring + count, t * lane_count : (t + 1) * lane_count] = part


def head_forward(held, gains, rows, lanes):
    query_unit, query_inverse = norm_parts(held[0, rows, lanes])
    key_unit, key_inverse = norm_parts(held[1, rows, lanes])
    query_half = (query_unit * gains[0:1, :]).astype(BF16)
    key_half = (key_unit * gains[1:2, :]).astype(BF16)
    value_half = held[2, rows, lanes].astype(BF16)
    exponent = jnp.exp(dot_nt(query_half, key_half) * (1.0 / math.sqrt(HS)))
    probs = exponent * (1.0 / jnp.sum(exponent, axis=-1, keepdims=True))
    return (
        probs,
        probs.astype(BF16),
        query_half,
        key_half,
        value_half,
        query_unit,
        query_inverse,
        key_unit,
        key_inverse,
    )


def each_head(held):
    row_count, lane_count = held.shape[-2:]
    for image in range(row_count // PATCHES):
        for head in range(lane_count // HS):
            yield (
                image,
                slice(image * PATCHES, (image + 1) * PATCHES),
                slice(head * HS, (head + 1) * HS),
            )


def attend_own_kernel(local_count, depth, width, *refs):
    slabs, gain_ref, out_ref, held, mixed = refs[:depth], *refs[depth:]
    pieces = piece_rows(local_count, depth, width)
    to_section_order(slabs, held, pieces)
    gains = gain_ref[...]
    for _, rows, lanes in each_head(held):
        state = head_forward(held, gains, rows, lanes)
        mixed[rows, lanes] = dot(state[1], state[4]).astype(BF16)
    to_ring_order(mixed, out_ref, pieces)


def attend_margin_kernel(local_count, depth, width, *refs):
    slabs = refs[:depth]
    gain_ref, out_weight_ref = refs[depth : depth + 2]
    row_sums = refs[depth + 2 : depth + 2 + HALVES]
    sums_ref, pooled_ref, held = refs[depth + 2 + HALVES :]
    pieces = piece_rows(local_count, depth, width)
    to_section_order(slabs, held, pieces)
    gains = gain_ref[...]
    for image, rows, lanes in each_head(held):
        state = head_forward(held, gains, rows, lanes)
        mixed = dot(state[1], state[4]).astype(BF16)
        sums_ref[image : image + 1, lanes] = jnp.sum(mixed.astype(F32), axis=0, keepdims=True)
    sums = sums_ref[...]
    count = sums.shape[0]
    high = sums.astype(BF16).astype(F32)
    middle = (sums - high).astype(BF16).astype(F32)
    low = sums - high - middle
    empty = jnp.zeros((-3 * count % 16, sums.shape[1]), F32)
    stacked = jnp.concatenate([high, middle, low, empty], axis=0).astype(BF16)
    product = dot(stacked, out_weight_ref[...])
    pooled_ref[...] = sum(ref[...] for ref in row_sums) + (
        product[:count] + (product[count : 2 * count] + product[2 * count : 3 * count])
    )


def state_kernel(local_count, depth, width, *refs):
    slabs = refs[:depth]
    gain_ref, probs_ref, turned_ref, halves_ref, units_ref, inverse_ref, held = refs[depth:]
    to_section_order(slabs, held, piece_rows(local_count, depth, width))
    gains = gain_ref[...]
    for place, (_, rows, lanes) in enumerate(each_head(held)):
        head = lanes.start // HS
        state = head_forward(held, gains, rows, lanes)
        probs_ref[place, :, :] = state[0]
        turned_ref[place, :, :] = state[1].T
        for t in range(3):
            halves_ref[t, rows, lanes] = state[2 + t]
        for t in range(2):
            units_ref[t, rows, lanes] = state[5 + 2 * t]
            inverse_ref[t, rows, head : head + 1] = state[6 + 2 * t]


def attend_back_kernel(local_count, depth, width, broadcast, *refs):
    probs_ref, turned_ref, halves_ref, units_ref, inverse_ref = refs[:5]
    grads = refs[5 : 6 if broadcast else 5 + depth]
    gain_ref, out_ref, held, *grad_held = refs[5 + len(grads) :]
    pieces = piece_rows(local_count, depth, width)
    if not broadcast:
        to_section_order(grads, grad_held[0], pieces)
    gains = gain_ref[...]
    for place, (image, rows, lanes) in enumerate(each_head(held)):
        head = lanes.start // HS
        if broadcast:
            row = grads[0][image : image + 1, lanes].astype(BF16).astype(F32)
            grad_mixed = jnp.broadcast_to(row, (PATCHES, HS)).astype(BF16)
        else:
            grad_mixed = grad_held[0][rows, lanes].astype(BF16)
        probs = probs_ref[place]
        grad_probs = dot_nt(grad_mixed, halves_ref[2, rows, lanes])
        weighted = probs * grad_probs
        grad_scores = weighted - probs * jnp.sum(weighted, axis=-1, keepdims=True)
        score_half = (grad_scores * (1.0 / math.sqrt(HS))).astype(BF16)
        grads_out = (
            dot(score_half, halves_ref[1, rows, lanes]),
            dot_tn(score_half, halves_ref[0, rows, lanes]),
        )
        for t in range(2):
            held[t, rows, lanes] = norm_back(
                grads_out[t],
                units_ref[t, rows, lanes],
                inverse_ref[t, rows, head : head + 1],
                gains[t : t + 1, :],
            )
        held[2, rows, lanes] = dot(turned_ref[place], grad_mixed)
    to_joined_order(held, out_ref, pieces)


def project_kernel(*refs):
    *pieces, weights_ref, projected_ref, turned_ref = refs
    rows = jnp.concatenate([ref[...] for ref in pieces], axis=0)
    for t in range(weights_ref.shape[0]):
        projected_ref[t, :, :] = dot(rows, weights_ref[t])
    turned_ref[...] = rows.T


def cotangent_kernel(*refs):
    *pieces, weights_ref, out_ref, slab_ref = refs
    rows = jnp.concatenate([ref[...] for ref in pieces], axis=0)
    out_ref[...] = dot_nt(rows, weights_ref[...])
    slab_ref[...] = rows


def to_pieces(total, outs):
    count = outs[0].shape[0]
    for i, out in enumerate(outs):
        out[...] = total[i * count : (i + 1) * count].astype(BF16)


def branch_kernel(starts, attention_ref, weights_ref, *outs):
    half = outs[0].shape[0]
    rows = jnp.concatenate([attention_ref[i : i + half, :] for i in starts], axis=0)
    to_pieces(dot(rows, weights_ref[...]), outs)


def input_kernel(starts, gradient_ref, weights_ref, *outs):
    half = outs[0].shape[0]
    projections, _, lane_count = weights_ref.shape
    total = None
    for t in range(projections):
        lanes = slice(t * lane_count, (t + 1) * lane_count)
        part = jnp.concatenate([gradient_ref[i : i + half, lanes] for i in starts], axis=0)
        part = dot_nt(part, weights_ref[t])
        total = part if total is None else total + part
    to_pieces(total, outs)


def weight_gradient_kernel(depth, *refs):
    *slabs, margin_ref, own_ref, out_ref = refs
    lane_count = out_ref.shape[2]
    total = None
    for blocks, gradient_ref in ((slabs[:depth], margin_ref), (slabs[depth:], own_ref)):
        turned = jnp.concatenate([block[...] for block in blocks], axis=1)
        part = dot(turned, gradient_ref[...])
        total = part if total is None else total + part
    for t in range(out_ref.shape[0]):
        out_ref[t, :, :] = total[:, t * lane_count : (t + 1) * lane_count].astype(BF16)


def out_gradient_kernel(*refs):
    *slabs, attention_ref, sums_ref, grad_image_ref, out_ref, turned = refs

    @pl.when(pl.program_id(0) == 0)
    def _():
        turned[...] = attention_ref[...].T

    total = dot(turned[...], jnp.concatenate([block[...] for block in slabs], axis=0))
    sums = sums_ref[...]
    image_count, lane_count = sums.shape
    sums = jnp.concatenate([sums, jnp.zeros((-image_count % 8, lane_count), F32)], axis=0).T
    grad_image = grad_image_ref[...].astype(BF16).astype(F32)
    for image in range(image_count):
        total = total + sums[:, image : image + 1] * grad_image[image : image + 1, :]
    out_ref[...] = total.astype(BF16)


def head_gradient_kernel(width, pooled_half_ref, grad_logits_ref, out_ref):
    member = lax.axis_index("dp") * width + lax.axis_index("tensor")
    count = out_ref.shape[0]
    start = pl.multiple_of(member * count, HS)
    pooled = pooled_half_ref[:, pl.ds(start, count)].astype(F32)
    grad_logits = grad_logits_ref[...].astype(F32)

    def padded(rows):
        empty = jnp.zeros((-rows.shape[0] % 16, rows.shape[1]), F32)
        return jnp.concatenate([rows, empty], axis=0).astype(BF16)

    out_ref[...] = dot_tn(padded(pooled), padded(grad_logits)).astype(BF16)


def join_kernel(*refs):
    refs[-1][...] = jnp.concatenate([ref[...] for ref in refs[:-1]], axis=0)


def norm_rows_kernel(first, rows_ref, gain_ref, out_ref):
    rows = rows_ref[first : first + out_ref.shape[0], :].astype(F32)
    unit_rows, _ = norm_parts(rows)
    out_ref[...] = (unit_rows * gain_ref[...]).astype(BF16)


def norm_margin_kernel(
    first, flag_ref, rows_ref, received_ref, select_ref, gain_ref, out_ref, margin_ref, sums_ref
):
    own = rows_ref[first : first + out_ref.shape[0], :]
    margin = jnp.where(flag_ref[0] == 1, own.astype(F32), received_ref[...].astype(F32))
    margin_ref[...] = margin.astype(BF16)
    unit_rows, _ = norm_parts(margin)
    out_ref[...] = (unit_rows * gain_ref[...]).astype(BF16)
    select = select_ref[...]
    for image in range(select.shape[1]):
        sums_ref[image : image + 1, :] = jnp.sum(
            margin * select[:, image : image + 1], axis=0, keepdims=True
        )


def out_rows_kernel(first, rows_ref, *refs):
    *terms, out_ref = refs
    total = sum(term[...].astype(F32) for term in terms)
    rows = rows_ref[first : first + out_ref.shape[0], :].astype(F32)
    out_ref[...] = (rows + total).astype(BF16)


def judge_kernel(
    patch_count,
    pooled_ref,
    gain_ref,
    head_ref,
    label_ref,
    out_weight_ref,
    loss_ref,
    pooled_half_ref,
    grad_logits_ref,
    grad_image_ref,
    per_image_ref,
):
    image_count = pooled_ref.shape[0]
    unit_rows, inverse = norm_parts(pooled_ref[...] * (1.0 / patch_count))
    gain_row = gain_ref[...]
    pooled_half = (unit_rows * gain_row).astype(BF16)
    pooled_half_ref[...] = pooled_half
    head = head_ref[...]
    logits = dot(pooled_half, head)
    classes = lax.broadcasted_iota(jnp.int32, logits.shape, 1)
    images = lax.broadcasted_iota(jnp.int32, logits.shape, 0)
    label = jnp.zeros_like(classes)
    for image in range(image_count):
        label = jnp.where(images == image, label_ref[image], label)
    targets = (classes == label).astype(F32)
    softplus = jnp.maximum(logits, 0.0) + jnp.log1p(jnp.exp(-jnp.abs(logits)))
    terms = softplus - targets * logits
    for image in range(image_count):
        loss_ref[0, image] = jnp.sum(terms[image : image + 1, :]) * (1.0 / terms.shape[1])
    sigmoid = 1.0 / (1.0 + jnp.exp(-logits))
    grad_logits = ((sigmoid - targets) * (1.0 / image_count)).astype(BF16)
    grad_logits_ref[...] = grad_logits
    grad_pooled = norm_back(dot_nt(grad_logits, head), unit_rows, inverse, gain_row)
    grad_image = grad_pooled * (1.0 / patch_count)
    grad_image_ref[...] = grad_image
    per_image_ref[...] = dot_nt(grad_image.astype(BF16), out_weight_ref[...])


def grad_rows_kernel(rows_ref, select_ref, grad_image_ref, gain_ref, *refs):
    *terms, out_ref = refs
    unit_rows, inverse = norm_parts(rows_ref[...].astype(F32))
    grad = sum(term[...].astype(F32) for term in terms)
    total = norm_back(grad, unit_rows, inverse, gain_ref[...])
    select = select_ref[...]
    for image in range(grad_image_ref.shape[0]):
        total = total + select[:, image : image + 1] * grad_image_ref[image : image + 1, :]
    out_ref[...] = total.astype(BF16)


def on_device(
    block_inputs, qkv_weights, out_weights, norm_gain, query_key_gain, pool_gain, class_head, labels
):
    rows_in = block_inputs[0]
    qkv_local = qkv_weights[0]
    out_local = out_weights[0]
    gain_pair = query_key_gain[0]
    label_row = labels[0]
    local_count, model_width = rows_in.shape
    image_count = label_row.shape[0]
    class_count = class_head.shape[2]
    depth, width = lax.axis_size("dp"), lax.axis_size("tensor")
    group_size = depth * width
    row_count = local_count * group_size
    lane_count = qkv_local.shape[2]
    half = local_count // HALVES
    place = (local_count, depth, width)
    member = lax.axis_index(GROUP)
    image_ids = (member * local_count + lax.iota(jnp.int32, local_count)) // PATCHES
    own_select = (image_ids[:, None] == lax.iota(jnp.int32, image_count)[None, :]).astype(F32)

    def shape(dims, dtype=F32):
        return jax.ShapeDtypeStruct(dims, dtype)

    half_shape = shape((half, model_width), BF16)
    three = (3, row_count, lane_count)
    slab_rows = local_count * width
    heads = image_count * (lane_count // HS)
    product_flops = 2 * row_count * lane_count * PATCHES
    slab_flops = 2 * slab_rows * model_width * lane_count
    chunk = 2 * PATCHES if model_width % (2 * PATCHES) == 0 else PATCHES
    piece_shapes = [half_shape] * (width * HALVES)

    select_halves = [own_select[h * half : (h + 1) * half] for h in range(HALVES)]

    def project(_, pieces):
        return call(
            project_kernel,
            [shape((3, slab_rows, lane_count)), shape((model_width, slab_rows), BF16)],
            (*pieces, qkv_local),
            flops=3 * slab_flops,
            limit=12,
        )

    def state_of(projected):
        return call(
            functools.partial(state_kernel, *place),
            [
                shape((heads, PATCHES, PATCHES)),
                shape((heads, PATCHES, PATCHES), BF16),
                shape(three, BF16),
                shape((2, row_count, lane_count)),
                shape((2, row_count, lane_count // HS)),
            ],
            (*projected, gain_pair),
            scratch=[pltpu.VMEM(three, F32)],
            flops=2 * product_flops,
        )

    _, own_results = gather_slabs(
        [
            call(
                functools.partial(norm_rows_kernel, h * half),
                half_shape,
                (rows_in, norm_gain),
                limit=4,
            )
            for h in range(HALVES)
        ],
        project,
    )
    own_projected, own_turned = zip(*own_results)
    attention = call(
        functools.partial(attend_own_kernel, *place),
        shape((row_count, lane_count), BF16),
        (*own_projected, gain_pair),
        scratch=[pltpu.VMEM(three, F32), pltpu.VMEM(three[1:], BF16)],
        flops=2 * product_flops,
    )

    def branch(s):
        return call(
            functools.partial(branch_kernel, slab_starts(s, half, depth, width, OUT_WAYS)),
            piece_shapes,
            (attention, out_local),
            flops=slab_flops,
            limit=12,
        )

    out_halves = [
        call(
            functools.partial(out_rows_kernel, h * half),
            half_shape,
            (rows_in, *terms),
            limit=4,
        )
        for h, terms in enumerate(scatter_slabs(branch, OUT_WAYS))
    ]

    first = (lax.axis_index("section") == 0).astype(jnp.int32).reshape(1)
    margin_normed, margin_halves, row_sums = zip(
        *[
            call(
                functools.partial(norm_margin_kernel, h * half),
                [half_shape, half_shape, shape((image_count, model_width))],
                (first, rows_in, from_behind(out, "section", 1), select, norm_gain),
                specs=[SMEM_SPEC] + [VMEM_SPEC] * 4,
                limit=4,
            )
            for h, (out, select) in enumerate(zip(out_halves, select_halves))
        ]
    )
    _, margin_results = gather_slabs(margin_normed, project)
    margin_projected, margin_turned = zip(*margin_results)
    image_sums, pooled_part = call(
        functools.partial(attend_margin_kernel, *place),
        [shape((image_count, lane_count)), shape((image_count, model_width))],
        (*margin_projected, gain_pair, out_local, *row_sums),
        scratch=[pltpu.VMEM(three, F32)],
        flops=2 * product_flops,
    )
    margin_state = state_of(margin_projected)
    own_state = state_of(own_projected)
    out_own = call(join_kernel, shape((local_count, model_width), BF16), tuple(out_halves), limit=4)
    pooled = after(sum_group(pooled_part), margin_state[4])
    losses, pooled_half, grad_logits, grad_image, per_image = call(
        functools.partial(judge_kernel, PATCHES),
        [
            shape((1, image_count)),
            shape((image_count, model_width), BF16),
            shape((image_count, class_count), BF16),
            shape((image_count, model_width)),
            shape((image_count, lane_count)),
        ],
        (pooled, pool_gain, class_head[0], label_row, out_local),
        specs=[VMEM_SPEC] * 3 + [SMEM_SPEC, VMEM_SPEC],
        outs=[SMEM_SPEC] + [VMEM_SPEC] * 4,
        flops=4 * class_count * model_width * 8,
        limit=12,
    )
    grad_head = call(
        functools.partial(head_gradient_kernel, width),
        shape((model_width // group_size, class_count), BF16),
        (pooled_half, grad_logits),
        limit=4,
    )

    margin_gradient = call(
        functools.partial(attend_back_kernel, *place, True),
        shape((row_count, 3 * lane_count), BF16),
        (*margin_state, per_image, gain_pair),
        scratch=[pltpu.VMEM(three, F32)],
        flops=5 * product_flops,
    )

    def input_term(s):
        return call(
            functools.partial(input_kernel, slab_starts(s, half, depth, width, GRAD_WAYS)),
            piece_shapes,
            (margin_gradient, qkv_local),
            flops=3 * slab_flops,
            limit=12,
        )

    grad_normed = scatter_slabs(input_term, GRAD_WAYS)
    grad_inputs = [
        call(
            grad_rows_kernel,
            half_shape,
            (rows, select, grad_image, norm_gain, *terms),
            limit=6,
        )
        for terms, rows, select in zip(grad_normed, margin_halves, select_halves)
    ]
    returned = [from_behind(grad, "section", -1) for grad in grad_inputs]

    def cotangent(s, pieces):
        if s < 2:
            beside = (grad_head, out_own) if s == 0 else (own_state[4],)
            pieces = [after(pieces[0], *beside)] + pieces[1:]
        return call(
            cotangent_kernel,
            [shape((slab_rows, lane_count)), shape((slab_rows, model_width), BF16)],
            (*pieces, out_local),
            flops=slab_flops,
            limit=12,
        )

    _, cotangent_results = gather_slabs(returned, cotangent)
    grad_attention, cotangent_slabs = zip(*cotangent_results)
    own_gradient = call(
        functools.partial(attend_back_kernel, *place, False),
        shape((row_count, 3 * lane_count), BF16),
        (*own_state, *grad_attention, gain_pair),
        scratch=[pltpu.VMEM(three, F32), pltpu.VMEM(three[1:], F32)],
        flops=5 * product_flops,
    )
    turned = (*margin_turned, *own_turned)
    query_key_value_gradient = pl.pallas_call(
        functools.partial(weight_gradient_kernel, depth),
        grid=(model_width // chunk,),
        out_shape=shape((3, model_width, lane_count), BF16),
        in_specs=[pl.BlockSpec((chunk, slab_rows), lambda i: (i, 0))] * len(turned)
        + [pl.BlockSpec((row_count, 3 * lane_count), lambda i: (0, 0))] * 2,
        out_specs=pl.BlockSpec((3, chunk, lane_count), lambda i: (0, i, 0)),
        compiler_params=pltpu.CompilerParams(vmem_limit_bytes=60 * 2**20),
        cost_estimate=pl.CostEstimate(
            flops=6 * depth * slab_flops,
            bytes_accessed=6 * model_width * lane_count,
            transcendentals=0,
        ),
    )(*turned, margin_gradient, own_gradient)
    wide = 2 * chunk if model_width % (2 * chunk) == 0 else chunk
    grad_out = pl.pallas_call(
        out_gradient_kernel,
        grid=(model_width // wide,),
        out_shape=shape((lane_count, model_width), BF16),
        in_specs=[pl.BlockSpec((slab_rows, wide), lambda i: (0, i))] * depth
        + [
            pl.BlockSpec((row_count, lane_count), lambda i: (0, 0)),
            pl.BlockSpec((image_count, lane_count), lambda i: (0, 0)),
            pl.BlockSpec((image_count, wide), lambda i: (0, i)),
        ],
        out_specs=pl.BlockSpec((lane_count, wide), lambda i: (0, i)),
        scratch_shapes=[pltpu.VMEM((lane_count, row_count), BF16)],
        compiler_params=pltpu.CompilerParams(vmem_limit_bytes=GRAD_OUT_LIMIT * 2**20),
        cost_estimate=pl.CostEstimate(
            flops=depth * slab_flops,
            bytes_accessed=4 * model_width * lane_count,
            transcendentals=0,
        ),
    )(*cotangent_slabs, attention, image_sums, grad_image)
    return (
        out_own[None],
        query_key_value_gradient[None],
        grad_out[None],
        grad_head[None],
        losses,
    )


def solution(mesh):
    in_specs = (
        P("section", GROUP, None),
        P("section", None, None, GROUP),
        P("section", GROUP, None),
        P("section", None),
        P("section", None, None),
        P("section", None),
        P("section", None, None),
        P("section", None),
    )
    out_specs = (
        P("section", GROUP, None),
        P("section", None, None, GROUP),
        P("section", GROUP, None),
        P("section", GROUP, None),
        P("section", None),
    )
    return jax.shard_map(
        on_device, mesh=mesh, in_specs=in_specs, out_specs=out_specs, check_vma=False
    )
```

```python
import functools
import math

import jax
import jax.numpy as jnp
from jax import lax
from jax.experimental import pallas as pl
from jax.experimental.pallas import tpu as pltpu
from jax.sharding import PartitionSpec as P

HS = 128
PATCHES = 256
GROUP = ("dp", "tensor")
HALVES = 2
OUT_WAYS = (1, 1)
GRAD_WAYS = (1, 1)
GRAD_OUT_LIMIT = 24

epsilon = 1e-06
F32 = jnp.float32
BF16 = jnp.bfloat16
VMEM_SPEC = pl.BlockSpec(memory_space=pltpu.VMEM)
HBM_SPEC = pl.BlockSpec(memory_space=pltpu.HBM)
SMEM_SPEC = pl.BlockSpec(memory_space=pltpu.SMEM)


def from_behind(block, axis, distance):
    devices = range(lax.axis_size(axis))
    route = [(i - distance, i) for i in devices if i - distance in devices]
    return lax.ppermute(block, axis, route)


def shift(block, axis, distance):
    count = lax.axis_size(axis)
    return lax.ppermute(block, axis, [(i, (i + distance) % count) for i in range(count)])


def after(value, *others):
    return lax.optimization_barrier((value,) + others)[0]


def way(half):
    return 1


def gather_slabs(halves, work):
    depth, width = lax.axis_size("dp"), lax.axis_size("tensor")
    ring, slabs, results = [list(halves)], [], []
    across = [[None] * HALVES for _ in range(width)]
    for s in range(depth):
        if s:
            ring.append([shift(ring[-1][h], "dp", way(h)) for h in range(HALVES)])
        pieces = list(ring[s])
        for j in range(1, width):
            for h in range(HALVES):
                piece = ring[s][h]
                if s:
                    piece = after(piece, across[j][h], *[r[0] for r in results[: s - 1][-1:]])
                across[j][h] = shift(piece, "tensor", j)
                pieces.append(across[j][h])
        slabs.append(pieces)
        results.append(work(s, pieces))
    return slabs, results


def scatter_slabs(slab_pieces, ways):
    depth, width = lax.axis_size("dp"), lax.axis_size("tensor")
    running = [None] * HALVES
    last = [[None] * HALVES for _ in range(width)]
    for s in list(range(1, depth)) + [0]:
        terms = slab_pieces(s)
        for h in range(HALVES):
            parts = [terms[h]]
            for j in range(1, width):
                piece = terms[j * HALVES + h]
                if last[j][h] is not None:
                    piece = after(piece, last[j][h])
                last[j][h] = shift(piece, "tensor", -j)
                parts.append(last[j][h])
            if running[h] is not None:
                parts.append(shift(running[h], "dp", ways[h]))
            running[h] = parts if s == 0 else sum(part.astype(F32) for part in parts).astype(BF16)
    return running


def slab_starts(s, half, depth, width, ways):
    starts = []
    for j in range(width):
        for h in range(HALVES):
            slab = s if ways[h] == way(h) else (depth - s) % depth
            starts.append(((slab * width + j) * HALVES + h) * half)
    return tuple(starts)


def exchange(value, axis, steps):
    route = [(i, i ^ steps) for i in range(lax.axis_size(axis))]
    return lax.ppermute(value, axis, route)


def sum_group(value):
    counts = [lax.axis_size(axis) for axis in ("tensor", "dp")]
    if any(count & (count - 1) for count in counts):
        return lax.psum(value, GROUP)
    for axis, count in zip(("tensor", "dp"), counts):
        parts = [value] + [exchange(value, axis, step) for step in range(1, count)]
        while len(parts) > 1:
            parts = [parts[i] + parts[i + 1] for i in range(0, len(parts), 2)]
        value = parts[0]
    return value


def norm_parts(values):
    centered = values - jnp.mean(values, axis=-1, keepdims=True)
    inverse = lax.rsqrt(jnp.mean(centered * centered, axis=-1, keepdims=True) + epsilon)
    return centered * inverse, inverse


def norm_back(grad_normed, unit_rows, inverse, gain_row):
    scaled = grad_normed * gain_row
    return inverse * (
        scaled
        - jnp.mean(scaled, axis=-1, keepdims=True)
        - unit_rows * jnp.mean(scaled * unit_rows, axis=-1, keepdims=True)
    )


def dot_nt(left, right):
    return lax.dot_general(left, right, (((1,), (1,)), ((), ())), preferred_element_type=F32)


def dot_tn(left, right):
    return lax.dot_general(left, right, (((0,), (0,)), ((), ())), preferred_element_type=F32)


def dot(left, right):
    return jnp.dot(left, right, preferred_element_type=F32)


def call(
    kernel, out_shape, ins, specs=None, outs=None, scratch=(), flops=0, moved=1000000, limit=16
):
    many = isinstance(out_shape, (tuple, list))
    return pl.pallas_call(
        kernel,
        out_shape=out_shape,
        in_specs=specs or [VMEM_SPEC] * len(ins),
        out_specs=outs or ([VMEM_SPEC] * len(out_shape) if many else VMEM_SPEC),
        scratch_shapes=list(scratch),
        compiler_params=pltpu.CompilerParams(vmem_limit_bytes=limit * 2**20),
        cost_estimate=pl.CostEstimate(flops=flops, bytes_accessed=moved, transcendentals=0),
    )(*ins)


def piece_rows(local_count, depth, width):
    half = local_count // HALVES
    z, y = lax.axis_index("dp"), lax.axis_index("tensor")
    out = []
    for s in range(depth):
        for j in range(width):
            for h in range(HALVES):
                far_z = lax.rem(z + (depth - s if way(h) > 0 else s), depth)
                far_y = lax.rem(y + width - j, width)
                first = (far_z * width + far_y) * local_count + h * half
                out.append(
                    (((s * width + j) * HALVES + h) * half, pl.multiple_of(first, half), half)
                )
    return out


def to_section_order(slabs, held, pieces):
    rows = held.shape[-2] // len(slabs)
    for ring, first, count in pieces:
        s, r = divmod(ring, rows)
        if len(held.shape) == 3:
            held[:, pl.ds(first, count), :] = slabs[s][:, r : r + count, :].astype(held.dtype)
        else:
            held[pl.ds(first, count), :] = slabs[s][r : r + count, :].astype(held.dtype)


def to_ring_order(held, out, pieces):
    for ring, first, count in pieces:
        if len(held.shape) == 3:
            out[:, ring : ring + count, :] = held[:, pl.ds(first, count), :].astype(out.dtype)
        else:
            out[ring : ring + count, :] = held[pl.ds(first, count), :].astype(out.dtype)


def to_joined_order(held, out, pieces):
    lane_count = held.shape[2]
    for ring, first, count in pieces:
        for t in range(held.shape[0]):
            part = held[t, pl.ds(first, count), :].astype(out.dtype)
            out[ring : ring + count, t * lane_count : (t + 1) * lane_count] = part


def head_forward(held, gains, rows, lanes):
    query_unit, query_inverse = norm_parts(held[0, rows, lanes])
    key_unit, key_inverse = norm_parts(held[1, rows, lanes])
    query_half = (query_unit * gains[0:1, :]).astype(BF16)
    key_half = (key_unit * gains[1:2, :]).astype(BF16)
    value_half = held[2, rows, lanes].astype(BF16)
    exponent = jnp.exp(dot_nt(query_half, key_half) * (1.0 / math.sqrt(HS)))
    probs = exponent * (1.0 / jnp.sum(exponent, axis=-1, keepdims=True))
    return (
        probs,
        probs.astype(BF16),
        query_half,
        key_half,
        value_half,
        query_unit,
        query_inverse,
        key_unit,
        key_inverse,
    )


def each_head(held):
    row_count, lane_count = held.shape[-2:]
    for image in range(row_count // PATCHES):
        for head in range(lane_count // HS):
            yield (
                image,
                slice(image * PATCHES, (image + 1) * PATCHES),
                slice(head * HS, (head + 1) * HS),
            )


def attend_own_kernel(local_count, depth, width, *refs):
    slabs, gain_ref, out_ref, held, mixed = refs[:depth], *refs[depth:]
    pieces = piece_rows(local_count, depth, width)
    to_section_order(slabs, held, pieces)
    gains = gain_ref[...]
    for _, rows, lanes in each_head(held):
        state = head_forward(held, gains, rows, lanes)
        mixed[rows, lanes] = dot(state[1], state[4]).astype(BF16)
    to_ring_order(mixed, out_ref, pieces)


def attend_margin_kernel(local_count, depth, width, *refs):
    slabs = refs[:depth]
    gain_ref, out_weight_ref = refs[depth : depth + 2]
    row_sums = refs[depth + 2 : depth + 2 + HALVES]
    sums_ref, pooled_ref, held = refs[depth + 2 + HALVES :]
    pieces = piece_rows(local_count, depth, width)
    to_section_order(slabs, held, pieces)
    gains = gain_ref[...]
    for image, rows, lanes in each_head(held):
        state = head_forward(held, gains, rows, lanes)
        mixed = dot(state[1], state[4]).astype(BF16)
        sums_ref[image : image + 1, lanes] = jnp.sum(mixed.astype(F32), axis=0, keepdims=True)
    sums = sums_ref[...]
    count = sums.shape[0]
    high = sums.astype(BF16).astype(F32)
    middle = (sums - high).astype(BF16).astype(F32)
    low = sums - high - middle
    empty = jnp.zeros((-3 * count % 16, sums.shape[1]), F32)
    stacked = jnp.concatenate([high, middle, low, empty], axis=0).astype(BF16)
    product = dot(stacked, out_weight_ref[...])
    pooled_ref[...] = sum(ref[...] for ref in row_sums) + (
        product[:count] + (product[count : 2 * count] + product[2 * count : 3 * count])
    )


def state_kernel(local_count, depth, width, *refs):
    slabs = refs[:depth]
    gain_ref, probs_ref, turned_ref, halves_ref, units_ref, inverse_ref, held = refs[depth:]
    to_section_order(slabs, held, piece_rows(local_count, depth, width))
    gains = gain_ref[...]
    for place, (_, rows, lanes) in enumerate(each_head(held)):
        head = lanes.start // HS
        state = head_forward(held, gains, rows, lanes)
        probs_ref[place, :, :] = state[0]
        turned_ref[place, :, :] = state[1].T
        for t in range(3):
            halves_ref[t, rows, lanes] = state[2 + t]
        for t in range(2):
            units_ref[t, rows, lanes] = state[5 + 2 * t]
            inverse_ref[t, rows, head : head + 1] = state[6 + 2 * t]


def attend_back_kernel(local_count, depth, width, broadcast, *refs):
    probs_ref, turned_ref, halves_ref, units_ref, inverse_ref = refs[:5]
    grads = refs[5 : 6 if broadcast else 5 + depth]
    gain_ref, out_ref, held, *grad_held = refs[5 + len(grads) :]
    pieces = piece_rows(local_count, depth, width)
    if not broadcast:
        to_section_order(grads, grad_held[0], pieces)
    gains = gain_ref[...]
    for place, (image, rows, lanes) in enumerate(each_head(held)):
        head = lanes.start // HS
        if broadcast:
            row = grads[0][image : image + 1, lanes].astype(BF16).astype(F32)
            grad_mixed = jnp.broadcast_to(row, (PATCHES, HS)).astype(BF16)
        else:
            grad_mixed = grad_held[0][rows, lanes].astype(BF16)
        probs = probs_ref[place]
        grad_probs = dot_nt(grad_mixed, halves_ref[2, rows, lanes])
        weighted = probs * grad_probs
        grad_scores = weighted - probs * jnp.sum(weighted, axis=-1, keepdims=True)
        score_half = (grad_scores * (1.0 / math.sqrt(HS))).astype(BF16)
        grads_out = (
            dot(score_half, halves_ref[1, rows, lanes]),
            dot_tn(score_half, halves_ref[0, rows, lanes]),
        )
        for t in range(2):
            held[t, rows, lanes] = norm_back(
                grads_out[t],
                units_ref[t, rows, lanes],
                inverse_ref[t, rows, head : head + 1],
                gains[t : t + 1, :],
            )
        held[2, rows, lanes] = dot(turned_ref[place], grad_mixed)
    to_joined_order(held, out_ref, pieces)


def project_kernel(*refs):
    *pieces, weights_ref, projected_ref, turned_ref = refs
    rows = jnp.concatenate([ref[...] for ref in pieces], axis=0)
    for t in range(weights_ref.shape[0]):
        projected_ref[t, :, :] = dot(rows, weights_ref[t])
    turned_ref[...] = rows.T


def cotangent_kernel(*refs):
    *pieces, weights_ref, out_ref, slab_ref = refs
    rows = jnp.concatenate([ref[...] for ref in pieces], axis=0)
    out_ref[...] = dot_nt(rows, weights_ref[...])
    slab_ref[...] = rows


def to_pieces(total, outs):
    count = outs[0].shape[0]
    for i, out in enumerate(outs):
        out[...] = total[i * count : (i + 1) * count].astype(BF16)


def branch_kernel(starts, attention_ref, weights_ref, *outs):
    half = outs[0].shape[0]
    rows = jnp.concatenate([attention_ref[i : i + half, :] for i in starts], axis=0)
    to_pieces(dot(rows, weights_ref[...]), outs)


def input_kernel(starts, gradient_ref, weights_ref, *outs):
    half = outs[0].shape[0]
    projections, _, lane_count = weights_ref.shape
    total = None
    for t in range(projections):
        lanes = slice(t * lane_count, (t + 1) * lane_count)
        part = jnp.concatenate([gradient_ref[i : i + half, lanes] for i in starts], axis=0)
        part = dot_nt(part, weights_ref[t])
        total = part if total is None else total + part
    to_pieces(total, outs)


def weight_gradient_kernel(depth, *refs):
    *slabs, margin_ref, own_ref, out_ref = refs
    lane_count = out_ref.shape[2]
    total = None
    for blocks, gradient_ref in ((slabs[:depth], margin_ref), (slabs[depth:], own_ref)):
        turned = jnp.concatenate([block[...] for block in blocks], axis=1)
        part = dot(turned, gradient_ref[...])
        total = part if total is None else total + part
    for t in range(out_ref.shape[0]):
        out_ref[t, :, :] = total[:, t * lane_count : (t + 1) * lane_count].astype(BF16)


def out_gradient_kernel(*refs):
    *slabs, attention_ref, sums_ref, grad_image_ref, out_ref, turned = refs

    @pl.when(pl.program_id(0) == 0)
    def _():
        turned[...] = attention_ref[...].T

    total = dot(turned[...], jnp.concatenate([block[...] for block in slabs], axis=0))
    sums = sums_ref[...]
    image_count, lane_count = sums.shape
    sums = jnp.concatenate([sums, jnp.zeros((-image_count % 8, lane_count), F32)], axis=0).T
    grad_image = grad_image_ref[...].astype(BF16).astype(F32)
    for image in range(image_count):
        total = total + sums[:, image : image + 1] * grad_image[image : image + 1, :]
    out_ref[...] = total.astype(BF16)


def head_gradient_kernel(width, pooled_half_ref, grad_logits_ref, out_ref):
    member = lax.axis_index("dp") * width + lax.axis_index("tensor")
    count = out_ref.shape[0]
    start = pl.multiple_of(member * count, HS)
    pooled = pooled_half_ref[:, pl.ds(start, count)].astype(F32)
    grad_logits = grad_logits_ref[...].astype(F32)

    def padded(rows):
        empty = jnp.zeros((-rows.shape[0] % 16, rows.shape[1]), F32)
        return jnp.concatenate([rows, empty], axis=0).astype(BF16)

    out_ref[...] = dot_tn(padded(pooled), padded(grad_logits)).astype(BF16)


def join_kernel(*refs):
    refs[-1][...] = jnp.concatenate([ref[...] for ref in refs[:-1]], axis=0)


def norm_rows_kernel(first, rows_ref, gain_ref, out_ref):
    rows = rows_ref[first : first + out_ref.shape[0], :].astype(F32)
    unit_rows, _ = norm_parts(rows)
    out_ref[...] = (unit_rows * gain_ref[...]).astype(BF16)


def norm_margin_kernel(
    first, flag_ref, rows_ref, received_ref, select_ref, gain_ref, out_ref, margin_ref, sums_ref
):
    own = rows_ref[first : first + out_ref.shape[0], :]
    margin = jnp.where(flag_ref[0] == 1, own.astype(F32), received_ref[...].astype(F32))
    margin_ref[...] = margin.astype(BF16)
    unit_rows, _ = norm_parts(margin)
    out_ref[...] = (unit_rows * gain_ref[...]).astype(BF16)
    select = select_ref[...]
    for image in range(select.shape[1]):
        sums_ref[image : image + 1, :] = jnp.sum(
            margin * select[:, image : image + 1], axis=0, keepdims=True
        )


def out_rows_kernel(first, rows_ref, *refs):
    *terms, out_ref = refs
    total = sum(term[...].astype(F32) for term in terms)
    rows = rows_ref[first : first + out_ref.shape[0], :].astype(F32)
    out_ref[...] = (rows + total).astype(BF16)


def judge_kernel(
    patch_count,
    pooled_ref,
    gain_ref,
    head_ref,
    label_ref,
    out_weight_ref,
    loss_ref,
    pooled_half_ref,
    grad_logits_ref,
    grad_image_ref,
    per_image_ref,
):
    image_count = pooled_ref.shape[0]
    unit_rows, inverse = norm_parts(pooled_ref[...] * (1.0 / patch_count))
    gain_row = gain_ref[...]
    pooled_half = (unit_rows * gain_row).astype(BF16)
    pooled_half_ref[...] = pooled_half
    head = head_ref[...]
    logits = dot(pooled_half, head)
    classes = lax.broadcasted_iota(jnp.int32, logits.shape, 1)
    images = lax.broadcasted_iota(jnp.int32, logits.shape, 0)
    label = jnp.zeros_like(classes)
    for image in range(image_count):
        label = jnp.where(images == image, label_ref[image], label)
    targets = (classes == label).astype(F32)
    softplus = jnp.maximum(logits, 0.0) + jnp.log1p(jnp.exp(-jnp.abs(logits)))
    terms = softplus - targets * logits
    for image in range(image_count):
        loss_ref[0, image] = jnp.sum(terms[image : image + 1, :]) * (1.0 / terms.shape[1])
    sigmoid = 1.0 / (1.0 + jnp.exp(-logits))
    grad_logits = ((sigmoid - targets) * (1.0 / image_count)).astype(BF16)
    grad_logits_ref[...] = grad_logits
    grad_pooled = norm_back(dot_nt(grad_logits, head), unit_rows, inverse, gain_row)
    grad_image = grad_pooled * (1.0 / patch_count)
    grad_image_ref[...] = grad_image
    per_image_ref[...] = dot_nt(grad_image.astype(BF16), out_weight_ref[...])


def grad_rows_kernel(rows_ref, select_ref, grad_image_ref, gain_ref, *refs):
    *terms, out_ref = refs
    unit_rows, inverse = norm_parts(rows_ref[...].astype(F32))
    grad = sum(term[...].astype(F32) for term in terms)
    total = norm_back(grad, unit_rows, inverse, gain_ref[...])
    select = select_ref[...]
    for image in range(grad_image_ref.shape[0]):
        total = total + select[:, image : image + 1] * grad_image_ref[image : image + 1, :]
    out_ref[...] = total.astype(BF16)


def on_device(
    block_inputs, qkv_weights, out_weights, norm_gain, query_key_gain, pool_gain, class_head, labels
):
    rows_in = block_inputs[0]
    qkv_local = qkv_weights[0]
    out_local = out_weights[0]
    gain_pair = query_key_gain[0]
    label_row = labels[0]
    local_count, model_width = rows_in.shape
    image_count = label_row.shape[0]
    class_count = class_head.shape[2]
    depth, width = lax.axis_size("dp"), lax.axis_size("tensor")
    group_size = depth * width
    row_count = local_count * group_size
    lane_count = qkv_local.shape[2]
    half = local_count // HALVES
    place = (local_count, depth, width)
    member = lax.axis_index(GROUP)
    image_ids = (member * local_count + lax.iota(jnp.int32, local_count)) // PATCHES
    own_select = (image_ids[:, None] == lax.iota(jnp.int32, image_count)[None, :]).astype(F32)

    def shape(dims, dtype=F32):
        return jax.ShapeDtypeStruct(dims, dtype)

    half_shape = shape((half, model_width), BF16)
    three = (3, row_count, lane_count)
    slab_rows = local_count * width
    heads = image_count * (lane_count // HS)
    product_flops = 2 * row_count * lane_count * PATCHES
    slab_flops = 2 * slab_rows * model_width * lane_count
    chunk = 2 * PATCHES if model_width % (2 * PATCHES) == 0 else PATCHES
    piece_shapes = [half_shape] * (width * HALVES)

    select_halves = [own_select[h * half : (h + 1) * half] for h in range(HALVES)]

    def project(_, pieces):
        return call(
            project_kernel,
            [shape((3, slab_rows, lane_count)), shape((model_width, slab_rows), BF16)],
            (*pieces, qkv_local),
            flops=3 * slab_flops,
            limit=12,
        )

    def state_of(projected):
        return call(
            functools.partial(state_kernel, *place),
            [
                shape((heads, PATCHES, PATCHES)),
                shape((heads, PATCHES, PATCHES), BF16),
                shape(three, BF16),
                shape((2, row_count, lane_count)),
                shape((2, row_count, lane_count // HS)),
            ],
            (*projected, gain_pair),
            scratch=[pltpu.VMEM(three, F32)],
            flops=2 * product_flops,
        )

    _, own_results = gather_slabs(
        [
            call(
                functools.partial(norm_rows_kernel, h * half),
                half_shape,
                (rows_in, norm_gain),
                limit=4,
            )
            for h in range(HALVES)
        ],
        project,
    )
    own_projected, own_turned = zip(*own_results)
    attention = call(
        functools.partial(attend_own_kernel, *place),
        shape((row_count, lane_count), BF16),
        (*own_projected, gain_pair),
        scratch=[pltpu.VMEM(three, F32), pltpu.VMEM(three[1:], BF16)],
        flops=2 * product_flops,
    )

    def branch(s):
        return call(
            functools.partial(branch_kernel, slab_starts(s, half, depth, width, OUT_WAYS)),
            piece_shapes,
            (attention, out_local),
            flops=slab_flops,
            limit=12,
        )

    out_halves = [
        call(
            functools.partial(out_rows_kernel, h * half),
            half_shape,
            (rows_in, *terms),
            limit=4,
        )
        for h, terms in enumerate(scatter_slabs(branch, OUT_WAYS))
    ]

    first = (lax.axis_index("section") == 0).astype(jnp.int32).reshape(1)
    margin_normed, margin_halves, row_sums = zip(
        *[
            call(
                functools.partial(norm_margin_kernel, h * half),
                [half_shape, half_shape, shape((image_count, model_width))],
                (first, rows_in, from_behind(out, "section", 1), select, norm_gain),
                specs=[SMEM_SPEC] + [VMEM_SPEC] * 4,
                limit=4,
            )
            for h, (out, select) in enumerate(zip(out_halves, select_halves))
        ]
    )
    _, margin_results = gather_slabs(margin_normed, project)
    margin_projected, margin_turned = zip(*margin_results)
    image_sums, pooled_part = call(
        functools.partial(attend_margin_kernel, *place),
        [shape((image_count, lane_count)), shape((image_count, model_width))],
        (*margin_projected, gain_pair, out_local, *row_sums),
        scratch=[pltpu.VMEM(three, F32)],
        flops=2 * product_flops,
    )
    margin_state = state_of(margin_projected)
    own_state = state_of(own_projected)
    out_own = call(join_kernel, shape((local_count, model_width), BF16), tuple(out_halves), limit=4)
    pooled = after(sum_group(pooled_part), margin_state[4])
    losses, pooled_half, grad_logits, grad_image, per_image = call(
        functools.partial(judge_kernel, PATCHES),
        [
            shape((1, image_count)),
            shape((image_count, model_width), BF16),
            shape((image_count, class_count), BF16),
            shape((image_count, model_width)),
            shape((image_count, lane_count)),
        ],
        (pooled, pool_gain, class_head[0], label_row, out_local),
        specs=[VMEM_SPEC] * 3 + [SMEM_SPEC, VMEM_SPEC],
        outs=[SMEM_SPEC] + [VMEM_SPEC] * 4,
        flops=4 * class_count * model_width * 8,
        limit=12,
    )
    grad_head = call(
        functools.partial(head_gradient_kernel, width),
        shape((model_width // group_size, class_count), BF16),
        (pooled_half, grad_logits),
        limit=4,
    )

    margin_gradient = call(
        functools.partial(attend_back_kernel, *place, True),
        shape((row_count, 3 * lane_count), BF16),
        (*margin_state, per_image, gain_pair),
        scratch=[pltpu.VMEM(three, F32)],
        flops=5 * product_flops,
    )

    def input_term(s):
        return call(
            functools.partial(input_kernel, slab_starts(s, half, depth, width, GRAD_WAYS)),
            piece_shapes,
            (margin_gradient, qkv_local),
            flops=3 * slab_flops,
            limit=12,
        )

    grad_normed = scatter_slabs(input_term, GRAD_WAYS)
    grad_inputs = [
        call(
            grad_rows_kernel,
            half_shape,
            (rows, select, grad_image, norm_gain, *terms),
            limit=6,
        )
        for terms, rows, select in zip(grad_normed, margin_halves, select_halves)
    ]
    returned = [from_behind(grad, "section", -1) for grad in grad_inputs]

    def cotangent(s, pieces):
        if s < 2:
            beside = (grad_head, out_own) if s == 0 else (own_state[4],)
            pieces = [after(pieces[0], *beside)] + pieces[1:]
        return call(
            cotangent_kernel,
            [shape((slab_rows, lane_count)), shape((slab_rows, model_width), BF16)],
            (*pieces, out_local),
            flops=slab_flops,
            limit=12,
        )

    _, cotangent_results = gather_slabs(returned, cotangent)
    grad_attention, cotangent_slabs = zip(*cotangent_results)
    own_gradient = call(
        functools.partial(attend_back_kernel, *place, False),
        shape((row_count, 3 * lane_count), BF16),
        (*own_state, *grad_attention, gain_pair),
        scratch=[pltpu.VMEM(three, F32), pltpu.VMEM(three[1:], F32)],
        flops=5 * product_flops,
    )
    wide = 2 * chunk if model_width % (2 * chunk) == 0 else chunk
    turned = (*margin_turned, *own_turned)
    query_key_value_gradient = pl.pallas_call(
        functools.partial(weight_gradient_kernel, depth),
        grid=(model_width // wide,),
        out_shape=shape((3, model_width, lane_count), BF16),
        in_specs=[pl.BlockSpec((wide, slab_rows), lambda i: (i, 0))] * len(turned)
        + [pl.BlockSpec((row_count, 3 * lane_count), lambda i: (0, 0))] * 2,
        out_specs=pl.BlockSpec((3, wide, lane_count), lambda i: (0, i, 0)),
        compiler_params=pltpu.CompilerParams(vmem_limit_bytes=36 * 2**20),
        cost_estimate=pl.CostEstimate(
            flops=6 * depth * slab_flops,
            bytes_accessed=6 * model_width * lane_count,
            transcendentals=0,
        ),
    )(*turned, margin_gradient, own_gradient)
    grad_out = pl.pallas_call(
        out_gradient_kernel,
        grid=(model_width // wide,),
        out_shape=shape((lane_count, model_width), BF16),
        in_specs=[pl.BlockSpec((slab_rows, wide), lambda i: (0, i))] * depth
        + [
            pl.BlockSpec((row_count, lane_count), lambda i: (0, 0)),
            pl.BlockSpec((image_count, lane_count), lambda i: (0, 0)),
            pl.BlockSpec((image_count, wide), lambda i: (0, i)),
        ],
        out_specs=pl.BlockSpec((lane_count, wide), lambda i: (0, i)),
        scratch_shapes=[pltpu.VMEM((lane_count, row_count), BF16)],
        compiler_params=pltpu.CompilerParams(vmem_limit_bytes=GRAD_OUT_LIMIT * 2**20),
        cost_estimate=pl.CostEstimate(
            flops=depth * slab_flops,
            bytes_accessed=4 * model_width * lane_count,
            transcendentals=0,
        ),
    )(*cotangent_slabs, attention, image_sums, grad_image)
    return (
        out_own[None],
        query_key_value_gradient[None],
        grad_out[None],
        grad_head[None],
        losses,
    )


def solution(mesh):
    in_specs = (
        P("section", GROUP, None),
        P("section", None, None, GROUP),
        P("section", GROUP, None),
        P("section", None),
        P("section", None, None),
        P("section", None),
        P("section", None, None),
        P("section", None),
    )
    out_specs = (
        P("section", GROUP, None),
        P("section", None, None, GROUP),
        P("section", GROUP, None),
        P("section", GROUP, None),
        P("section", None),
    )
    return jax.shard_map(
        on_device, mesh=mesh, in_specs=in_specs, out_specs=out_specs, check_vma=False
    )
```

```python
import functools
import math

import jax
import jax.numpy as jnp
from jax import lax
from jax.experimental import pallas as pl
from jax.experimental.pallas import tpu as pltpu
from jax.sharding import PartitionSpec as P

HS = 128
PATCHES = 256
GROUP = ("dp", "tensor")
HALVES = 2
OUT_WAYS = (1, 1)
GRAD_WAYS = (1, 1)
GRAD_OUT_LIMIT = 16

epsilon = 1e-06
F32 = jnp.float32
BF16 = jnp.bfloat16
VMEM_SPEC = pl.BlockSpec(memory_space=pltpu.VMEM)
HBM_SPEC = pl.BlockSpec(memory_space=pltpu.HBM)
SMEM_SPEC = pl.BlockSpec(memory_space=pltpu.SMEM)


def from_behind(block, axis, distance):
    devices = range(lax.axis_size(axis))
    route = [(i - distance, i) for i in devices if i - distance in devices]
    return lax.ppermute(block, axis, route)


def shift(block, axis, distance):
    count = lax.axis_size(axis)
    return lax.ppermute(block, axis, [(i, (i + distance) % count) for i in range(count)])


def after(value, *others):
    return lax.optimization_barrier((value,) + others)[0]


def way(half):
    return 1


def gather_slabs(halves, work):
    depth, width = lax.axis_size("dp"), lax.axis_size("tensor")
    ring, slabs, results = [list(halves)], [], []
    across = [[None] * HALVES for _ in range(width)]
    for s in range(depth):
        if s + 1 < depth:
            ring.append([shift(ring[-1][h], "dp", way(h)) for h in range(HALVES)])
        pieces = list(ring[s])
        for j in range(1, width):
            for h in range(HALVES):
                piece = ring[s][h]
                if s:
                    piece = after(piece, across[j][h], *[r[0] for r in results[: s - 1][-1:]])
                across[j][h] = shift(piece, "tensor", j)
                pieces.append(across[j][h])
        slabs.append(pieces)
        results.append(work(s, pieces))
    return slabs, results


def scatter_slabs(slab_pieces, ways):
    depth, width = lax.axis_size("dp"), lax.axis_size("tensor")
    running = [None] * HALVES
    last = [[None] * HALVES for _ in range(width)]
    for s in list(range(1, depth)) + [0]:
        terms = slab_pieces(s)
        for h in range(HALVES):
            parts = [terms[h]]
            for j in range(1, width):
                piece = terms[j * HALVES + h]
                if last[j][h] is not None:
                    piece = after(piece, last[j][h])
                last[j][h] = shift(piece, "tensor", -j)
                parts.append(last[j][h])
            if running[h] is not None:
                parts.append(shift(running[h], "dp", ways[h]))
            running[h] = parts if s == 0 else sum(part.astype(F32) for part in parts).astype(BF16)
    return running


def slab_starts(s, half, depth, width, ways):
    starts = []
    for j in range(width):
        for h in range(HALVES):
            slab = s if ways[h] == way(h) else (depth - s) % depth
            starts.append(((slab * width + j) * HALVES + h) * half)
    return tuple(starts)


def exchange(value, axis, steps):
    route = [(i, i ^ steps) for i in range(lax.axis_size(axis))]
    return lax.ppermute(value, axis, route)


def sum_group(value):
    counts = [lax.axis_size(axis) for axis in ("tensor", "dp")]
    if any(count & (count - 1) for count in counts):
        return lax.psum(value, GROUP)
    for axis, count in zip(("tensor", "dp"), counts):
        parts = [value] + [exchange(value, axis, step) for step in range(1, count)]
        while len(parts) > 1:
            parts = [parts[i] + parts[i + 1] for i in range(0, len(parts), 2)]
        value = parts[0]
    return value


def norm_parts(values):
    centered = values - jnp.mean(values, axis=-1, keepdims=True)
    inverse = lax.rsqrt(jnp.mean(centered * centered, axis=-1, keepdims=True) + epsilon)
    return centered * inverse, inverse


def norm_back(grad_normed, unit_rows, inverse, gain_row):
    scaled = grad_normed * gain_row
    return inverse * (
        scaled
        - jnp.mean(scaled, axis=-1, keepdims=True)
        - unit_rows * jnp.mean(scaled * unit_rows, axis=-1, keepdims=True)
    )


def dot_nt(left, right):
    return lax.dot_general(left, right, (((1,), (1,)), ((), ())), preferred_element_type=F32)


def dot_tn(left, right):
    return lax.dot_general(left, right, (((0,), (0,)), ((), ())), preferred_element_type=F32)


def dot(left, right):
    return jnp.dot(left, right, preferred_element_type=F32)


def call(
    kernel, out_shape, ins, specs=None, outs=None, scratch=(), flops=0, moved=1000000, limit=13
):
    many = isinstance(out_shape, (tuple, list))
    return pl.pallas_call(
        kernel,
        out_shape=out_shape,
        in_specs=specs or [VMEM_SPEC] * len(ins),
        out_specs=outs or ([VMEM_SPEC] * len(out_shape) if many else VMEM_SPEC),
        scratch_shapes=list(scratch),
        compiler_params=pltpu.CompilerParams(vmem_limit_bytes=limit * 2**20),
        cost_estimate=pl.CostEstimate(flops=flops, bytes_accessed=moved, transcendentals=0),
    )(*ins)


def piece_rows(local_count, depth, width):
    half = local_count // HALVES
    z, y = lax.axis_index("dp"), lax.axis_index("tensor")
    out = []
    for s in range(depth):
        for j in range(width):
            for h in range(HALVES):
                far_z = lax.rem(z + (depth - s if way(h) > 0 else s), depth)
                far_y = lax.rem(y + width - j, width)
                first = (far_z * width + far_y) * local_count + h * half
                out.append(
                    (((s * width + j) * HALVES + h) * half, pl.multiple_of(first, half), half)
                )
    return out


def to_section_order(slabs, held, pieces):
    rows = held.shape[-2] // len(slabs)
    for ring, first, count in pieces:
        s, r = divmod(ring, rows)
        if len(held.shape) == 3:
            held[:, pl.ds(first, count), :] = slabs[s][:, r : r + count, :].astype(held.dtype)
        else:
            held[pl.ds(first, count), :] = slabs[s][r : r + count, :].astype(held.dtype)


def to_ring_order(held, out, pieces):
    for ring, first, count in pieces:
        if len(held.shape) == 3:
            out[:, ring : ring + count, :] = held[:, pl.ds(first, count), :].astype(out.dtype)
        else:
            out[ring : ring + count, :] = held[pl.ds(first, count), :].astype(out.dtype)


def to_joined_order(held, out, pieces):
    lane_count = held.shape[2]
    for ring, first, count in pieces:
        for t in range(held.shape[0]):
            part = held[t, pl.ds(first, count), :].astype(out.dtype)
            out[ring : ring + count, t * lane_count : (t + 1) * lane_count] = part


def head_forward(held, gains, rows, lanes):
    query_unit, query_inverse = norm_parts(held[0, rows, lanes])
    key_unit, key_inverse = norm_parts(held[1, rows, lanes])
    query_half = (query_unit * gains[0:1, :]).astype(BF16)
    key_half = (key_unit * gains[1:2, :]).astype(BF16)
    value_half = held[2, rows, lanes].astype(BF16)
    exponent = jnp.exp(dot_nt(query_half, key_half) * (1.0 / math.sqrt(HS)))
    probs = exponent * (1.0 / jnp.sum(exponent, axis=-1, keepdims=True))
    return (
        probs,
        probs.astype(BF16),
        query_half,
        key_half,
        value_half,
        query_unit,
        query_inverse,
        key_unit,
        key_inverse,
    )


def each_head(held):
    row_count, lane_count = held.shape[-2:]
    for image in range(row_count // PATCHES):
        for head in range(lane_count // HS):
            yield (
                image,
                slice(image * PATCHES, (image + 1) * PATCHES),
                slice(head * HS, (head + 1) * HS),
            )


def attend_own_kernel(local_count, depth, width, *refs):
    slabs, gain_ref, out_ref, held, mixed = refs[:depth], *refs[depth:]
    pieces = piece_rows(local_count, depth, width)
    to_section_order(slabs, held, pieces)
    gains = gain_ref[...]
    for _, rows, lanes in each_head(held):
        state = head_forward(held, gains, rows, lanes)
        mixed[rows, lanes] = dot(state[1], state[4]).astype(BF16)
    to_ring_order(mixed, out_ref, pieces)


def attend_margin_kernel(local_count, depth, width, *refs):
    slabs = refs[:depth]
    gain_ref, out_weight_ref = refs[depth : depth + 2]
    row_sums = refs[depth + 2 : depth + 2 + HALVES]
    sums_ref, pooled_ref, held = refs[depth + 2 + HALVES :]
    pieces = piece_rows(local_count, depth, width)
    to_section_order(slabs, held, pieces)
    gains = gain_ref[...]
    for image, rows, lanes in each_head(held):
        state = head_forward(held, gains, rows, lanes)
        mixed = dot(state[1], state[4]).astype(BF16)
        sums_ref[image : image + 1, lanes] = jnp.sum(mixed.astype(F32), axis=0, keepdims=True)
    sums = sums_ref[...]
    count = sums.shape[0]
    high = sums.astype(BF16).astype(F32)
    middle = (sums - high).astype(BF16).astype(F32)
    low = sums - high - middle
    empty = jnp.zeros((-3 * count % 16, sums.shape[1]), F32)
    stacked = jnp.concatenate([high, middle, low, empty], axis=0).astype(BF16)
    product = dot(stacked, out_weight_ref[...])
    pooled_ref[...] = sum(ref[...] for ref in row_sums) + (
        product[:count] + (product[count : 2 * count] + product[2 * count : 3 * count])
    )


def state_kernel(local_count, depth, width, *refs):
    slabs = refs[:depth]
    gain_ref, probs_ref, turned_ref, halves_ref, units_ref, inverse_ref, held = refs[depth:]
    to_section_order(slabs, held, piece_rows(local_count, depth, width))
    gains = gain_ref[...]
    for place, (_, rows, lanes) in enumerate(each_head(held)):
        head = lanes.start // HS
        state = head_forward(held, gains, rows, lanes)
        probs_ref[place, :, :] = state[0]
        turned_ref[place, :, :] = state[1].T
        for t in range(3):
            halves_ref[t, rows, lanes] = state[2 + t]
        for t in range(2):
            units_ref[t, rows, lanes] = state[5 + 2 * t]
            inverse_ref[t, rows, head : head + 1] = state[6 + 2 * t]


def attend_back_kernel(local_count, depth, width, broadcast, *refs):
    probs_ref, turned_ref, halves_ref, units_ref, inverse_ref = refs[:5]
    grads = refs[5 : 6 if broadcast else 5 + depth]
    gain_ref, out_ref, held, *grad_held = refs[5 + len(grads) :]
    pieces = piece_rows(local_count, depth, width)
    if not broadcast:
        to_section_order(grads, grad_held[0], pieces)
    gains = gain_ref[...]
    for place, (image, rows, lanes) in enumerate(each_head(held)):
        head = lanes.start // HS
        if broadcast:
            row = grads[0][image : image + 1, lanes].astype(BF16).astype(F32)
            grad_mixed = jnp.broadcast_to(row, (PATCHES, HS)).astype(BF16)
        else:
            grad_mixed = grad_held[0][rows, lanes].astype(BF16)
        probs = probs_ref[place]
        grad_probs = dot_nt(grad_mixed, halves_ref[2, rows, lanes])
        weighted = probs * grad_probs
        grad_scores = weighted - probs * jnp.sum(weighted, axis=-1, keepdims=True)
        score_half = (grad_scores * (1.0 / math.sqrt(HS))).astype(BF16)
        grads_out = (
            dot(score_half, halves_ref[1, rows, lanes]),
            dot_tn(score_half, halves_ref[0, rows, lanes]),
        )
        for t in range(2):
            held[t, rows, lanes] = norm_back(
                grads_out[t],
                units_ref[t, rows, lanes],
                inverse_ref[t, rows, head : head + 1],
                gains[t : t + 1, :],
            )
        held[2, rows, lanes] = dot(turned_ref[place], grad_mixed)
    to_joined_order(held, out_ref, pieces)


def project_kernel(*refs):
    *pieces, weights_ref, projected_ref, turned_ref = refs
    rows = jnp.concatenate([ref[...] for ref in pieces], axis=0)
    for t in range(weights_ref.shape[0]):
        projected_ref[t, :, :] = dot(rows, weights_ref[t])
    turned_ref[...] = rows.T


def cotangent_kernel(*refs):
    *pieces, weights_ref, out_ref, slab_ref = refs
    rows = jnp.concatenate([ref[...] for ref in pieces], axis=0)
    out_ref[...] = dot_nt(rows, weights_ref[...])
    slab_ref[...] = rows


def to_pieces(total, outs):
    count = outs[0].shape[0]
    for i, out in enumerate(outs):
        out[...] = total[i * count : (i + 1) * count].astype(BF16)


def branch_kernel(starts, attention_ref, weights_ref, *outs):
    half = outs[0].shape[0]
    rows = jnp.concatenate([attention_ref[i : i + half, :] for i in starts], axis=0)
    to_pieces(dot(rows, weights_ref[...]), outs)


def input_kernel(starts, gradient_ref, weights_ref, *outs):
    half = outs[0].shape[0]
    projections, _, lane_count = weights_ref.shape
    total = None
    for t in range(projections):
        lanes = slice(t * lane_count, (t + 1) * lane_count)
        part = jnp.concatenate([gradient_ref[i : i + half, lanes] for i in starts], axis=0)
        part = dot_nt(part, weights_ref[t])
        total = part if total is None else total + part
    to_pieces(total, outs)


def weight_gradient_kernel(depth, *refs):
    *slabs, margin_ref, own_ref, out_ref = refs
    lane_count = out_ref.shape[2]
    total = None
    for blocks, gradient_ref in ((slabs[:depth], margin_ref), (slabs[depth:], own_ref)):
        turned = jnp.concatenate([block[...] for block in blocks], axis=1)
        part = dot(turned, gradient_ref[...])
        total = part if total is None else total + part
    for t in range(out_ref.shape[0]):
        out_ref[t, :, :] = total[:, t * lane_count : (t + 1) * lane_count].astype(BF16)


def out_gradient_kernel(*refs):
    *slabs, attention_ref, sums_ref, grad_image_ref, out_ref, turned = refs

    @pl.when(pl.program_id(0) == 0)
    def _():
        turned[...] = attention_ref[...].T

    total = dot(turned[...], jnp.concatenate([block[...] for block in slabs], axis=0))
    sums = sums_ref[...]
    image_count, lane_count = sums.shape
    sums = jnp.concatenate([sums, jnp.zeros((-image_count % 8, lane_count), F32)], axis=0).T
    grad_image = grad_image_ref[...].astype(BF16).astype(F32)
    for image in range(image_count):
        total = total + sums[:, image : image + 1] * grad_image[image : image + 1, :]
    out_ref[...] = total.astype(BF16)


def head_gradient_kernel(width, pooled_half_ref, grad_logits_ref, out_ref):
    member = lax.axis_index("dp") * width + lax.axis_index("tensor")
    count = out_ref.shape[0]
    start = pl.multiple_of(member * count, HS)
    pooled = pooled_half_ref[:, pl.ds(start, count)].astype(F32)
    grad_logits = grad_logits_ref[...].astype(F32)

    def padded(rows):
        empty = jnp.zeros((-rows.shape[0] % 16, rows.shape[1]), F32)
        return jnp.concatenate([rows, empty], axis=0).astype(BF16)

    out_ref[...] = dot_tn(padded(pooled), padded(grad_logits)).astype(BF16)


def join_kernel(*refs):
    refs[-1][...] = jnp.concatenate([ref[...] for ref in refs[:-1]], axis=0)


def norm_rows_kernel(first, rows_ref, gain_ref, out_ref):
    rows = rows_ref[first : first + out_ref.shape[0], :].astype(F32)
    unit_rows, _ = norm_parts(rows)
    out_ref[...] = (unit_rows * gain_ref[...]).astype(BF16)


def norm_margin_kernel(
    first, flag_ref, rows_ref, received_ref, select_ref, gain_ref, out_ref, margin_ref, sums_ref
):
    own = rows_ref[first : first + out_ref.shape[0], :]
    margin = jnp.where(flag_ref[0] == 1, own.astype(F32), received_ref[...].astype(F32))
    margin_ref[...] = margin.astype(BF16)
    unit_rows, _ = norm_parts(margin)
    out_ref[...] = (unit_rows * gain_ref[...]).astype(BF16)
    select = select_ref[...]
    for image in range(select.shape[1]):
        sums_ref[image : image + 1, :] = jnp.sum(
            margin * select[:, image : image + 1], axis=0, keepdims=True
        )


def out_rows_kernel(first, rows_ref, *refs):
    *terms, out_ref = refs
    total = sum(term[...].astype(F32) for term in terms)
    rows = rows_ref[first : first + out_ref.shape[0], :].astype(F32)
    out_ref[...] = (rows + total).astype(BF16)


def judge_kernel(
    patch_count,
    pooled_ref,
    gain_ref,
    head_ref,
    label_ref,
    out_weight_ref,
    loss_ref,
    pooled_half_ref,
    grad_logits_ref,
    grad_image_ref,
    per_image_ref,
):
    image_count = pooled_ref.shape[0]
    unit_rows, inverse = norm_parts(pooled_ref[...] * (1.0 / patch_count))
    gain_row = gain_ref[...]
    pooled_half = (unit_rows * gain_row).astype(BF16)
    pooled_half_ref[...] = pooled_half
    head = head_ref[...]
    logits = dot(pooled_half, head)
    classes = lax.broadcasted_iota(jnp.int32, logits.shape, 1)
    images = lax.broadcasted_iota(jnp.int32, logits.shape, 0)
    label = jnp.zeros_like(classes)
    for image in range(image_count):
        label = jnp.where(images == image, label_ref[image], label)
    targets = (classes == label).astype(F32)
    softplus = jnp.maximum(logits, 0.0) + jnp.log1p(jnp.exp(-jnp.abs(logits)))
    terms = softplus - targets * logits
    for image in range(image_count):
        loss_ref[0, image] = jnp.sum(terms[image : image + 1, :]) * (1.0 / terms.shape[1])
    sigmoid = 1.0 / (1.0 + jnp.exp(-logits))
    grad_logits = ((sigmoid - targets) * (1.0 / image_count)).astype(BF16)
    grad_logits_ref[...] = grad_logits
    grad_pooled = norm_back(dot_nt(grad_logits, head), unit_rows, inverse, gain_row)
    grad_image = grad_pooled * (1.0 / patch_count)
    grad_image_ref[...] = grad_image
    per_image_ref[...] = dot_nt(grad_image.astype(BF16), out_weight_ref[...])


def grad_rows_kernel(rows_ref, select_ref, grad_image_ref, gain_ref, *refs):
    *terms, out_ref = refs
    unit_rows, inverse = norm_parts(rows_ref[...].astype(F32))
    grad = sum(term[...].astype(F32) for term in terms)
    total = norm_back(grad, unit_rows, inverse, gain_ref[...])
    select = select_ref[...]
    for image in range(grad_image_ref.shape[0]):
        total = total + select[:, image : image + 1] * grad_image_ref[image : image + 1, :]
    out_ref[...] = total.astype(BF16)


def on_device(
    block_inputs, qkv_weights, out_weights, norm_gain, query_key_gain, pool_gain, class_head, labels
):
    rows_in = block_inputs[0]
    qkv_local = qkv_weights[0]
    out_local = out_weights[0]
    gain_pair = query_key_gain[0]
    label_row = labels[0]
    local_count, model_width = rows_in.shape
    image_count = label_row.shape[0]
    class_count = class_head.shape[2]
    depth, width = lax.axis_size("dp"), lax.axis_size("tensor")
    group_size = depth * width
    row_count = local_count * group_size
    lane_count = qkv_local.shape[2]
    half = local_count // HALVES
    place = (local_count, depth, width)
    member = lax.axis_index(GROUP)
    image_ids = (member * local_count + lax.iota(jnp.int32, local_count)) // PATCHES
    own_select = (image_ids[:, None] == lax.iota(jnp.int32, image_count)[None, :]).astype(F32)

    def shape(dims, dtype=F32):
        return jax.ShapeDtypeStruct(dims, dtype)

    half_shape = shape((half, model_width), BF16)
    three = (3, row_count, lane_count)
    slab_rows = local_count * width
    heads = image_count * (lane_count // HS)
    product_flops = 2 * row_count * lane_count * PATCHES
    slab_flops = 2 * slab_rows * model_width * lane_count
    chunk = 2 * PATCHES if model_width % (2 * PATCHES) == 0 else PATCHES
    piece_shapes = [half_shape] * (width * HALVES)

    select_halves = [own_select[h * half : (h + 1) * half] for h in range(HALVES)]

    def project(_, pieces):
        return call(
            project_kernel,
            [shape((3, slab_rows, lane_count)), shape((model_width, slab_rows), BF16)],
            (*pieces, qkv_local),
            flops=3 * slab_flops,
            limit=12,
        )

    def state_of(projected):
        return call(
            functools.partial(state_kernel, *place),
            [
                shape((heads, PATCHES, PATCHES)),
                shape((heads, PATCHES, PATCHES), BF16),
                shape(three, BF16),
                shape((2, row_count, lane_count)),
                shape((2, row_count, lane_count // HS)),
            ],
            (*projected, gain_pair),
            scratch=[pltpu.VMEM(three, F32)],
            flops=2 * product_flops,
        )

    _, own_results = gather_slabs(
        [
            call(
                functools.partial(norm_rows_kernel, h * half),
                half_shape,
                (rows_in, norm_gain),
                limit=4,
            )
            for h in range(HALVES)
        ],
        project,
    )
    own_projected, own_turned = zip(*own_results)
    attention = call(
        functools.partial(attend_own_kernel, *place),
        shape((row_count, lane_count), BF16),
        (*own_projected, gain_pair),
        scratch=[pltpu.VMEM(three, F32), pltpu.VMEM(three[1:], BF16)],
        flops=2 * product_flops,
    )

    def branch(s):
        return call(
            functools.partial(branch_kernel, slab_starts(s, half, depth, width, OUT_WAYS)),
            piece_shapes,
            (attention, out_local),
            flops=slab_flops,
            limit=12,
        )

    out_halves = [
        call(
            functools.partial(out_rows_kernel, h * half),
            half_shape,
            (rows_in, *terms),
            limit=4,
        )
        for h, terms in enumerate(scatter_slabs(branch, OUT_WAYS))
    ]

    first = (lax.axis_index("section") == 0).astype(jnp.int32).reshape(1)
    margin_normed, margin_halves, row_sums = zip(
        *[
            call(
                functools.partial(norm_margin_kernel, h * half),
                [half_shape, half_shape, shape((image_count, model_width))],
                (first, rows_in, from_behind(out, "section", 1), select, norm_gain),
                specs=[SMEM_SPEC] + [VMEM_SPEC] * 4,
                limit=4,
            )
            for h, (out, select) in enumerate(zip(out_halves, select_halves))
        ]
    )
    _, margin_results = gather_slabs(margin_normed, project)
    margin_projected, margin_turned = zip(*margin_results)
    image_sums, pooled_part = call(
        functools.partial(attend_margin_kernel, *place),
        [shape((image_count, lane_count)), shape((image_count, model_width))],
        (*margin_projected, gain_pair, out_local, *row_sums),
        scratch=[pltpu.VMEM(three, F32)],
        flops=2 * product_flops,
    )
    margin_state = state_of(margin_projected)
    own_state = state_of(own_projected)
    out_own = call(join_kernel, shape((local_count, model_width), BF16), tuple(out_halves), limit=4)
    pooled = after(sum_group(pooled_part), margin_state[4])
    losses, pooled_half, grad_logits, grad_image, per_image = call(
        functools.partial(judge_kernel, PATCHES),
        [
            shape((1, image_count)),
            shape((image_count, model_width), BF16),
            shape((image_count, class_count), BF16),
            shape((image_count, model_width)),
            shape((image_count, lane_count)),
        ],
        (pooled, pool_gain, class_head[0], label_row, out_local),
        specs=[VMEM_SPEC] * 3 + [SMEM_SPEC, VMEM_SPEC],
        outs=[SMEM_SPEC] + [VMEM_SPEC] * 4,
        flops=4 * class_count * model_width * 8,
        limit=12,
    )
    grad_head = call(
        functools.partial(head_gradient_kernel, width),
        shape((model_width // group_size, class_count), BF16),
        (pooled_half, grad_logits),
        limit=4,
    )

    margin_gradient = call(
        functools.partial(attend_back_kernel, *place, True),
        shape((row_count, 3 * lane_count), BF16),
        (*margin_state, per_image, gain_pair),
        scratch=[pltpu.VMEM(three, F32)],
        flops=5 * product_flops,
    )

    def input_term(s):
        return call(
            functools.partial(input_kernel, slab_starts(s, half, depth, width, GRAD_WAYS)),
            piece_shapes,
            (margin_gradient, qkv_local),
            flops=3 * slab_flops,
            limit=12,
        )

    grad_normed = scatter_slabs(input_term, GRAD_WAYS)
    grad_inputs = [
        call(
            grad_rows_kernel,
            half_shape,
            (rows, select, grad_image, norm_gain, *terms),
            limit=6,
        )
        for terms, rows, select in zip(grad_normed, margin_halves, select_halves)
    ]
    returned = [from_behind(grad, "section", -1) for grad in grad_inputs]

    def cotangent(s, pieces):
        if s < 2:
            beside = (grad_head, out_own) if s == 0 else (own_state[4],)
            pieces = [after(pieces[0], *beside)] + pieces[1:]
        return call(
            cotangent_kernel,
            [shape((slab_rows, lane_count)), shape((slab_rows, model_width), BF16)],
            (*pieces, out_local),
            flops=slab_flops,
            limit=12,
        )

    _, cotangent_results = gather_slabs(returned, cotangent)
    grad_attention, cotangent_slabs = zip(*cotangent_results)
    own_gradient = call(
        functools.partial(attend_back_kernel, *place, False),
        shape((row_count, 3 * lane_count), BF16),
        (*own_state, *grad_attention, gain_pair),
        scratch=[pltpu.VMEM(three, F32), pltpu.VMEM(three[1:], F32)],
        flops=5 * product_flops,
    )
    wide = 2 * chunk if model_width % (2 * chunk) == 0 else chunk
    turned = (*margin_turned, *own_turned)
    query_key_value_gradient = pl.pallas_call(
        functools.partial(weight_gradient_kernel, depth),
        grid=(model_width // wide,),
        out_shape=shape((3, model_width, lane_count), BF16),
        in_specs=[pl.BlockSpec((wide, slab_rows), lambda i: (i, 0))] * len(turned)
        + [pl.BlockSpec((row_count, 3 * lane_count), lambda i: (0, 0))] * 2,
        out_specs=pl.BlockSpec((3, wide, lane_count), lambda i: (0, i, 0)),
        compiler_params=pltpu.CompilerParams(vmem_limit_bytes=36 * 2**20),
        cost_estimate=pl.CostEstimate(
            flops=6 * depth * slab_flops,
            bytes_accessed=6 * model_width * lane_count,
            transcendentals=0,
        ),
    )(*turned, margin_gradient, own_gradient)
    grad_out = pl.pallas_call(
        out_gradient_kernel,
        grid=(model_width // wide,),
        out_shape=shape((lane_count, model_width), BF16),
        in_specs=[pl.BlockSpec((slab_rows, wide), lambda i: (0, i))] * depth
        + [
            pl.BlockSpec((row_count, lane_count), lambda i: (0, 0)),
            pl.BlockSpec((image_count, lane_count), lambda i: (0, 0)),
            pl.BlockSpec((image_count, wide), lambda i: (0, i)),
        ],
        out_specs=pl.BlockSpec((lane_count, wide), lambda i: (0, i)),
        scratch_shapes=[pltpu.VMEM((lane_count, row_count), BF16)],
        compiler_params=pltpu.CompilerParams(vmem_limit_bytes=GRAD_OUT_LIMIT * 2**20),
        cost_estimate=pl.CostEstimate(
            flops=depth * slab_flops,
            bytes_accessed=4 * model_width * lane_count,
            transcendentals=0,
        ),
    )(*cotangent_slabs, attention, image_sums, grad_image)
    return (
        out_own[None],
        query_key_value_gradient[None],
        grad_out[None],
        grad_head[None],
        losses,
    )


def solution(mesh):
    in_specs = (
        P("section", GROUP, None),
        P("section", None, None, GROUP),
        P("section", GROUP, None),
        P("section", None),
        P("section", None, None),
        P("section", None),
        P("section", None, None),
        P("section", None),
    )
    out_specs = (
        P("section", GROUP, None),
        P("section", None, None, GROUP),
        P("section", GROUP, None),
        P("section", GROUP, None),
        P("section", None),
    )
    return jax.shard_map(
        on_device, mesh=mesh, in_specs=in_specs, out_specs=out_specs, check_vma=False
    )
```
